256 devices in a mesh: dp: 4 (over y_lo, core), seq: 8 (over y_hi, x), head: 8 (over z).
Axes of the slice: x: 4, y: 4 (y_hi: 2, y_lo: 2; y = y_hi * 2 + y_lo), z: 8, core: 2. Of those that a mesh axis runs over, the one named last changes fastest.
Arguments:
- queries: bfloat16 [4, 2048, 3072], P('dp', 'seq', 'head'), may hold values from -160 to 160
- key_cache: bfloat16 [4, 2048, 1024], P('dp', 'seq', 'head'), may hold values from -7 to 7
- value_cache: bfloat16 [4, 2048, 1024], P('dp', 'seq', 'head'), may hold values from -6 to 6
- out_grad: bfloat16 [4, 2048, 3072], P('dp', 'seq', 'head'), may hold values from -6 to 6
- doc_ids: int32 [4, 2048], P('dp', 'seq'), may hold values from 0 to 1, never falling along the last dimension, each value on 1 to 2047 neighbouring positions
- layer_input: bfloat16 [4, 2048, 3072], P('dp', ('seq', 'head')), may hold values from -6 to 6
- key_proj: bfloat16 [3072, 1024], P(None, 'head'), may hold values from -0.109375 to 0.109375
- value_proj: bfloat16 [3072, 1024], P(None, 'head'), may hold values from -0.109375 to 0.109375
Outputs:
- query_grad: bfloat16 [4, 2048, 3072], P('dp', 'seq', 'head')
- input_grad: bfloat16 [4, 2048, 3072], P('dp', ('seq', 'head'))
- grad_keyproj: float32 [3072, 1024], P(None, 'head')
- grad_valueproj: float32 [3072, 1024], P(None, 'head')
The draws below stay inside these ranges and needn't reach their ends.
Inputs may be any that keep to these rules, and one draw needn't show every extreme that they name: `doc_ids`: document numbers never fall along a sequence; a document spans 1 to 2047 positions.
All inputs are finite; a program needn't handle non-finite values.
Results may differ from the reference program's by a relative error of at most 0.02.
Values may be sent and summed in bfloat16 or wider, within the bound.
A program may use at most 64 MiB of HBM per device.

```python
import math
import jax
import jax.numpy as jnp
import numpy as np
from jax import lax

D = 3072
HD = 128
GROUP = 3
KVH = 8
QH = 24
LEN = 2048
SEQS = 4


def shared_draw(key):
    base_keys = jax.random.truncated_normal(jax.random.fold_in(key, 101), -6.0, 6.0, (SEQS, LEN, KVH * HD), jnp.float32)
    return base_keys


def draw_key_cache(key, part):
    base_keys = shared_draw(key)
    return base_keys.astype(jnp.bfloat16)


def draw_queries(key, part):
    base_query = jax.random.truncated_normal(jax.random.fold_in(key, 303), -6.0, 6.0, (SEQS, LEN, QH * HD), jnp.float32)
    return base_query.astype(jnp.bfloat16)


def levels(stream_key, dims, cuts, smallest, high):
    def one(axis_at, parts):
        steps = jax.random.uniform(jax.random.fold_in(jax.random.fold_in(stream_key, 6), axis_at), (parts,), jnp.float32, smallest / len(cuts), high / len(cuts))
        return jnp.repeat(jnp.exp(steps), dims[axis_at] // parts).reshape((-1,) + (1,) * (len(dims) - axis_at - 1))

    loudness = one(*cuts[0])
    for cut in cuts[1:]:
        loudness = loudness * one(*cut)
    return loudness


def profile(count, total, limit, slope):
    portions = [(1 << 20) // math.isqrt(grade ** slope) + 1 for grade in range(2, count + 1)]
    spare, given = total - limit - (count - 1), [1] * (count - 1)
    while spare > 0:
        free = [i for i in range(count - 1) if given[i] < limit]
        whole, left = sum([portions[i] for i in free]), spare
        for i in free:
            addition = min(limit - given[i], max(1, left * portions[i] // whole), spare)
            given[i] = given[i] + addition
            spare = spare - addition
    return np.array([limit] + given)


def uneven_parts(own_key, count, total, bound, slope):
    if count == 2:
        one = jax.random.randint(own_key, (), max(1, total - bound), min(bound, total - 1) + 1)
        return jnp.stack([one, total - one])
    sizes = jnp.asarray(profile(count, total, bound, slope), jnp.int32)
    couples = (count - 1) // 2
    source_of, receiver = sizes[1:1 + 2 * couples:2], sizes[2:2 + 2 * couples:2]
    room = jnp.minimum(source_of - 1, bound - receiver)
    shifted = jax.random.randint(jax.random.fold_in(own_key, 1), (couples,), 0, 1 << 20) % (room + 1)
    sizes = sizes.at[1:1 + 2 * couples:2].set(source_of - shifted).at[2:2 + 2 * couples:2].set(receiver + shifted)
    return sizes[jax.random.permutation(jax.random.fold_in(own_key, 2), count)]


def gaussian(own_key, extent, deviation, bound, pieces=(), kind=jnp.bfloat16):
    values = jax.random.normal(own_key, extent, jnp.float32) * deviation
    if len(pieces) > 0:
        values = levels(own_key, extent, pieces, -0.22, 0.18) * values
    return jnp.clip(values, min=-bound, max=bound).astype(kind)


def setup_inputs(seed: int = 0) -> dict:
    seeds = jax.random.split(jax.random.key(seed), 9)
    return {
        "queries": draw_queries(jax.random.fold_in(seeds[8], 71), 0),
        "key_cache": draw_key_cache(jax.random.fold_in(seeds[8], 71), 0),
        "value_cache": gaussian(seeds[2], (SEQS, LEN, KVH * HD), 1.0, 6.0, ((0, 4), (1, 8), (2, 8))),
        "out_grad": gaussian(seeds[3], (SEQS, LEN, QH * HD), 1.0, 6.0, ((0, 4), (1, 8), (2, 8))),
        "doc_ids": jax.vmap(lambda own: jnp.searchsorted(jnp.cumsum(uneven_parts(own, 2, LEN, LEN - 1, 0)), jnp.arange(LEN), side="right"))(jax.random.split(seeds[4], SEQS)).reshape((SEQS, LEN)).astype(jnp.int32),
        "layer_input": gaussian(seeds[5], (SEQS, LEN, D), 1.0, 6.0, ((0, 4), (1, 64))),
        "key_proj": gaussian(seeds[6], (D, KVH * HD), D ** -0.5, 0.109375, ((1, 8),)),
        "value_proj": gaussian(seeds[7], (D, KVH * HD), D ** -0.5, 0.109375, ((1, 8),)),
    }


NEG_FILL = -1e30


def head_grads(query_block, key_block, value_block, grad_block, doc_row):
    score_scale = HD ** -0.5
    query_full = query_block.astype(jnp.float32)
    key_full = key_block.astype(jnp.float32)
    value_full = value_block.astype(jnp.float32)
    grad_full = grad_block.astype(jnp.float32)
    positions = jnp.arange(LEN, dtype=jnp.int32)
    allowed = (positions[None, :] <= positions[:, None]) & (doc_row[None, :] == doc_row[:, None])
    scores = jnp.einsum('gid,jd->gij', query_full, key_full) * score_scale
    masked = jnp.where(allowed, scores, NEG_FILL)
    row_top = jnp.max(masked, axis=-1, keepdims=True)
    row_sum = jnp.sum(jnp.where(allowed, jnp.exp(masked - row_top), 0.0), axis=-1, keepdims=True)
    log_total = row_top + jnp.log(row_sum)
    weights = jnp.where(allowed, jnp.exp(masked - log_total), 0.0)
    weight_grad = jnp.einsum('gid,jd->gij', grad_full, value_full)
    row_delta = jnp.sum(weights * weight_grad, axis=-1, keepdims=True)
    score_grad = lax.optimization_barrier((weights * (weight_grad - row_delta) * score_scale).astype(jnp.bfloat16)).astype(jnp.float32)
    weights_low = lax.optimization_barrier(weights.astype(jnp.bfloat16)).astype(jnp.float32)
    query_part = jnp.einsum('gij,jd->gid', score_grad, key_full)
    key_part = jnp.einsum('gij,gid->jd', score_grad, query_full)
    value_part = jnp.einsum('gij,gid->jd', weights_low, grad_full)
    return query_part.astype(jnp.bfloat16), key_part, value_part


def reference(queries, key_cache, value_cache, out_grad, doc_ids, layer_input, key_proj, value_proj):
    def one_sequence(items):
        query_seq, key_seq, value_seq, grad_seq, doc_row = items
        query_heads = query_seq.reshape(LEN, KVH, GROUP, HD).transpose(1, 2, 0, 3)
        grad_heads = grad_seq.reshape(LEN, KVH, GROUP, HD).transpose(1, 2, 0, 3)
        key_heads = key_seq.reshape(LEN, KVH, HD).transpose(1, 0, 2)
        value_heads = value_seq.reshape(LEN, KVH, HD).transpose(1, 0, 2)

        def one_head(head_items):
            return head_grads(head_items[0], head_items[1], head_items[2], head_items[3], doc_row)

        query_part, key_part, value_part = lax.map(one_head, (query_heads, key_heads, value_heads, grad_heads))
        query_part = query_part.transpose(2, 0, 1, 3).reshape(LEN, QH * HD)
        key_part = key_part.transpose(1, 0, 2).reshape(LEN, KVH * HD)
        value_part = value_part.transpose(1, 0, 2).reshape(LEN, KVH * HD)
        return query_part, key_part, value_part

    query_grad, key_grad, value_grad = lax.map(one_sequence, (queries, key_cache, value_cache, out_grad, doc_ids))
    key_low = key_grad.astype(jnp.bfloat16).reshape(SEQS * LEN, KVH * HD)
    value_low = value_grad.astype(jnp.bfloat16).reshape(SEQS * LEN, KVH * HD)
    input_sum = jnp.dot(key_low, key_proj.T, preferred_element_type=jnp.float32) + jnp.dot(value_low, value_proj.T, preferred_element_type=jnp.float32)
    input_grad = input_sum.astype(jnp.bfloat16).reshape(SEQS, LEN, D)
    flat_input = layer_input.reshape(SEQS * LEN, D)
    grad_keyproj = jnp.dot(flat_input.T, key_low, preferred_element_type=jnp.float32)
    grad_valueproj = jnp.dot(flat_input.T, value_low, preferred_element_type=jnp.float32)
    return query_grad, input_grad, grad_keyproj, grad_valueproj
```

```python
import functools
import math

import jax
import jax.numpy as jnp
from jax import lax
from jax.experimental import pallas as pl
from jax.experimental.pallas import tpu as pltpu
from jax.sharding import PartitionSpec as P

D = 3072
HD = 128
GROUP = 3
ROWS = 256
NX = 4
NZ = 8
NEG_FILL = -1e30
SCALE = HD ** (-0.5)
EXP_SCALE = SCALE * math.log2(math.e)
HALF = D // 2
BF = jnp.bfloat16
F32 = jnp.float32
NT = (((1,), (1,)), ((), ()))
NN = (((1,), (0,)), ((), ()))


def dot(a, b, dims):
    return lax.dot_general(a, b, dims, preferred_element_type=F32)


def kernel(
    q_hbm, k_hbm, v_hbm, do_hbm, docs_ref, li_hbm, wk_hbm, wv_hbm,
    qg_hbm, ig_hbm, gp_hbm,
    q_v, do_v, kvbuf, li_buf, li_t, wcat,
    p_buf, dp_buf, m_buf, l_buf, a_buf, f_buf, dq_t,
    gsend, grecv, crecv, xsend, xrecv, acc, kv_low,
    ipart, zs, zr, ig_out,
    csend, ccr, h32, s1, r1, a32, s2, r2, gfull, qg_out,
    loc, kv_ss, kv_rs, li_ss, li_rs, g_ss, g_rs, c_rs, x_sem,
    z_ss, z_rs, core_sem, st1_ss, st1_rs, st2_ss, st2_rs,
    ag1_ss, ag1_rs, ag2_ss, ag2_rs, p_ss, p_rs, out_sem,
):
    dp = lax.axis_index("dp")
    sq = lax.axis_index("seq")
    hd = lax.axis_index("head")
    core = lax.rem(dp, 2)
    y_lo = lax.div(dp, 2)
    y_hi = lax.div(sq, NX)
    x = lax.rem(sq, NX)
    yi = y_hi * 2 + y_lo

    def x_mate(idx):
        return (dp, y_hi * NX + idx, hd)

    def y_mate(idx):
        return (lax.rem(idx, 2) * 2 + core, lax.div(idx, 2) * NX + x, hd)

    other_half = (dp, (1 - y_hi) * NX + x, hd)
    other_core = (y_lo * 2 + 1 - core, sq, hd)
    z_next = (dp, sq, lax.rem(hd + 1, NZ))
    z_prev = (dp, sq, lax.rem(hd + NZ - 1, NZ))

    def remote(src, dst, ssem, rsem, dev):
        return pltpu.make_async_remote_copy(
            src_ref=src, dst_ref=dst, send_sem=ssem, recv_sem=rsem,
            device_id=dev, device_id_type=pl.DeviceIdType.MESH,
        )

    loads = [
        pltpu.make_async_copy(k_hbm, kvbuf.at[sq, pl.ds(0, ROWS), :], loc.at[0]),
        pltpu.make_async_copy(v_hbm, kvbuf.at[sq, pl.ds(ROWS, ROWS), :], loc.at[1]),
        pltpu.make_async_copy(li_hbm, li_buf.at[hd], loc.at[2]),
    ]
    for g in range(GROUP):
        loads.append(pltpu.make_async_copy(q_hbm.at[:, pl.ds(g * HD, HD)], q_v.at[g], loc.at[3 + g]))
        loads.append(pltpu.make_async_copy(do_hbm.at[:, pl.ds(g * HD, HD)], do_v.at[g], loc.at[6 + g]))
    loads.append(pltpu.make_async_copy(wk_hbm, wcat.at[:, pl.ds(0, HD)], loc.at[9]))
    loads.append(pltpu.make_async_copy(wv_hbm, wcat.at[:, pl.ds(HD, HD)], loc.at[10]))
    for c in loads:
        c.start()

    barrier = pltpu.get_barrier_semaphore()
    partners = [x_mate(lax.rem(x + d, NX)) for d in range(1, NX)]
    partners += [y_mate(lax.rem(yi + d, NX)) for d in range(1, NX)]
    partners += [other_core, z_next, z_prev]
    for dev in partners:
        pl.semaphore_signal(barrier, inc=1, device_id=dev, device_id_type=pl.DeviceIdType.MESH)

    doc_row = docs_ref[...].astype(F32)
    upper = lax.broadcasted_iota(jnp.int32, (16, HD), 0) < 8
    doc_tile = jnp.where(
        upper,
        jnp.broadcast_to(doc_row[:, 0:HD], (16, HD)),
        jnp.broadcast_to(doc_row[:, HD:], (16, HD)),
    )
    kvbuf[sq, pl.ds(2 * ROWS, 16), :] = doc_tile.astype(BF)
    m_buf[...] = jnp.full(m_buf.shape, NEG_FILL, F32)
    l_buf[...] = jnp.zeros(l_buf.shape, F32)
    a_buf[...] = jnp.zeros(a_buf.shape, F32)
    dq_t[...] = jnp.zeros(dq_t.shape, F32)
    for c in loads[:3]:
        c.wait()
    pl.semaphore_wait(barrier, len(partners))

    def kv_copy(block, dev, s):
        return remote(kvbuf.at[block], kvbuf.at[block], kv_ss.at[s], kv_rs.at[block], dev)

    @pl.when(y_hi == 0)
    def _():
        kv_copy(sq, other_half, 3).start()

    for d in range(1, NX):
        xt = lax.rem(x + d, NX)

        @pl.when(xt > x)
        def _():
            kv_copy(sq, x_mate(xt), d - 1).start()

    def li_copy(direction, k):
        if direction == 0:
            chunk, dev = lax.rem(hd - k + NZ, NZ), z_next
        else:
            chunk, dev = lax.rem(hd + k, NZ), z_prev
        ref = li_buf.at[chunk]
        if k == 3:
            ref = li_buf.at[chunk, pl.ds(16 * direction, 16), :]
        return remote(ref, ref, li_ss.at[direction, k], li_rs.at[direction, k], dev)

    def li_arrived(direction, k):
        if direction == 0:
            chunk = lax.rem(hd - 1 - k + NZ, NZ)
        else:
            chunk = lax.rem(hd + 1 + k, NZ)
        ref = li_buf.at[chunk]
        if k == 3:
            ref = li_buf.at[chunk, pl.ds(16 * direction, 16), :]
        dev = z_next if direction == 0 else z_prev
        return remote(ref, ref, li_ss.at[direction, k], li_rs.at[direction, k], dev)

    def li_pump(k):
        for direction in range(2):
            li_arrived(direction, k - 1).wait_recv()
        for direction in range(2):
            li_copy(direction, k).start()

    for direction in range(2):
        li_copy(direction, 0).start()

    for c in loads[3:9]:
        c.wait()

    key_iota = lax.broadcasted_iota(jnp.int32, (ROWS, ROWS), 0).astype(F32)

    def score_block(b, diagonal):
        kb = kvbuf[b, pl.ds(0, ROWS), :]
        vb = kvbuf[b, pl.ds(ROWS, ROWS), :]
        docs = kvbuf[b, pl.ds(2 * ROWS, 16), :].astype(F32)
        ones = jnp.sum(jnp.sum(docs, axis=0, keepdims=True), axis=1, keepdims=True) * 0.125
        zeros = ROWS - ones
        low = doc_row * zeros
        high = zeros + doc_row * ones
        if diagonal:
            own = lax.broadcasted_iota(jnp.int32, (1, ROWS), 1).astype(F32)
            high = jnp.minimum(high, own + 1.0)
        allowed = (key_iota >= low) & (key_iota < high)
        for g in range(GROUP):
            s = jnp.where(allowed, dot(kb, q_v[g], NT), NEG_FILL)
            top = jnp.max(s, axis=0, keepdims=True)
            p = jnp.exp2((s - top) * EXP_SCALE)
            wg = dot(vb, do_v[g], NT)
            p_buf[b, g] = p
            dp_buf[b, g] = wg
            m_buf[b, g : g + 1, :] = top
            l_buf[b, g : g + 1, :] = jnp.sum(p, axis=0, keepdims=True)
            a_buf[b, g : g + 1, :] = jnp.sum(p * wg, axis=0, keepdims=True)

    score_block(sq, True)

    @pl.when(y_hi == 1)
    def _():
        kv_copy(x, other_half, 0).wait_recv()
        for d in range(1, NX):
            kv_copy(x, x_mate(lax.rem(x + d, NX)), 3 + d).start()
        score_block(x, False)

    li_pump(1)

    @pl.loop(1, NX)
    def _(d):
        xt = lax.rem(x - d + NX, NX)

        @pl.when(xt < x)
        def _():
            b = y_hi * NX + xt
            kv_copy(b, other_half, 0).wait_recv()
            score_block(b, False)

    li_pump(2)

    @pl.when(y_hi == 1)
    def _():
        @pl.loop(1, NX)
        def _(d):
            b = lax.rem(x - d + NX, NX)
            kv_copy(b, other_half, 0).wait_recv()
            score_block(b, False)

    top = jnp.max(m_buf[...], axis=0)
    factor = jnp.exp2((m_buf[...] - top[None]) * EXP_SCALE)
    total = jnp.sum(factor * l_buf[...], axis=0)
    gathered = jnp.sum(factor * a_buf[...], axis=0)
    safe = jnp.where(total > 0.0, total, 1.0)
    inv = 1.0 / safe
    delta = gathered * inv
    f_buf[...] = factor * inv[None]

    def grad_block(b):
        kbt = kvbuf[b, pl.ds(0, ROWS), :].T
        dk = jnp.zeros((ROWS, HD), F32)
        dv = jnp.zeros((ROWS, HD), F32)
        for g in range(GROUP):
            w = p_buf[b, g] * f_buf[b, g : g + 1, :]
            sg = (w * (dp_buf[b, g] - delta[g : g + 1, :]) * SCALE).astype(BF)
            dv = dv + dot(w.astype(BF), do_v[g], NN)
            dk = dk + dot(sg, q_v[g], NN)
            dq_t[g] += dot(kbt, sg, NN)
        gsend[b, :, 0:HD] = dk.astype(BF)
        gsend[b, :, HD:] = dv.astype(BF)

    def c_copy(d):
        xt = lax.rem(x + d, NX)
        return remote(gsend.at[xt], crecv.at[d - 1], g_ss.at[2 + d], c_rs.at[d - 1], x_mate(xt))

    def g_copy(d):
        xt = lax.rem(x + d, NX)
        return remote(
            gsend.at[y_hi * NX + xt], grecv.at[d - 1], g_ss.at[d - 1], g_rs.at[d - 1], x_mate(xt)
        )

    cross = remote(xsend, xrecv, x_sem.at[0], x_sem.at[1], other_half)

    @pl.when(y_hi == 1)
    def _():
        @pl.loop(1, NX)
        def _(d):
            grad_block(lax.rem(x + d, NX))
            c_copy(d).start()

        grad_block(x)

    @pl.loop(1, NX)
    def _(d):
        xt = lax.rem(x + d, NX)

        @pl.when(xt < x)
        def _():
            grad_block(y_hi * NX + xt)
            g_copy(d).start()

    @pl.when(y_hi == 1)
    def _():
        acc[...] = gsend[x].astype(F32)
        for d in range(1, NX):
            c_copy(d).wait_recv()
            acc[...] += crecv[d - 1].astype(F32)
        xsend[...] = acc[...].astype(BF)
        cross.start()

    grad_block(sq)
    li_pump(3)

    for g in range(GROUP):
        qg_out[:, g * HD : (g + 1) * HD] = dq_t[g].T.astype(BF)
    qg_copy = pltpu.make_async_copy(qg_out, qg_hbm, out_sem.at[0])
    qg_copy.start()

    for direction in range(2):
        li_arrived(direction, 3).wait_recv()

    for n in range(D // 512):
        cols = li_buf[:, :, n * 512 : (n + 1) * 512].reshape(ROWS, 512)
        li_t[n * 512 : (n + 1) * 512, :] = cols.T

    for c in loads[9:]:
        c.wait()

    acc[...] = gsend[sq].astype(F32)

    for d in range(1, NX):
        @pl.when(lax.rem(x - d + NX, NX) > x)
        def _():
            g_copy(d).wait_recv()
            acc[...] += grecv[d - 1].astype(F32)

    @pl.when(y_hi == 0)
    def _():
        cross.wait_recv()
        acc[...] += xrecv[...].astype(F32)

    kv_low[...] = acc[...].astype(BF)

    for n in range(D // 512):
        part = dot(kv_low[...], wcat[n * 512 : (n + 1) * 512, :], NT)
        ipart[:, :, n * 512 : (n + 1) * 512] = part.reshape(NZ, 32, 512)

    def z_copy(direction, k, half):
        return remote(
            zs.at[direction, k, half], zr.at[direction, k, half],
            z_ss.at[direction, k, half], z_rs.at[direction, k, half],
            z_next if direction == 0 else z_prev,
        )

    def z_send(direction, k, half, add):
        t = lax.rem(hd + 4 - k, NZ) if direction == 0 else lax.rem(hd + 4 + k, NZ)
        term = ipart[t, :, half * HALF : (half + 1) * HALF]
        if add:
            z_copy(direction, k - 1, half).wait_recv()
            term = term + zr[direction, k - 1, half].astype(F32)
        zs[direction, k, half] = term.astype(BF)
        z_copy(direction, k, half).start()

    z_send(0, 0, 0, False)
    z_send(1, 0, 1, False)
    z_send(0, 1, 1, False)
    z_send(1, 1, 0, False)

    low = kv_low[...]
    for n in range(3):
        rows = pl.ds(pl.multiple_of((1 - core) * HALF + n * 512, 512), 512)
        csend[n * 512 : (n + 1) * 512, :] = dot(li_t[rows, :], low, NN).astype(BF)
    core_copy = remote(csend, ccr, core_sem.at[0], core_sem.at[1], other_core)
    core_copy.start()
    for n in range(3):
        rows = pl.ds(pl.multiple_of(core * HALF + n * 512, 512), 512)
        h32[n * 512 : (n + 1) * 512, :] = dot(li_t[rows, :], low, NN)

    z_send(0, 1, 0, True)
    z_send(1, 1, 1, True)

    core_copy.wait_recv()
    for n in range(8):
        rows = pl.ds(n * 192, 192)
        total_n = h32[rows, :] + ccr[rows, :].astype(F32)
        h32[rows, :] = total_n
        s1[n // 4, n % 4] = total_n.astype(BF)

    def mate(stage, part, d):
        if (stage + part) % 2 == 0:
            return x_mate(lax.rem(x + d, NX))
        return y_mate(lax.rem(yi + d, NX))

    own1 = (x, yi)
    own2 = (yi, x)

    def st1_copy(part, d):
        to = lax.rem(own1[part] + d, NX)
        return remote(
            s1.at[part, to], r1.at[part, d - 1], st1_ss.at[part, d - 1], st1_rs.at[part, d - 1],
            mate(0, part, d),
        )

    def st2_copy(part, d):
        to = lax.rem(own2[part] + d, NX)
        return remote(
            s2.at[part, to], r2.at[part, d - 1], st2_ss.at[part, d - 1], st2_rs.at[part, d - 1],
            mate(1, part, d),
        )

    for d in (2, 1, 3):
        for part in range(2):
            st1_copy(part, d).start()

    for half in (1, 0):
        z_send(0, 2, half, True)
        z_send(1, 2, 1 - half, True)

    for part in range(2):
        base = pl.multiple_of(part * 768 + own1[part] * 192, 192)
        term = h32[pl.ds(base, 192), :]
        for d in range(1, NX):
            st1_copy(part, d).wait_recv()
            term = term + r1[part, d - 1].astype(F32)
        term = term.reshape(NX, 48, 2 * HD)
        a32[part] = term
        s2[part] = term.astype(BF)
        for d in (2, 1, 3):
            st2_copy(part, d).start()

    for half in (1, 0):
        z_send(0, 3, half, True)
        z_send(1, 3, 1 - half, True)

    def full(c, part, i, j):
        return gfull.at[c, part, i, j]

    def ag1_copy(part, d):
        ref = full(core, part, own1[part], own2[part])
        return remote(ref, ref, ag1_ss.at[part, d - 1], ag1_rs.at[part, d - 1], mate(1, part, d))

    def ag1_arrived(part, d):
        ref = full(core, part, own1[part], lax.rem(own2[part] - d + NX, NX))
        return remote(ref, ref, ag1_ss.at[part, d - 1], ag1_rs.at[part, d - 1], mate(1, part, d))

    def ag2_copy(part, d):
        ref = gfull.at[core, part, own1[part]]
        return remote(ref, ref, ag2_ss.at[part, d - 1], ag2_rs.at[part, d - 1], mate(0, part, d))

    def ag2_arrived(part, d):
        ref = gfull.at[core, part, lax.rem(own1[part] - d + NX, NX)]
        return remote(ref, ref, ag2_ss.at[part, d - 1], ag2_rs.at[part, d - 1], mate(0, part, d))

    def pair_copy(part, d):
        ref = gfull.at[core, part, lax.rem(own1[part] - d + NX, NX)]
        return remote(ref, ref, p_ss.at[part, d], p_rs.at[part, d], other_core)

    def pair_arrived(part, d):
        ref = gfull.at[1 - core, part, lax.rem(own1[part] - d + NX, NX)]
        return remote(ref, ref, p_ss.at[part, d], p_rs.at[part, d], other_core)

    for part in range(2):
        term = a32[part, own2[part]]
        for d in range(1, NX):
            st2_copy(part, d).wait_recv()
            term = term + r2[part, d - 1].astype(F32)
        gfull[core, part, own1[part], own2[part]] = term.astype(BF)
        for d in (2, 1, 3):
            ag1_copy(part, d).start()

    for part in range(2):
        for d in range(1, NX):
            ag1_arrived(part, d).wait_recv()
        for d in (2, 1, 3):
            ag2_copy(part, d).start()
        pair_copy(part, 0).start()

    for part in range(2):
        for d in (1, 3, 2):
            ag2_arrived(part, d).wait_recv()
            pair_copy(part, d).start()

    for half in range(2):
        term = ipart[hd, :, half * HALF : (half + 1) * HALF]
        for direction in range(2):
            z_copy(direction, 3, half).wait_recv()
            term = term + zr[direction, 3, half].astype(F32)
        ig_out[:, half * HALF : (half + 1) * HALF] = term.astype(BF)
    ig_copy = pltpu.make_async_copy(ig_out, ig_hbm, out_sem.at[1])
    ig_copy.start()

    for part in range(2):
        for d in range(NX):
            pair_arrived(part, d).wait_recv()
    gp_copy = pltpu.make_async_copy(gfull, gp_hbm, out_sem.at[2])
    gp_copy.start()

    @pl.when(y_hi == 0)
    def _():
        kv_copy(sq, other_half, 3).wait_send()

    for d in range(1, NX):
        xt = lax.rem(x + d, NX)

        @pl.when(xt > x)
        def _():
            kv_copy(sq, x_mate(xt), d - 1).wait_send()

        @pl.when(xt < x)
        def _():
            g_copy(d).wait_send()

    @pl.when(y_hi == 1)
    def _():
        for d in range(1, NX):
            kv_copy(x, x_mate(lax.rem(x + d, NX)), 3 + d).wait_send()
            c_copy(d).wait_send()
        cross.wait_send()

    for direction in range(2):
        for k in range(4):
            li_copy(direction, k).wait_send()
            for half in range(2):
                if k > 0 or half == direction:
                    z_copy(direction, k, half).wait_send()
    core_copy.wait_send()
    for part in range(2):
        for d in range(1, NX):
            st1_copy(part, d).wait_send()
            st2_copy(part, d).wait_send()
            ag1_copy(part, d).wait_send()
            ag2_copy(part, d).wait_send()
        for d in range(NX):
            pair_copy(part, d).wait_send()
    qg_copy.wait()
    ig_copy.wait()
    gp_copy.wait()


def shards(queries, key_cache, value_cache, out_grad, doc_ids, layer_input, key_proj, value_proj):
    hbm = pl.BlockSpec(memory_space=pl.ANY)
    vmem = pl.BlockSpec(memory_space=pltpu.VMEM)
    dma = pltpu.SemaphoreType.DMA
    scratch = [
        pltpu.VMEM((GROUP, ROWS, HD), BF),
        pltpu.VMEM((GROUP, ROWS, HD), BF),
        pltpu.VMEM((8, 2 * ROWS + 16, HD), BF),
        pltpu.VMEM((NZ, 32, D), BF),
        pltpu.VMEM((D, ROWS), BF),
        pltpu.VMEM((D, 2 * HD), BF),
        pltpu.VMEM((8, GROUP, ROWS, ROWS), F32),
        pltpu.VMEM((8, GROUP, ROWS, ROWS), F32),
        pltpu.VMEM((8, 8, ROWS), F32),
        pltpu.VMEM((8, 8, ROWS), F32),
        pltpu.VMEM((8, 8, ROWS), F32),
        pltpu.VMEM((8, 8, ROWS), F32),
        pltpu.VMEM((GROUP, HD, ROWS), F32),
        pltpu.VMEM((8, ROWS, 2 * HD), BF),
        pltpu.VMEM((3, ROWS, 2 * HD), BF),
        pltpu.VMEM((3, ROWS, 2 * HD), BF),
        pltpu.VMEM((ROWS, 2 * HD), BF),
        pltpu.VMEM((ROWS, 2 * HD), BF),
        pltpu.VMEM((ROWS, 2 * HD), F32),
        pltpu.VMEM((ROWS, 2 * HD), BF),
        pltpu.VMEM((NZ, 32, D), F32),
        pltpu.VMEM((2, 4, 2, 32, HALF), BF),
        pltpu.VMEM((2, 4, 2, 32, HALF), BF),
        pltpu.VMEM((32, D), BF),
        pltpu.VMEM((HALF, 2 * HD), BF),
        pltpu.VMEM((HALF, 2 * HD), BF),
        pltpu.VMEM((HALF, 2 * HD), F32),
        pltpu.VMEM((2, NX, 192, 2 * HD), BF),
        pltpu.VMEM((2, 3, 192, 2 * HD), BF),
        pltpu.VMEM((2, NX, 48, 2 * HD), F32),
        pltpu.VMEM((2, NX, 48, 2 * HD), BF),
        pltpu.VMEM((2, 3, 48, 2 * HD), BF),
        pltpu.VMEM((2, 2, NX, NX, 48, 2 * HD), BF),
        pltpu.VMEM((ROWS, GROUP * HD), BF),
        dma((11,)),
        dma((7,)),
        dma((8,)),
        dma((2, 4)),
        dma((2, 4)),
        dma((6,)),
        dma((3,)),
        dma((3,)),
        dma((2,)),
        dma((2, 4, 2)),
        dma((2, 4, 2)),
        dma((2,)),
        dma((2, 3)),
        dma((2, 3)),
        dma((2, 3)),
        dma((2, 3)),
        dma((2, 3)),
        dma((2, 3)),
        dma((2, 3)),
        dma((2, 3)),
        dma((2, 4)),
        dma((2, 4)),
        dma((3,)),
    ]
    qg, ig, gp = pl.pallas_call(
        kernel,
        out_shape=(
            jax.ShapeDtypeStruct((ROWS, GROUP * HD), BF),
            jax.ShapeDtypeStruct((32, D), BF),
            jax.ShapeDtypeStruct((2, 2, NX, NX, 48, 2 * HD), BF),
        ),
        in_specs=[hbm, hbm, hbm, hbm, vmem, hbm, hbm, hbm],
        out_specs=(hbm, hbm, hbm),
        scratch_shapes=scratch,
        compiler_params=pltpu.CompilerParams(
            collective_id=0, has_side_effects=True, vmem_limit_bytes=56 * 1024 * 1024
        ),
        cost_estimate=pl.CostEstimate(
            flops=3 * 10**9, bytes_accessed=8 * 10**6, transcendentals=2 * 10**6
        ),
    )(
        queries[0], key_cache[0], value_cache[0], out_grad[0], doc_ids, layer_input[0],
        key_proj, value_proj,
    )
    grads = gp.reshape(D, 2 * HD)
    return (
        qg[None],
        ig[None],
        grads[:, :HD].astype(F32),
        grads[:, HD:].astype(F32),
    )


def solution(mesh):
    return jax.shard_map(
        shards,
        mesh=mesh,
        in_specs=(
            P("dp", "seq", "head"),
            P("dp", "seq", "head"),
            P("dp", "seq", "head"),
            P("dp", "seq", "head"),
            P("dp", "seq"),
            P("dp", ("seq", "head"), None),
            P(None, "head"),
            P(None, "head"),
        ),
        out_specs=(
            P("dp", "seq", "head"),
            P("dp", ("seq", "head"), None),
            P(None, "head"),
            P(None, "head"),
        ),
        check_vma=False,
    )
```

```python
import functools
import math

import jax
import jax.numpy as jnp
from jax import lax
from jax.experimental import pallas as pl
from jax.experimental.pallas import tpu as pltpu
from jax.sharding import PartitionSpec as P

D = 3072
HD = 128
GROUP = 3
ROWS = 256
NX = 4
NZ = 8
NEG_FILL = -1e30
SCALE = HD ** (-0.5)
EXP_SCALE = SCALE * math.log2(math.e)
HALF = D // 2
NS = 8
PARTS = 4
PART = HALF // PARTS
SUB = PART // NX
PIECES = 4
BF = jnp.bfloat16
F32 = jnp.float32
NT = (((1,), (1,)), ((), ()))
NN = (((1,), (0,)), ((), ()))


def dot(a, b, dims):
    return lax.dot_general(a, b, dims, preferred_element_type=F32)


def kernel(
    q_hbm, k_hbm, v_hbm, do_hbm, docs_hbm, li_hbm, wk_hbm, wv_hbm,
    qg_hbm, ig_hbm, gp_hbm,
    q_v, do_v, docs_ref, kvbuf, li_buf, li_t, wcat,
    p_buf, dp_buf, m_buf, l_buf, a_buf, f_buf, dq_t,
    gsend, grecv, acc, kv_low,
    ipart, zs, zr, ig_out,
    csend, ccr, h32, s1, r1, r2, gfull, qg_out,
    loc, kv_ss, kv_rs, li_ss, li_rs, g_ss, g_rs,
    z_ss, z_rs, core_ss, core_rs, st1_ss, st1_rs, st2_ss, st2_rs,
    ag_ss, ag_rs, p_ss, p_rs, out_sem,
):
    dp = lax.axis_index("dp")
    sq = lax.axis_index("seq")
    hd = lax.axis_index("head")
    core = lax.rem(dp, 2)
    y_lo = lax.div(dp, 2)
    y_hi = lax.div(sq, NX)
    x = lax.rem(sq, NX)
    yi = y_hi * 2 + y_lo

    def seq_mate(idx):
        return (dp, idx, hd)

    def x_mate(idx):
        return (dp, y_hi * NX + idx, hd)

    def y_mate(idx):
        return (lax.rem(idx, 2) * 2 + core, lax.div(idx, 2) * NX + x, hd)

    other_core = (y_lo * 2 + 1 - core, sq, hd)

    def z_mate(d):
        return (dp, sq, lax.rem(hd + d + NZ, NZ))

    def remote(src, dst, ssem, rsem, dev):
        return pltpu.make_async_remote_copy(
            src_ref=src, dst_ref=dst, send_sem=ssem, recv_sem=rsem,
            device_id=dev, device_id_type=pl.DeviceIdType.MESH,
        )

    barrier = pltpu.get_barrier_semaphore()
    partners = [seq_mate(lax.rem(sq + d, NS)) for d in range(1, NS)]
    partners += [y_mate(lax.rem(yi + d, NX)) for d in (1, 3)]
    partners += [other_core, z_mate(1), z_mate(-1), z_mate(2), z_mate(-2)]
    for dev in partners:
        pl.semaphore_signal(barrier, inc=1, device_id=dev, device_id_type=pl.DeviceIdType.MESH)

    loads = [
        pltpu.make_async_copy(docs_hbm, docs_ref, loc.at[0]),
        pltpu.make_async_copy(k_hbm, kvbuf.at[sq, pl.ds(0, ROWS), :], loc.at[1]),
        pltpu.make_async_copy(v_hbm, kvbuf.at[sq, pl.ds(ROWS, ROWS), :], loc.at[2]),
        pltpu.make_async_copy(li_hbm, li_buf.at[hd], loc.at[3]),
    ]
    for g in range(GROUP):
        loads.append(pltpu.make_async_copy(q_hbm.at[:, pl.ds(g * HD, HD)], q_v.at[g], loc.at[4 + g]))
        loads.append(pltpu.make_async_copy(do_hbm.at[:, pl.ds(g * HD, HD)], do_v.at[g], loc.at[7 + g]))
    loads.append(pltpu.make_async_copy(wk_hbm, wcat.at[:, pl.ds(0, HD)], loc.at[10]))
    loads.append(pltpu.make_async_copy(wv_hbm, wcat.at[:, pl.ds(HD, HD)], loc.at[11]))
    for c in loads:
        c.start()

    m_buf[...] = jnp.full(m_buf.shape, NEG_FILL, F32)
    l_buf[...] = jnp.zeros(l_buf.shape, F32)
    a_buf[...] = jnp.zeros(a_buf.shape, F32)
    dq_t[...] = jnp.zeros(dq_t.shape, F32)

    loads[0].wait()
    doc_row = docs_ref[...].astype(F32)
    upper = lax.broadcasted_iota(jnp.int32, (16, HD), 0) < 8
    doc_tile = jnp.where(
        upper,
        jnp.broadcast_to(doc_row[:, 0:HD], (16, HD)),
        jnp.broadcast_to(doc_row[:, HD:], (16, HD)),
    )
    kvbuf[sq, pl.ds(2 * ROWS, 16), :] = doc_tile.astype(BF)
    for c in loads[1:4]:
        c.wait()
    pl.semaphore_wait(barrier, len(partners))

    def kv_copy(block, dev, s):
        return remote(kvbuf.at[block], kvbuf.at[block], kv_ss.at[s], kv_rs.at[block], dev)

    def kv_arrived(block):
        return kv_copy(block, seq_mate(lax.rem(sq + 1, NS)), 0)

    for d in range(NS - 1, 0, -1):

        @pl.when(sq + d < NS)
        def _():
            kv_copy(sq, seq_mate(sq + d), d - 1).start()

    li_moves = ((1, 0, (0, 32)), (2, 0, (0, 16)), (1, 1, (16, 16)), (2, 1, (0, 16)), (1, 2, (16, 16)), None)

    def li_copy(direction, n, arrived=False):
        hops, away, (row, size) = li_moves[n] or (2, 2, (16 * direction, 16))
        sign = 1 - 2 * direction
        away = away + hops if arrived else away
        ref = li_buf.at[lax.rem(hd - sign * away + NZ, NZ), pl.ds(row, size), :]
        return remote(ref, ref, li_ss.at[direction, n], li_rs.at[direction, n], z_mate(sign * hops))

    def li_start(*moves):
        for n in moves:
            for direction in range(2):
                li_copy(direction, n).start()

    def li_wait(*moves):
        for n in moves:
            for direction in range(2):
                li_copy(direction, n, True).wait_recv()

    li_start(0, 1)

    for c in loads[4:10]:
        c.wait()

    key_iota = lax.broadcasted_iota(jnp.int32, (ROWS, ROWS), 0).astype(F32)

    def score_block(b, diagonal):
        kb = kvbuf[b, pl.ds(0, ROWS), :]
        vb = kvbuf[b, pl.ds(ROWS, ROWS), :]
        docs = kvbuf[b, pl.ds(2 * ROWS, 16), :].astype(F32)
        ones = jnp.sum(jnp.sum(docs, axis=0, keepdims=True), axis=1, keepdims=True) * 0.125
        zeros = ROWS - ones
        low = doc_row * zeros
        high = zeros + doc_row * ones
        if diagonal:
            own = lax.broadcasted_iota(jnp.int32, (1, ROWS), 1).astype(F32)
            high = jnp.minimum(high, own + 1.0)
        allowed = (key_iota >= low) & (key_iota < high)
        for g in range(GROUP):
            s = jnp.where(allowed, dot(kb, q_v[g], NT), NEG_FILL)
            top = jnp.max(s, axis=0, keepdims=True)
            p = jnp.exp2((s - top) * EXP_SCALE)
            wg = dot(vb, do_v[g], NT)
            p_buf[b, g] = p
            dp_buf[b, g] = wg
            m_buf[b, g : g + 1, :] = top
            l_buf[b, g : g + 1, :] = jnp.sum(p, axis=0, keepdims=True)
            a_buf[b, g : g + 1, :] = jnp.sum(p * wg, axis=0, keepdims=True)

    score_block(sq, True)

    @pl.loop(1, NX)
    def _(d):
        @pl.when(d <= x)
        def _():
            kv_arrived(sq - d).wait_recv()
            score_block(sq - d, False)

    li_wait(0)
    li_start(2, 3)

    @pl.when(y_hi == 1)
    def _():
        @pl.loop(0, NX)
        def _(d):
            kv_arrived(NX - 1 - d).wait_recv()
            score_block(NX - 1 - d, False)

    top = jnp.max(m_buf[...], axis=0)
    factor = jnp.exp2((m_buf[...] - top[None]) * EXP_SCALE)
    total = jnp.sum(factor * l_buf[...], axis=0)
    gathered = jnp.sum(factor * a_buf[...], axis=0)
    safe = jnp.where(total > 0.0, total, 1.0)
    inv = 1.0 / safe
    delta = gathered * inv
    f_buf[...] = factor * inv[None]

    def grad_block(b):
        kbt = kvbuf[b, pl.ds(0, ROWS), :].T
        dk = jnp.zeros((ROWS, HD), F32)
        dv = jnp.zeros((ROWS, HD), F32)
        for g in range(GROUP):
            w = p_buf[b, g] * f_buf[b, g : g + 1, :]
            sg = (w * (dp_buf[b, g] - delta[g : g + 1, :]) * SCALE).astype(BF)
            dv = dv + dot(w.astype(BF), do_v[g], NN)
            dk = dk + dot(sg, q_v[g], NN)
            dq_t[g] += dot(kbt, sg, NN)
        gsend[b, :, 0:HD] = dk.astype(BF)
        gsend[b, :, HD:] = dv.astype(BF)

    def g_copy(d):
        return remote(
            gsend.at[sq - d], grecv.at[d - 1], g_ss.at[d - 1], g_rs.at[d - 1], seq_mate(sq - d)
        )

    def g_arrived(d):
        return remote(
            gsend.at[sq], grecv.at[d - 1], g_ss.at[d - 1], g_rs.at[d - 1], seq_mate(sq + d)
        )

    @pl.loop(0, NS - 1)
    def _(b):
        @pl.when(b < sq)
        def _():
            grad_block(b)
            g_copy(sq - b).start()

    li_wait(1, 2)
    li_start(4, 5)

    grad_block(sq)

    for g in range(GROUP):
        qg_out[:, g * HD : (g + 1) * HD] = dq_t[g].T.astype(BF)
    qg_copy = pltpu.make_async_copy(qg_out, qg_hbm, out_sem.at[0])
    qg_copy.start()

    for c in loads[10:]:
        c.wait()

    acc[...] = gsend[sq].astype(F32)

    @pl.loop(1, NS)
    def _(d):
        @pl.when(sq + d < NS)
        def _():
            g_arrived(d).wait_recv()
            acc[...] += grecv[d - 1].astype(F32)

    kv_low[...] = acc[...].astype(BF)

    li_wait(3, 4, 5)
    for n in range(D // 512):
        cols = li_buf[:, :, n * 512 : (n + 1) * 512].reshape(ROWS, 512)
        li_t[n * 512 : (n + 1) * 512, :] = cols.T

    def core_copy(p):
        return remote(csend.at[p], ccr.at[p], core_ss.at[p], core_rs.at[p], other_core)

    def proj_part(which, p):
        rows = pl.ds(pl.multiple_of(which * HALF + p * PART, PART), PART)
        return dot(li_t[rows, :], kv_low[...], NN)

    for p in range(PARTS):
        csend[p] = proj_part(1 - core, p).astype(BF)
        core_copy(p).start()

    for n in range(D // 512):
        part = dot(kv_low[...], wcat[n * 512 : (n + 1) * 512, :], NT)
        ipart[:, :, n * 512 : (n + 1) * 512] = part.reshape(NZ, 32, 512)

    def z_copy(direction, k, half):
        return remote(
            zs.at[direction, k, half], zr.at[direction, k, half],
            z_ss.at[direction, k, half], z_rs.at[direction, k, half],
            z_mate(1 - 2 * direction),
        )

    def z_send(direction, k, half, add):
        t = lax.rem(hd + 4 - k, NZ) if direction == 0 else lax.rem(hd + 4 + k, NZ)
        term = ipart[t, :, half * HALF : (half + 1) * HALF]
        if add:
            z_copy(direction, k - 1, half).wait_recv()
            term = term + zr[direction, k - 1, half].astype(F32)
        zs[direction, k, half] = term.astype(BF)
        z_copy(direction, k, half).start()

    def z_step(k, half, add=True):
        z_send(0, k, half, add)
        z_send(1, k, 1 - half, add)

    z_step(0, 0, False)
    z_step(1, 1, False)

    def index(axis):
        return yi if axis else x

    def mate(axis, d):
        if axis:
            return y_mate(lax.rem(yi + d, NX))
        return x_mate(lax.rem(x + d, NX))

    def st1_copy(p, d):
        a = p % 2
        return remote(
            s1.at[p, lax.rem(index(a) + d, NX)], r1.at[p, d - 1],
            st1_ss.at[p, d - 1], st1_rs.at[p, d - 1], mate(a, d),
        )

    def st2_copy(p, d, arrived=False):
        a = 1 - p % 2
        own = index(a)
        slot = lax.rem(own - d + NX, NX) if arrived else own
        return remote(
            r2.at[p, own], r2.at[p, slot], st2_ss.at[p, d - 1], st2_rs.at[p, d - 1], mate(a, d)
        )

    def ag_copy(p, d, arrived=False):
        own = index(p % 2)
        ref = gfull.at[core, p, lax.rem(own - d + NX, NX) if arrived else own]
        return remote(ref, ref, ag_ss.at[p, d - 1], ag_rs.at[p, d - 1], mate(p % 2, d))

    def pair_copy(p, d, arrived=False):
        ref = gfull.at[1 - core if arrived else core, p, lax.rem(index(p % 2) - d + NX, NX)]
        return remote(ref, ref, p_ss.at[p, d], p_rs.at[p, d], other_core)

    for p in range(PARTS):
        h32[p] = proj_part(core, p).reshape(NX, SUB, 2 * HD)

    for p in range(PARTS):
        core_copy(p).wait_recv()
        term = h32[p] + ccr[p].astype(F32).reshape(NX, SUB, 2 * HD)
        h32[p] = term
        s1[p] = term.astype(BF)
        for d in (2, 1, 3):
            st1_copy(p, d).start()

    def stage2(p):
        term = h32[p, index(p % 2)]
        for d in (1, 3, 2):
            st1_copy(p, d).wait_recv()
            term = term + r1[p, d - 1].astype(F32)
        r2[p, index(1 - p % 2)] = term.astype(BF)
        for d in (2, 1, 3):
            st2_copy(p, d).start()

    def gather(p):
        for d in (1, 3, 2):
            st2_copy(p, d, True).wait_recv()
        term = r2[p, 0].astype(F32)
        for i in range(1, NX):
            term = term + r2[p, i].astype(F32)
        gfull[core, p, index(p % 2)] = term.astype(BF)
        for d in (2, 1, 3):
            ag_copy(p, d).start()
        pair_copy(p, 0).start()

    def hand_over(p):
        for d in (1, 3, 2):
            ag_copy(p, d, True).wait_recv()
            pair_copy(p, d).start()

    z_step(1, 0)
    stage2(0)
    stage2(1)
    z_step(2, 1)
    stage2(2)
    stage2(3)
    z_step(2, 0)
    gather(0)
    gather(1)
    z_step(3, 1)
    gather(2)
    gather(3)
    z_step(3, 0)
    hand_over(0)
    hand_over(1)

    for half in range(2):
        term = ipart[hd, :, half * HALF : (half + 1) * HALF]
        for direction in range(2):
            z_copy(direction, 3, half).wait_recv()
            term = term + zr[direction, 3, half].astype(F32)
        ig_out[:, half * HALF : (half + 1) * HALF] = term.astype(BF)
    ig_copy = pltpu.make_async_copy(ig_out, ig_hbm, out_sem.at[1])
    ig_copy.start()

    hand_over(2)
    hand_over(3)

    for p in range(PARTS):
        for d in range(NX):
            pair_copy(p, d, True).wait_recv()
    gp_copy = pltpu.make_async_copy(gfull, gp_hbm, out_sem.at[2])
    gp_copy.start()

    for d in range(1, NS):

        @pl.when(sq + d < NS)
        def _():
            kv_copy(sq, seq_mate(sq + d), d - 1).wait_send()

        @pl.when(d <= sq)
        def _():
            g_copy(d).wait_send()

    for direction in range(2):
        for n in range(6):
            li_copy(direction, n).wait_send()
        for k in range(4):
            for half in range(2):
                if k > 0 or half == direction:
                    z_copy(direction, k, half).wait_send()
    for p in range(PARTS):
        core_copy(p).wait_send()
        for d in range(1, NX):
            st1_copy(p, d).wait_send()
            st2_copy(p, d).wait_send()
            ag_copy(p, d).wait_send()
        for d in range(NX):
            pair_copy(p, d).wait_send()
    qg_copy.wait()
    ig_copy.wait()
    gp_copy.wait()


def finish(qg_in, ig_in, gp_in, qg_ref, ig_ref, gk_ref, gv_ref, low, key, value, sem_in, sem_key, sem_value, sem):
    copies = [
        pltpu.make_async_copy(qg_in, qg_ref, sem.at[0]),
        pltpu.make_async_copy(ig_in, ig_ref, sem.at[1]),
    ]
    step = D // PIECES
    loads = []
    for n in range(PIECES):
        loads.append(pltpu.make_async_copy(gp_in.at[pl.ds(n * step, step), :], low.at[n], sem_in.at[n]))
        loads[-1].start()
    for c in copies:
        c.start()
    for n in range(PIECES):
        rows = pl.ds(n * step, step)
        loads[n].wait()
        key[n] = low[n, :, 0:HD].astype(F32)
        copies.append(pltpu.make_async_copy(key.at[n], gk_ref.at[rows, :], sem_key.at[n]))
        copies[-1].start()
        value[n] = low[n, :, HD:].astype(F32)
        copies.append(pltpu.make_async_copy(value.at[n], gv_ref.at[rows, :], sem_value.at[n]))
        copies[-1].start()
    for c in copies:
        c.wait()


def shards(queries, key_cache, value_cache, out_grad, doc_ids, layer_input, key_proj, value_proj):
    hbm = pl.BlockSpec(memory_space=pl.ANY)
    dma = pltpu.SemaphoreType.DMA
    scratch = [
        pltpu.VMEM((GROUP, ROWS, HD), BF),
        pltpu.VMEM((GROUP, ROWS, HD), BF),
        pltpu.VMEM((1, ROWS), jnp.int32),
        pltpu.VMEM((NS, 2 * ROWS + 16, HD), BF),
        pltpu.VMEM((NZ, 32, D), BF),
        pltpu.VMEM((D, ROWS), BF),
        pltpu.VMEM((D, 2 * HD), BF),
        pltpu.VMEM((NS, GROUP, ROWS, ROWS), F32),
        pltpu.VMEM((NS, GROUP, ROWS, ROWS), F32),
        pltpu.VMEM((NS, 8, ROWS), F32),
        pltpu.VMEM((NS, 8, ROWS), F32),
        pltpu.VMEM((NS, 8, ROWS), F32),
        pltpu.VMEM((NS, 8, ROWS), F32),
        pltpu.VMEM((GROUP, HD, ROWS), F32),
        pltpu.VMEM((NS, ROWS, 2 * HD), BF),
        pltpu.VMEM((NS - 1, ROWS, 2 * HD), BF),
        pltpu.VMEM((ROWS, 2 * HD), F32),
        pltpu.VMEM((ROWS, 2 * HD), BF),
        pltpu.VMEM((NZ, 32, D), F32),
        pltpu.VMEM((2, 4, 2, 32, HALF), BF),
        pltpu.VMEM((2, 4, 2, 32, HALF), BF),
        pltpu.VMEM((32, D), BF),
        pltpu.VMEM((PARTS, PART, 2 * HD), BF),
        pltpu.VMEM((PARTS, PART, 2 * HD), BF),
        pltpu.VMEM((PARTS, NX, SUB, 2 * HD), F32),
        pltpu.VMEM((PARTS, NX, SUB, 2 * HD), BF),
        pltpu.VMEM((PARTS, NX - 1, SUB, 2 * HD), BF),
        pltpu.VMEM((PARTS, NX, SUB, 2 * HD), BF),
        pltpu.VMEM((2, PARTS, NX, SUB, 2 * HD), BF),
        pltpu.VMEM((ROWS, GROUP * HD), BF),
        dma((12,)),
        dma((NS - 1,)),
        dma((NS,)),
        dma((2, 6)),
        dma((2, 6)),
        dma((NS - 1,)),
        dma((NS - 1,)),
        dma((2, 4, 2)),
        dma((2, 4, 2)),
        dma((PARTS,)),
        dma((PARTS,)),
        dma((PARTS, 3)),
        dma((PARTS, 3)),
        dma((PARTS, 3)),
        dma((PARTS, 3)),
        dma((PARTS, 3)),
        dma((PARTS, 3)),
        dma((PARTS, 4)),
        dma((PARTS, 4)),
        dma((3,)),
    ]
    qg, ig, gp = pl.pallas_call(
        kernel,
        out_shape=(
            jax.ShapeDtypeStruct((ROWS, GROUP * HD), BF),
            jax.ShapeDtypeStruct((32, D), BF),
            jax.ShapeDtypeStruct((2, PARTS, NX, SUB, 2 * HD), BF),
        ),
        in_specs=[hbm] * 8,
        out_specs=(hbm, hbm, hbm),
        scratch_shapes=scratch,
        compiler_params=pltpu.CompilerParams(
            collective_id=0, has_side_effects=True, vmem_limit_bytes=56 * 1024 * 1024
        ),
        cost_estimate=pl.CostEstimate(
            flops=3 * 10**9, bytes_accessed=8 * 10**6, transcendentals=2 * 10**6
        ),
    )(
        queries[0], key_cache[0], value_cache[0], out_grad[0], doc_ids, layer_input[0],
        key_proj, value_proj,
    )
    step = D // PIECES
    qg, ig, gk, gv = pl.pallas_call(
        finish,
        out_shape=(
            jax.ShapeDtypeStruct((ROWS, GROUP * HD), BF),
            jax.ShapeDtypeStruct((32, D), BF),
            jax.ShapeDtypeStruct((D, HD), F32),
            jax.ShapeDtypeStruct((D, HD), F32),
        ),
        in_specs=[hbm] * 3,
        out_specs=(hbm,) * 4,
        scratch_shapes=[
            pltpu.VMEM((PIECES, step, 2 * HD), BF),
            pltpu.VMEM((PIECES, step, HD), F32),
            pltpu.VMEM((PIECES, step, HD), F32),
            dma((PIECES,)),
            dma((PIECES,)),
            dma((PIECES,)),
            dma((2,)),
        ],
        compiler_params=pltpu.CompilerParams(vmem_limit_bytes=60 * 1024 * 1024),
        cost_estimate=pl.CostEstimate(flops=0, bytes_accessed=6 * 10**6, transcendentals=0),
    )(qg, ig, gp.reshape(D, 2 * HD))
    return qg[None], ig[None], gk, gv


def solution(mesh):
    return jax.shard_map(
        shards,
        mesh=mesh,
        in_specs=(
            P("dp", "seq", "head"),
            P("dp", "seq", "head"),
            P("dp", "seq", "head"),
            P("dp", "seq", "head"),
            P("dp", "seq"),
            P("dp", ("seq", "head"), None),
            P(None, "head"),
            P(None, "head"),
        ),
        out_specs=(
            P("dp", "seq", "head"),
            P("dp", ("seq", "head"), None),
            P(None, "head"),
            P(None, "head"),
        ),
        check_vma=False,
    )
```

```python
import functools
import math

import jax
import jax.numpy as jnp
from jax import lax
from jax.experimental import pallas as pl
from jax.experimental.pallas import tpu as pltpu
from jax.sharding import PartitionSpec as P

D = 3072
HD = 128
GROUP = 3
ROWS = 256
NX = 4
NZ = 8
NEG_FILL = -1e30
SCALE = HD ** (-0.5)
EXP_SCALE = SCALE * math.log2(math.e)
HALF = D // 2
NS = 8
PARTS = 4
PART = HALF // PARTS
SUB = PART // NX
PIECES = 4
BF = jnp.bfloat16
F32 = jnp.float32
NT = (((1,), (1,)), ((), ()))
NN = (((1,), (0,)), ((), ()))


def dot(a, b, dims):
    return lax.dot_general(a, b, dims, preferred_element_type=F32)


def kernel(
    q_hbm, k_hbm, v_hbm, do_hbm, docs_hbm, li_hbm, wk_hbm, wv_hbm,
    qg_hbm, ig_hbm, gp_hbm,
    q_v, do_v, docs_ref, kvbuf, li_buf, li_t, wcat,
    p_buf, dp_buf, m_buf, l_buf, a_buf, f_buf, dq_t,
    gsend, grecv, crecv, xsend, xrecv, acc, kv_low,
    ipart, zs, zr, ig_out,
    csend, ccr, h32, s1, r1, r2, gfull, qg_out,
    loc, kv_ss, kv_rs, li_ss, li_rs, g_ss, g_rs, c_ss, c_rs, x_ss, x_rs,
    z_ss, z_rs, core_ss, core_rs, st1_ss, st1_rs, st2_ss, st2_rs,
    ag_ss, ag_rs, p_ss, p_rs, out_sem, gp_sem,
):
    dp = lax.axis_index("dp")
    sq = lax.axis_index("seq")
    hd = lax.axis_index("head")
    core = lax.rem(dp, 2)
    y_lo = lax.div(dp, 2)
    y_hi = lax.div(sq, NX)
    x = lax.rem(sq, NX)
    yi = y_hi * 2 + y_lo

    def x_mate(idx):
        return (dp, y_hi * NX + idx, hd)

    def y_mate(idx):
        return (lax.rem(idx, 2) * 2 + core, lax.div(idx, 2) * NX + x, hd)

    other_half = (dp, (1 - y_hi) * NX + x, hd)
    far_x = lax.rem(x + 2, NX)
    far_mate = (dp, (1 - y_hi) * NX + far_x, hd)
    other_core = (y_lo * 2 + 1 - core, sq, hd)

    def z_mate(d):
        return (dp, sq, lax.rem(hd + d + NZ, NZ))

    def remote(src, dst, ssem, rsem, dev):
        return pltpu.make_async_remote_copy(
            src_ref=src, dst_ref=dst, send_sem=ssem, recv_sem=rsem,
            device_id=dev, device_id_type=pl.DeviceIdType.MESH,
        )

    barrier = pltpu.get_barrier_semaphore()
    partners = [x_mate(lax.rem(x + d, NX)) for d in range(1, NX)]
    partners += [y_mate(lax.rem(yi + d, NX)) for d in range(1, NX)]
    partners += [far_mate, other_core, z_mate(1), z_mate(-1)]
    for dev in partners:
        pl.semaphore_signal(barrier, inc=1, device_id=dev, device_id_type=pl.DeviceIdType.MESH)

    loads = [
        pltpu.make_async_copy(docs_hbm, docs_ref, loc.at[0]),
        pltpu.make_async_copy(k_hbm, kvbuf.at[sq, pl.ds(0, ROWS), :], loc.at[1]),
        pltpu.make_async_copy(v_hbm, kvbuf.at[sq, pl.ds(ROWS, ROWS), :], loc.at[2]),
        pltpu.make_async_copy(li_hbm, li_buf.at[hd], loc.at[3]),
    ]
    for g in range(GROUP):
        loads.append(pltpu.make_async_copy(q_hbm.at[:, pl.ds(g * HD, HD)], q_v.at[g], loc.at[4 + g]))
        loads.append(pltpu.make_async_copy(do_hbm.at[:, pl.ds(g * HD, HD)], do_v.at[g], loc.at[7 + g]))
    loads.append(pltpu.make_async_copy(wk_hbm, wcat.at[:, pl.ds(0, HD)], loc.at[10]))
    loads.append(pltpu.make_async_copy(wv_hbm, wcat.at[:, pl.ds(HD, HD)], loc.at[11]))
    for c in loads:
        c.start()

    m_buf[...] = jnp.full(m_buf.shape, NEG_FILL, F32)
    l_buf[...] = jnp.zeros(l_buf.shape, F32)
    a_buf[...] = jnp.zeros(a_buf.shape, F32)
    dq_t[...] = jnp.zeros(dq_t.shape, F32)

    loads[0].wait()
    doc_row = docs_ref[...].astype(F32)
    upper = lax.broadcasted_iota(jnp.int32, (16, HD), 0) < 8
    doc_tile = jnp.where(
        upper,
        jnp.broadcast_to(doc_row[:, 0:HD], (16, HD)),
        jnp.broadcast_to(doc_row[:, HD:], (16, HD)),
    )
    kvbuf[sq, pl.ds(2 * ROWS, 16), :] = doc_tile.astype(BF)
    for c in loads[1:4]:
        c.wait()
    for c in loads[4:10]:
        c.wait()

    key_iota = lax.broadcasted_iota(jnp.int32, (ROWS, ROWS), 0).astype(F32)

    def score_block(b, diagonal):
        kb = kvbuf[b, pl.ds(0, ROWS), :]
        vb = kvbuf[b, pl.ds(ROWS, ROWS), :]
        docs = kvbuf[b, pl.ds(2 * ROWS, 16), :].astype(F32)
        ones = jnp.sum(jnp.sum(docs, axis=0, keepdims=True), axis=1, keepdims=True) * 0.125
        zeros = ROWS - ones
        low = doc_row * zeros
        high = zeros + doc_row * ones
        if diagonal:
            own = lax.broadcasted_iota(jnp.int32, (1, ROWS), 1).astype(F32)
            high = jnp.minimum(high, own + 1.0)
        allowed = (key_iota >= low) & (key_iota < high)
        for g in range(GROUP):
            s = jnp.where(allowed, dot(kb, q_v[g], NT), NEG_FILL)
            top = jnp.max(s, axis=0, keepdims=True)
            p = jnp.exp2((s - top) * EXP_SCALE)
            wg = dot(vb, do_v[g], NT)
            p_buf[b, g] = p
            dp_buf[b, g] = wg
            m_buf[b, g : g + 1, :] = top
            l_buf[b, g : g + 1, :] = jnp.sum(p, axis=0, keepdims=True)
            a_buf[b, g : g + 1, :] = jnp.sum(p * wg, axis=0, keepdims=True)

    score_block(sq, True)
    pl.semaphore_wait(barrier, len(partners))

    def kv_copy(block, dev, s):
        return remote(kvbuf.at[block], kvbuf.at[block], kv_ss.at[s], kv_rs.at[block], dev)

    def kv_arrived(block):
        return kv_copy(block, other_half, 0)

    @pl.when(y_hi == 0)
    def _():
        kv_copy(sq, other_half, 3).start()
        kv_copy(sq, far_mate, 4).start()

    for d in (2, 1, 3):
        xt = lax.rem(x + d, NX)

        @pl.when(xt > x)
        def _():
            kv_copy(sq, x_mate(xt), d - 1).start()

    def li_copy(direction, n, arrived=False):
        sign = 1 - 2 * direction
        away = n // 2 + 1 if arrived else n // 2
        half = direction if n == 6 else n % 2
        ref = li_buf.at[lax.rem(hd - sign * away + NZ, NZ), pl.ds(16 * half, 16), :]
        return remote(ref, ref, li_ss.at[direction, n], li_rs.at[direction, n], z_mate(sign))

    def li_start(n):
        for direction in range(2):
            li_copy(direction, n).start()

    def li_wait(n):
        for direction in range(2):
            li_copy(direction, n, True).wait_recv()

    def li_next(n):
        li_wait(n)
        if n == 4:
            li_copy(0, 6).start()
        elif n == 5:
            li_copy(1, 6).start()
        else:
            li_start(n + 2)

    li_start(0)
    li_start(1)
    li_next(0)

    @pl.when(y_hi == 1)
    def _():
        kv_arrived(x).wait_recv()
        for n, d in enumerate((1, 3)):
            kv_copy(x, x_mate(lax.rem(x + d, NX)), 5 + n).start()

    @pl.loop(1, NX)
    def _(d):
        @pl.when(d <= x)
        def _():
            kv_arrived(sq - d).wait_recv()
            score_block(sq - d, False)

    li_next(1)

    @pl.when(y_hi == 1)
    def _():
        score_block(x, False)

    li_next(2)

    @pl.when(y_hi == 1)
    def _():
        @pl.loop(0, NX - 1)
        def _(n):
            b = lax.rem(x + 2 + n + lax.div(n, 2), NX)
            kv_arrived(b).wait_recv()
            score_block(b, False)

    li_next(3)

    top = jnp.max(m_buf[...], axis=0)
    factor = jnp.exp2((m_buf[...] - top[None]) * EXP_SCALE)
    total = jnp.sum(factor * l_buf[...], axis=0)
    gathered = jnp.sum(factor * a_buf[...], axis=0)
    safe = jnp.where(total > 0.0, total, 1.0)
    inv = 1.0 / safe
    delta = gathered * inv
    f_buf[...] = factor * inv[None]

    def grad_block(b):
        kbt = kvbuf[b, pl.ds(0, ROWS), :].T
        dk = jnp.zeros((ROWS, HD), F32)
        dv = jnp.zeros((ROWS, HD), F32)
        for g in range(GROUP):
            w = p_buf[b, g] * f_buf[b, g : g + 1, :]
            sg = (w * (dp_buf[b, g] - delta[g : g + 1, :]) * SCALE).astype(BF)
            dv = dv + dot(w.astype(BF), do_v[g], NN)
            dk = dk + dot(sg, q_v[g], NN)
            dq_t[g] += dot(kbt, sg, NN)
        gsend[b, :, 0:HD] = dk.astype(BF)
        gsend[b, :, HD:] = dv.astype(BF)

    def g_copy(d):
        xt = lax.rem(x + d, NX)
        return remote(
            gsend.at[y_hi * NX + xt], grecv.at[d - 1], g_ss.at[d - 1], g_rs.at[d - 1], x_mate(xt)
        )

    def c_copy(n):
        xt = lax.rem(x + 1 + 2 * n, NX)
        return remote(gsend.at[xt], crecv.at[n], c_ss.at[n], c_rs.at[n], x_mate(xt))

    far_copy = remote(gsend.at[far_x], xrecv.at[0], x_ss.at[0], x_rs.at[0], far_mate)
    cross = remote(xsend, xrecv.at[1], x_ss.at[1], x_rs.at[1], other_half)

    @pl.when(y_hi == 1)
    def _():
        grad_block(far_x)
        far_copy.start()

        @pl.loop(0, 2)
        def _(n):
            grad_block(lax.rem(x + 1 + 2 * n, NX))
            c_copy(n).start()

    li_next(4)

    @pl.when(y_hi == 1)
    def _():
        grad_block(x)

    @pl.loop(1, NX)
    def _(d):
        xt = lax.rem(x + d, NX)

        @pl.when(xt < x)
        def _():
            grad_block(y_hi * NX + xt)
            g_copy(d).start()

    li_next(5)

    @pl.when(y_hi == 1)
    def _():
        acc[...] = gsend[x].astype(F32)
        for n in range(2):
            c_copy(n).wait_recv()
            acc[...] += crecv[n].astype(F32)
        xsend[...] = acc[...].astype(BF)
        cross.start()

    grad_block(sq)

    for g in range(GROUP):
        qg_out[:, g * HD : (g + 1) * HD] = dq_t[g].T.astype(BF)
    qg_copy = pltpu.make_async_copy(qg_out, qg_hbm, out_sem.at[0])
    qg_copy.start()

    for c in loads[10:]:
        c.wait()

    li_wait(6)
    for n in range(D // 512):
        cols = li_buf[:, :, n * 512 : (n + 1) * 512].reshape(ROWS, 512)
        li_t[n * 512 : (n + 1) * 512, :] = cols.T

    acc[...] = gsend[sq].astype(F32)

    for d in range(1, NX):

        @pl.when(lax.rem(x - d + NX, NX) > x)
        def _():
            g_copy(d).wait_recv()
            acc[...] += grecv[d - 1].astype(F32)

    @pl.when(y_hi == 0)
    def _():
        far_copy.wait_recv()
        cross.wait_recv()
        acc[...] += xrecv[0].astype(F32) + xrecv[1].astype(F32)

    kv_low[...] = acc[...].astype(BF)

    def core_copy(p):
        return remote(csend.at[p], ccr.at[p], core_ss.at[p], core_rs.at[p], other_core)

    def proj_part(which, p):
        rows = pl.ds(pl.multiple_of(which * HALF + p * PART, PART), PART)
        return dot(li_t[rows, :], kv_low[...], NN)

    for p in range(PARTS):
        csend[p] = proj_part(1 - core, p).astype(BF)
        core_copy(p).start()

    for n in range(D // 512):
        part = dot(kv_low[...], wcat[n * 512 : (n + 1) * 512, :], NT)
        ipart[:, :, n * 512 : (n + 1) * 512] = part.reshape(NZ, 32, 512)

    def z_copy(direction, k, half):
        return remote(
            zs.at[direction, k, half], zr.at[direction, k, half],
            z_ss.at[direction, k, half], z_rs.at[direction, k, half],
            z_mate(1 - 2 * direction),
        )

    def z_send(direction, k, half, add):
        t = lax.rem(hd + 4 - k, NZ) if direction == 0 else lax.rem(hd + 4 + k, NZ)
        term = ipart[t, :, half * HALF : (half + 1) * HALF]
        if add:
            z_copy(direction, k - 1, half).wait_recv()
            term = term + zr[direction, k - 1, half].astype(F32)
        zs[direction, k, half] = term.astype(BF)
        z_copy(direction, k, half).start()

    def z_step(k, half, add=True):
        z_send(0, k, half, add)
        z_send(1, k, 1 - half, add)

    z_step(0, 0, False)
    z_step(1, 1, False)

    def index(axis):
        return yi if axis else x

    def mate(axis, d):
        if axis:
            return y_mate(lax.rem(yi + d, NX))
        return x_mate(lax.rem(x + d, NX))

    def st1_copy(p, d):
        a = p % 2
        return remote(
            s1.at[p, lax.rem(index(a) + d, NX)], r1.at[p, d - 1],
            st1_ss.at[p, d - 1], st1_rs.at[p, d - 1], mate(a, d),
        )

    def st2_copy(p, d, arrived=False):
        a = 1 - p % 2
        own = index(a)
        slot = lax.rem(own - d + NX, NX) if arrived else own
        return remote(
            r2.at[p, own], r2.at[p, slot], st2_ss.at[p, d - 1], st2_rs.at[p, d - 1], mate(a, d)
        )

    def ag_copy(p, d, arrived=False):
        own = index(p % 2)
        ref = gfull.at[core, p, lax.rem(own - d + NX, NX) if arrived else own]
        return remote(ref, ref, ag_ss.at[p, d - 1], ag_rs.at[p, d - 1], mate(p % 2, d))

    def pair_copy(p, d, arrived=False):
        ref = gfull.at[1 - core if arrived else core, p, lax.rem(index(p % 2) - d + NX, NX)]
        return remote(ref, ref, p_ss.at[p, d], p_rs.at[p, d], other_core)

    for p in range(PARTS):
        h32[p] = proj_part(core, p).reshape(NX, SUB, 2 * HD)

    for p in range(PARTS):
        core_copy(p).wait_recv()
        term = h32[p] + ccr[p].astype(F32).reshape(NX, SUB, 2 * HD)
        h32[p] = term
        s1[p] = term.astype(BF)
        for d in (2, 1, 3):
            st1_copy(p, d).start()

    def stage2(p):
        term = h32[p, index(p % 2)]
        for d in (1, 3, 2):
            st1_copy(p, d).wait_recv()
            term = term + r1[p, d - 1].astype(F32)
        r2[p, index(1 - p % 2)] = term.astype(BF)
        for d in (2, 1, 3):
            st2_copy(p, d).start()

    def gather(p):
        for d in (1, 3, 2):
            st2_copy(p, d, True).wait_recv()
        term = r2[p, 0].astype(F32)
        for i in range(1, NX):
            term = term + r2[p, i].astype(F32)
        gfull[core, p, index(p % 2)] = term.astype(BF)
        for d in (2, 1, 3):
            ag_copy(p, d).start()
        pair_copy(p, 0).start()

    def hand_over(p):
        for d in (1, 3, 2):
            ag_copy(p, d, True).wait_recv()
            pair_copy(p, d).start()

    z_step(1, 0)
    stage2(0)
    stage2(1)
    z_step(2, 1)
    stage2(2)
    stage2(3)
    z_step(2, 0)
    gather(0)
    gather(1)
    z_step(3, 1)
    gather(2)
    gather(3)
    z_step(3, 0)
    hand_over(0)
    hand_over(1)

    for half in range(2):
        term = ipart[hd, :, half * HALF : (half + 1) * HALF]
        for direction in range(2):
            z_copy(direction, 3, half).wait_recv()
            term = term + zr[direction, 3, half].astype(F32)
        ig_out[:, half * HALF : (half + 1) * HALF] = term.astype(BF)
    ig_copy = pltpu.make_async_copy(ig_out, ig_hbm, out_sem.at[1])
    ig_copy.start()

    def gp_copy(c, p):
        return pltpu.make_async_copy(gfull.at[c, p], gp_hbm.at[c, p], gp_sem.at[c, p])

    def part_done(p):
        for d in range(NX):
            pair_copy(p, d, True).wait_recv()
        for c in range(2):
            gp_copy(c, p).start()

    hand_over(2)
    part_done(0)
    part_done(1)
    hand_over(3)
    part_done(2)
    part_done(3)

    for d in range(1, NX):
        xt = lax.rem(x + d, NX)

        @pl.when(xt > x)
        def _():
            kv_copy(sq, x_mate(xt), d - 1).wait_send()

        @pl.when(xt < x)
        def _():
            g_copy(d).wait_send()

    @pl.when(y_hi == 0)
    def _():
        kv_copy(sq, other_half, 3).wait_send()
        kv_copy(sq, far_mate, 4).wait_send()

    @pl.when(y_hi == 1)
    def _():
        for n, d in enumerate((1, 3)):
            kv_copy(x, x_mate(lax.rem(x + d, NX)), 5 + n).wait_send()
            c_copy(n).wait_send()
        far_copy.wait_send()
        cross.wait_send()

    for direction in range(2):
        for n in range(7):
            li_copy(direction, n).wait_send()
        for k in range(4):
            for half in range(2):
                if k > 0 or half == direction:
                    z_copy(direction, k, half).wait_send()
    for p in range(PARTS):
        core_copy(p).wait_send()
        for d in range(1, NX):
            st1_copy(p, d).wait_send()
            st2_copy(p, d).wait_send()
            ag_copy(p, d).wait_send()
        for d in range(NX):
            pair_copy(p, d).wait_send()
    qg_copy.wait()
    ig_copy.wait()
    for p in range(PARTS):
        for c in range(2):
            gp_copy(c, p).wait()


def finish(
    qg_in, ig_in, gp_in, qg_ref, ig_ref, gk_ref, gv_ref,
    low, key, value, qg_v, ig_v, sem_in, sem_key, sem_value, sem,
):
    step = D // PIECES
    loads = [
        pltpu.make_async_copy(gp_in.at[pl.ds(n * step, step), :], low.at[n], sem_in.at[n])
        for n in range(PIECES)
    ]
    loads.append(pltpu.make_async_copy(qg_in, qg_v, sem.at[0]))
    loads.append(pltpu.make_async_copy(ig_in, ig_v, sem.at[1]))
    for c in loads:
        c.start()
    copies = []
    for n in range(PIECES):
        rows = pl.ds(n * step, step)
        loads[n].wait()
        key[n] = low[n, :, 0:HD].astype(F32)
        copies.append(pltpu.make_async_copy(key.at[n], gk_ref.at[rows, :], sem_key.at[n]))
        copies[-1].start()
        value[n] = low[n, :, HD:].astype(F32)
        copies.append(pltpu.make_async_copy(value.at[n], gv_ref.at[rows, :], sem_value.at[n]))
        copies[-1].start()
    loads[PIECES].wait()
    copies.append(pltpu.make_async_copy(qg_v, qg_ref, sem.at[2]))
    copies[-1].start()
    loads[PIECES + 1].wait()
    copies.append(pltpu.make_async_copy(ig_v, ig_ref, sem.at[3]))
    copies[-1].start()
    for c in copies:
        c.wait()


def shards(queries, key_cache, value_cache, out_grad, doc_ids, layer_input, key_proj, value_proj):
    hbm = pl.BlockSpec(memory_space=pl.ANY)
    dma = pltpu.SemaphoreType.DMA
    scratch = [
        pltpu.VMEM((GROUP, ROWS, HD), BF),
        pltpu.VMEM((GROUP, ROWS, HD), BF),
        pltpu.VMEM((1, ROWS), jnp.int32),
        pltpu.VMEM((NS, 2 * ROWS + 16, HD), BF),
        pltpu.VMEM((NZ, 32, D), BF),
        pltpu.VMEM((D, ROWS), BF),
        pltpu.VMEM((D, 2 * HD), BF),
        pltpu.VMEM((NS, GROUP, ROWS, ROWS), F32),
        pltpu.VMEM((NS, GROUP, ROWS, ROWS), F32),
        pltpu.VMEM((NS, 8, ROWS), F32),
        pltpu.VMEM((NS, 8, ROWS), F32),
        pltpu.VMEM((NS, 8, ROWS), F32),
        pltpu.VMEM((NS, 8, ROWS), F32),
        pltpu.VMEM((GROUP, HD, ROWS), F32),
        pltpu.VMEM((NS, ROWS, 2 * HD), BF),
        pltpu.VMEM((NX - 1, ROWS, 2 * HD), BF),
        pltpu.VMEM((2, ROWS, 2 * HD), BF),
        pltpu.VMEM((ROWS, 2 * HD), BF),
        pltpu.VMEM((2, ROWS, 2 * HD), BF),
        pltpu.VMEM((ROWS, 2 * HD), F32),
        pltpu.VMEM((ROWS, 2 * HD), BF),
        pltpu.VMEM((NZ, 32, D), F32),
        pltpu.VMEM((2, 4, 2, 32, HALF), BF),
        pltpu.VMEM((2, 4, 2, 32, HALF), BF),
        pltpu.VMEM((32, D), BF),
        pltpu.VMEM((PARTS, PART, 2 * HD), BF),
        pltpu.VMEM((PARTS, PART, 2 * HD), BF),
        pltpu.VMEM((PARTS, NX, SUB, 2 * HD), F32),
        pltpu.VMEM((PARTS, NX, SUB, 2 * HD), BF),
        pltpu.VMEM((PARTS, NX - 1, SUB, 2 * HD), BF),
        pltpu.VMEM((PARTS, NX, SUB, 2 * HD), BF),
        pltpu.VMEM((2, PARTS, NX, SUB, 2 * HD), BF),
        pltpu.VMEM((ROWS, GROUP * HD), BF),
        dma((12,)),
        dma((7,)),
        dma((NS,)),
        dma((2, 7)),
        dma((2, 7)),
        dma((NX - 1,)),
        dma((NX - 1,)),
        dma((2,)),
        dma((2,)),
        dma((2,)),
        dma((2,)),
        dma((2, 4, 2)),
        dma((2, 4, 2)),
        dma((PARTS,)),
        dma((PARTS,)),
        dma((PARTS, 3)),
        dma((PARTS, 3)),
        dma((PARTS, 3)),
        dma((PARTS, 3)),
        dma((PARTS, 3)),
        dma((PARTS, 3)),
        dma((PARTS, 4)),
        dma((PARTS, 4)),
        dma((2,)),
        dma((2, PARTS)),
    ]
    qg, ig, gp = pl.pallas_call(
        kernel,
        out_shape=(
            jax.ShapeDtypeStruct((ROWS, GROUP * HD), BF),
            jax.ShapeDtypeStruct((32, D), BF),
            jax.ShapeDtypeStruct((2, PARTS, NX, SUB, 2 * HD), BF),
        ),
        in_specs=[hbm] * 8,
        out_specs=(hbm, hbm, hbm),
        scratch_shapes=scratch,
        compiler_params=pltpu.CompilerParams(
            collective_id=0, has_side_effects=True, vmem_limit_bytes=56 * 1024 * 1024
        ),
        cost_estimate=pl.CostEstimate(
            flops=3 * 10**9, bytes_accessed=8 * 10**6, transcendentals=2 * 10**6
        ),
    )(
        queries[0], key_cache[0], value_cache[0], out_grad[0], doc_ids, layer_input[0],
        key_proj, value_proj,
    )
    step = D // PIECES
    qg, ig, gk, gv = pl.pallas_call(
        finish,
        out_shape=(
            jax.ShapeDtypeStruct((ROWS, GROUP * HD), BF),
            jax.ShapeDtypeStruct((32, D), BF),
            jax.ShapeDtypeStruct((D, HD), F32),
            jax.ShapeDtypeStruct((D, HD), F32),
        ),
        in_specs=[hbm] * 3,
        out_specs=(hbm,) * 4,
        scratch_shapes=[
            pltpu.VMEM((PIECES, step, 2 * HD), BF),
            pltpu.VMEM((PIECES, step, HD), F32),
            pltpu.VMEM((PIECES, step, HD), F32),
            pltpu.VMEM((ROWS, GROUP * HD), BF),
            pltpu.VMEM((32, D), BF),
            dma((PIECES,)),
            dma((PIECES,)),
            dma((PIECES,)),
            dma((4,)),
        ],
        compiler_params=pltpu.CompilerParams(vmem_limit_bytes=60 * 1024 * 1024),
        cost_estimate=pl.CostEstimate(flops=0, bytes_accessed=6 * 10**6, transcendentals=0),
    )(qg, ig, gp.reshape(D, 2 * HD))
    return qg[None], ig[None], gk, gv


def solution(mesh):
    return jax.shard_map(
        shards,
        mesh=mesh,
        in_specs=(
            P("dp", "seq", "head"),
            P("dp", "seq", "head"),
            P("dp", "seq", "head"),
            P("dp", "seq", "head"),
            P("dp", "seq"),
            P("dp", ("seq", "head"), None),
            P(None, "head"),
            P(None, "head"),
        ),
        out_specs=(
            P("dp", "seq", "head"),
            P("dp", ("seq", "head"), None),
            P(None, "head"),
            P(None, "head"),
        ),
        check_vma=False,
    )
```

```python
import functools
import math

import jax
import jax.numpy as jnp
from jax import lax
from jax.experimental import pallas as pl
from jax.experimental.pallas import tpu as pltpu
from jax.sharding import PartitionSpec as P

D = 3072
HD = 128
GROUP = 3
ROWS = 256
NX = 4
NZ = 8
NEG_FILL = -1e30
SCALE = HD ** (-0.5)
EXP_SCALE = SCALE * math.log2(math.e)
HALF = D // 2
NS = 8
PARTS = 4
PART = HALF // PARTS
SUB = PART // NX
PIECES = 4
BF = jnp.bfloat16
F32 = jnp.float32
NT = (((1,), (1,)), ((), ()))
NN = (((1,), (0,)), ((), ()))


def dot(a, b, dims):
    return lax.dot_general(a, b, dims, preferred_element_type=F32)


def kernel(
    q_hbm, k_hbm, v_hbm, do_hbm, docs_hbm, li_hbm, wk_hbm, wv_hbm,
    qg_hbm, ig_hbm, gp_hbm,
    q_v, do_v, docs_ref, kvbuf, li_buf, li_t, wcat,
    p_buf, dp_buf, m_buf, l_buf, a_buf, f_buf, dq_t,
    gsend, grecv, crecv, xsend, xrecv, frecv, acc, kv_low,
    ipart, zs, zr, ig_out,
    csend, ccr, h32, s1, r1, r2, gfull, qg_out,
    loc, kv_ss, kv_rs, kv_ps, kv_pr, li_ss, li_rs, g_ss, g_rs, c_ss, c_rs, x_ss, x_rs,
    z_ss, z_rs, core_ss, core_rs, st1_ss, st1_rs, st2_ss, st2_rs,
    ag_ss, ag_rs, p_ss, p_rs, out_sem, gp_sem,
):
    dp = lax.axis_index("dp")
    sq = lax.axis_index("seq")
    hd = lax.axis_index("head")
    core = lax.rem(dp, 2)
    y_lo = lax.div(dp, 2)
    y_hi = lax.div(sq, NX)
    x = lax.rem(sq, NX)
    yi = y_hi * 2 + y_lo

    def x_mate(idx):
        return (dp, y_hi * NX + idx, hd)

    def y_mate(idx):
        return (lax.rem(idx, 2) * 2 + core, lax.div(idx, 2) * NX + x, hd)

    other_half = (dp, (1 - y_hi) * NX + x, hd)
    far_x = lax.rem(x + 2, NX)
    far_mate = (dp, (1 - y_hi) * NX + far_x, hd)
    other_core = (y_lo * 2 + 1 - core, sq, hd)

    def z_mate(d):
        return (dp, sq, lax.rem(hd + d + NZ, NZ))

    def remote(src, dst, ssem, rsem, dev):
        return pltpu.make_async_remote_copy(
            src_ref=src, dst_ref=dst, send_sem=ssem, recv_sem=rsem,
            device_id=dev, device_id_type=pl.DeviceIdType.MESH,
        )

    barrier = pltpu.get_barrier_semaphore()
    partners = [x_mate(lax.rem(x + d, NX)) for d in range(1, NX)]
    partners += [y_mate(lax.rem(yi + d, NX)) for d in range(1, NX)]
    partners += [far_mate, other_core, z_mate(1), z_mate(-1)]
    for dev in partners:
        pl.semaphore_signal(barrier, inc=1, device_id=dev, device_id_type=pl.DeviceIdType.MESH)

    loads = [
        pltpu.make_async_copy(docs_hbm, docs_ref, loc.at[0]),
        pltpu.make_async_copy(k_hbm, kvbuf.at[sq, pl.ds(0, ROWS), :], loc.at[1]),
        pltpu.make_async_copy(v_hbm, kvbuf.at[sq, pl.ds(ROWS, ROWS), :], loc.at[2]),
        pltpu.make_async_copy(li_hbm, li_buf.at[hd], loc.at[3]),
    ]
    for g in range(GROUP):
        loads.append(pltpu.make_async_copy(q_hbm.at[:, pl.ds(g * HD, HD)], q_v.at[g], loc.at[4 + g]))
        loads.append(pltpu.make_async_copy(do_hbm.at[:, pl.ds(g * HD, HD)], do_v.at[g], loc.at[7 + g]))
    loads.append(pltpu.make_async_copy(wk_hbm, wcat.at[:, pl.ds(0, HD)], loc.at[10]))
    loads.append(pltpu.make_async_copy(wv_hbm, wcat.at[:, pl.ds(HD, HD)], loc.at[11]))
    for c in loads:
        c.start()

    m_buf[...] = jnp.full(m_buf.shape, NEG_FILL, F32)
    l_buf[...] = jnp.zeros(l_buf.shape, F32)
    a_buf[...] = jnp.zeros(a_buf.shape, F32)
    dq_t[...] = jnp.zeros(dq_t.shape, F32)

    loads[0].wait()
    doc_row = docs_ref[...].astype(F32)
    upper = lax.broadcasted_iota(jnp.int32, (16, HD), 0) < 8
    doc_tile = jnp.where(
        upper,
        jnp.broadcast_to(doc_row[:, 0:HD], (16, HD)),
        jnp.broadcast_to(doc_row[:, HD:], (16, HD)),
    )
    kvbuf[sq, pl.ds(2 * ROWS, 16), :] = doc_tile.astype(BF)
    for c in loads[1:4]:
        c.wait()
    for c in loads[4:10]:
        c.wait()

    key_iota = lax.broadcasted_iota(jnp.int32, (ROWS, ROWS), 0).astype(F32)

    def score_block(b, diagonal):
        kb = kvbuf[b, pl.ds(0, ROWS), :]
        vb = kvbuf[b, pl.ds(ROWS, ROWS), :]
        docs = kvbuf[b, pl.ds(2 * ROWS, 16), :].astype(F32)
        ones = jnp.sum(jnp.sum(docs, axis=0, keepdims=True), axis=1, keepdims=True) * 0.125
        zeros = ROWS - ones
        low = doc_row * zeros
        high = zeros + doc_row * ones
        if diagonal:
            own = lax.broadcasted_iota(jnp.int32, (1, ROWS), 1).astype(F32)
            high = jnp.minimum(high, own + 1.0)
        allowed = (key_iota >= low) & (key_iota < high)
        for g in range(GROUP):
            s = jnp.where(allowed, dot(kb, q_v[g], NT), NEG_FILL)
            top = jnp.max(s, axis=0, keepdims=True)
            p = jnp.exp2((s - top) * EXP_SCALE)
            wg = dot(vb, do_v[g], NT)
            p_buf[b, g] = p
            dp_buf[b, g] = wg
            m_buf[b, g : g + 1, :] = top
            l_buf[b, g : g + 1, :] = jnp.sum(p, axis=0, keepdims=True)
            a_buf[b, g : g + 1, :] = jnp.sum(p * wg, axis=0, keepdims=True)

    score_block(sq, True)
    pl.semaphore_wait(barrier, len(partners))

    def kv_copy(block, dev, s):
        return remote(kvbuf.at[block], kvbuf.at[block], kv_ss.at[s], kv_rs.at[block], dev)

    def kv_arrived(block):
        return kv_copy(block, other_half, 0)

    def kv_part(block, part, dev, s):
        ref = kvbuf.at[block, pl.ds(part * ROWS, ROWS + 16 * part), :]
        return remote(ref, ref, kv_ps.at[s], kv_pr.at[block, part], dev)

    @pl.when(y_hi == 0)
    def _():
        for part in range(2):
            kv_part(x, part, other_half, part).start()
        kv_copy(sq, far_mate, 3).start()

    for d in (2, 1, 3):
        xt = lax.rem(x + d, NX)

        @pl.when(xt > x)
        def _():
            kv_copy(sq, x_mate(xt), d - 1).start()

    def li_copy(direction, n, arrived=False):
        sign = 1 - 2 * direction
        away = n // 2 + 1 if arrived else n // 2
        half = direction if n == 6 else n % 2
        ref = li_buf.at[lax.rem(hd - sign * away + NZ, NZ), pl.ds(16 * half, 16), :]
        return remote(ref, ref, li_ss.at[direction, n], li_rs.at[direction, n], z_mate(sign))

    def li_start(n):
        for direction in range(2):
            li_copy(direction, n).start()

    def li_wait(n):
        for direction in range(2):
            li_copy(direction, n, True).wait_recv()

    def li_next(n):
        li_wait(n)
        if n == 4:
            li_copy(0, 6).start()
        elif n == 5:
            li_copy(1, 6).start()
        else:
            li_start(n + 2)

    li_start(0)
    li_start(1)
    li_next(0)

    @pl.when(y_hi == 1)
    def _():
        for part in range(2):
            kv_part(x, part, other_half, 0).wait_recv()
            for n, d in enumerate((1, 3)):
                kv_part(x, part, x_mate(lax.rem(x + d, NX)), 2 + 2 * part + n).start()

    @pl.loop(1, NX)
    def _(d):
        @pl.when(d <= x)
        def _():
            kv_arrived(sq - d).wait_recv()
            score_block(sq - d, False)

    li_next(1)

    @pl.when(y_hi == 1)
    def _():
        score_block(x, False)

    li_next(2)

    @pl.when(y_hi == 1)
    def _():
        kv_arrived(far_x).wait_recv()
        score_block(far_x, False)

        @pl.loop(0, 2)
        def _(n):
            b = lax.rem(x + 1 + 2 * n, NX)
            for part in range(2):
                kv_part(b, part, other_half, 0).wait_recv()
            score_block(b, False)

    li_next(3)

    top = jnp.max(m_buf[...], axis=0)
    factor = jnp.exp2((m_buf[...] - top[None]) * EXP_SCALE)
    total = jnp.sum(factor * l_buf[...], axis=0)
    gathered = jnp.sum(factor * a_buf[...], axis=0)
    safe = jnp.where(total > 0.0, total, 1.0)
    inv = 1.0 / safe
    delta = gathered * inv
    f_buf[...] = factor * inv[None]

    def grad_block(b):
        kbt = kvbuf[b, pl.ds(0, ROWS), :].T
        dk = jnp.zeros((ROWS, HD), F32)
        dv = jnp.zeros((ROWS, HD), F32)
        for g in range(GROUP):
            w = p_buf[b, g] * f_buf[b, g : g + 1, :]
            sg = (w * (dp_buf[b, g] - delta[g : g + 1, :]) * SCALE).astype(BF)
            dv = dv + dot(w.astype(BF), do_v[g], NN)
            dk = dk + dot(sg, q_v[g], NN)
            dq_t[g] += dot(kbt, sg, NN)
        gsend[b, :, 0:HD] = dk.astype(BF)
        gsend[b, :, HD:] = dv.astype(BF)

    def g_copy(d):
        xt = lax.rem(x + d, NX)
        return remote(
            gsend.at[y_hi * NX + xt], grecv.at[d - 1], g_ss.at[d - 1], g_rs.at[d - 1], x_mate(xt)
        )

    def columns(part):
        return pl.ds(part * HD, HD)

    def c_copy(n, part):
        xt = lax.rem(x + 1 + 2 * n, NX)
        return remote(
            gsend.at[xt, :, columns(part)], crecv.at[n, part],
            c_ss.at[n, part], c_rs.at[n, part], x_mate(xt),
        )

    far_copy = remote(gsend.at[far_x], frecv, x_ss.at[2], x_rs.at[2], far_mate)

    def cross(part):
        return remote(xsend.at[part], xrecv.at[part], x_ss.at[part], x_rs.at[part], other_half)

    @pl.when(y_hi == 1)
    def _():
        grad_block(far_x)
        far_copy.start()

        @pl.loop(0, 2)
        def _(n):
            grad_block(lax.rem(x + 1 + 2 * n, NX))
            for part in range(2):
                c_copy(n, part).start()

    li_next(4)

    @pl.when(y_hi == 1)
    def _():
        grad_block(x)

    @pl.loop(1, NX)
    def _(d):
        xt = lax.rem(x + d, NX)

        @pl.when(xt < x)
        def _():
            grad_block(y_hi * NX + xt)
            g_copy(d).start()

    li_next(5)

    @pl.when(y_hi == 1)
    def _():
        for part in range(2):
            term = gsend[x, :, columns(part)].astype(F32)
            for n in range(2):
                c_copy(n, part).wait_recv()
                term = term + crecv[n, part].astype(F32)
            xsend[part] = term.astype(BF)
            cross(part).start()

    grad_block(sq)

    for g in range(GROUP):
        qg_out[:, g * HD : (g + 1) * HD] = dq_t[g].T.astype(BF)
    qg_copy = pltpu.make_async_copy(qg_out, qg_hbm, out_sem.at[0])
    qg_copy.start()

    for c in loads[10:]:
        c.wait()

    li_wait(6)
    for n in range(D // 512):
        cols = li_buf[:, :, n * 512 : (n + 1) * 512].reshape(ROWS, 512)
        li_t[n * 512 : (n + 1) * 512, :] = cols.T

    acc[...] = gsend[sq].astype(F32)

    for d in range(1, NX):

        @pl.when(lax.rem(x - d + NX, NX) > x)
        def _():
            g_copy(d).wait_recv()
            acc[...] += grecv[d - 1].astype(F32)

    @pl.when(y_hi == 0)
    def _():
        far_copy.wait_recv()
        acc[...] += frecv[...].astype(F32)
        for part in range(2):
            cross(part).wait_recv()
            acc[:, columns(part)] += xrecv[part].astype(F32)

    kv_low[...] = acc[...].astype(BF)

    def core_copy(p):
        return remote(csend.at[p], ccr.at[p], core_ss.at[p], core_rs.at[p], other_core)

    def proj_part(which, p):
        rows = pl.ds(pl.multiple_of(which * HALF + p * PART, PART), PART)
        return dot(li_t[rows, :], kv_low[...], NN)

    for p in range(PARTS):
        csend[p] = proj_part(1 - core, p).astype(BF)
        core_copy(p).start()

    for n in range(D // 512):
        part = dot(kv_low[...], wcat[n * 512 : (n + 1) * 512, :], NT)
        ipart[:, :, n * 512 : (n + 1) * 512] = part.reshape(NZ, 32, 512)

    def z_copy(direction, k, half):
        return remote(
            zs.at[direction, k, half], zr.at[direction, k, half],
            z_ss.at[direction, k, half], z_rs.at[direction, k, half],
            z_mate(1 - 2 * direction),
        )

    def z_send(direction, k, half, add):
        t = lax.rem(hd + 4 - k, NZ) if direction == 0 else lax.rem(hd + 4 + k, NZ)
        term = ipart[t, :, half * HALF : (half + 1) * HALF]
        if add:
            z_copy(direction, k - 1, half).wait_recv()
            term = term + zr[direction, k - 1, half].astype(F32)
        zs[direction, k, half] = term.astype(BF)
        z_copy(direction, k, half).start()

    def z_step(k, half, add=True):
        z_send(0, k, half, add)
        z_send(1, k, 1 - half, add)

    z_step(0, 0, False)
    z_step(1, 1, False)

    def index(axis):
        return yi if axis else x

    def mate(axis, d):
        if axis:
            return y_mate(lax.rem(yi + d, NX))
        return x_mate(lax.rem(x + d, NX))

    def st1_copy(p, d):
        a = p % 2
        return remote(
            s1.at[p, lax.rem(index(a) + d, NX)], r1.at[p, d - 1],
            st1_ss.at[p, d - 1], st1_rs.at[p, d - 1], mate(a, d),
        )

    def st2_copy(p, d, arrived=False):
        a = 1 - p % 2
        own = index(a)
        slot = lax.rem(own - d + NX, NX) if arrived else own
        return remote(
            r2.at[p, own], r2.at[p, slot], st2_ss.at[p, d - 1], st2_rs.at[p, d - 1], mate(a, d)
        )

    def ag_copy(p, d, arrived=False):
        own = index(p % 2)
        ref = gfull.at[core, p, lax.rem(own - d + NX, NX) if arrived else own]
        return remote(ref, ref, ag_ss.at[p, d - 1], ag_rs.at[p, d - 1], mate(p % 2, d))

    def pair_copy(p, d, arrived=False):
        ref = gfull.at[1 - core if arrived else core, p, lax.rem(index(p % 2) - d + NX, NX)]
        return remote(ref, ref, p_ss.at[p, d], p_rs.at[p, d], other_core)

    for p in range(PARTS):
        h32[p] = proj_part(core, p).reshape(NX, SUB, 2 * HD)

    for p in range(PARTS):
        core_copy(p).wait_recv()
        term = h32[p] + ccr[p].astype(F32).reshape(NX, SUB, 2 * HD)
        h32[p] = term
        s1[p] = term.astype(BF)
        for d in (2, 1, 3):
            st1_copy(p, d).start()

    def stage2(p):
        term = h32[p, index(p % 2)]
        for d in (1, 3, 2):
            st1_copy(p, d).wait_recv()
            term = term + r1[p, d - 1].astype(F32)
        r2[p, index(1 - p % 2)] = term.astype(BF)
        for d in (2, 1, 3):
            st2_copy(p, d).start()

    def gather(p):
        for d in (1, 3, 2):
            st2_copy(p, d, True).wait_recv()
        term = r2[p, 0].astype(F32)
        for i in range(1, NX):
            term = term + r2[p, i].astype(F32)
        gfull[core, p, index(p % 2)] = term.astype(BF)
        for d in (2, 1, 3):
            ag_copy(p, d).start()
        pair_copy(p, 0).start()

    def hand_over(p):
        for d in (1, 3, 2):
            ag_copy(p, d, True).wait_recv()
            pair_copy(p, d).start()

    z_step(1, 0)
    stage2(0)
    stage2(1)
    z_step(2, 1)
    stage2(2)
    stage2(3)
    z_step(2, 0)
    gather(0)
    gather(1)
    z_step(3, 1)
    gather(2)
    gather(3)
    z_step(3, 0)
    hand_over(0)
    hand_over(1)

    for half in range(2):
        term = ipart[hd, :, half * HALF : (half + 1) * HALF]
        for direction in range(2):
            z_copy(direction, 3, half).wait_recv()
            term = term + zr[direction, 3, half].astype(F32)
        ig_out[:, half * HALF : (half + 1) * HALF] = term.astype(BF)
    ig_copy = pltpu.make_async_copy(ig_out, ig_hbm, out_sem.at[1])
    ig_copy.start()

    def gp_copy(c, p):
        return pltpu.make_async_copy(gfull.at[c, p], gp_hbm.at[c, p], gp_sem.at[c, p])

    def part_done(p):
        for d in range(NX):
            pair_copy(p, d, True).wait_recv()
        for c in range(2):
            gp_copy(c, p).start()

    hand_over(2)
    part_done(0)
    part_done(1)
    hand_over(3)
    part_done(2)
    part_done(3)

    for d in range(1, NX):
        xt = lax.rem(x + d, NX)

        @pl.when(xt > x)
        def _():
            kv_copy(sq, x_mate(xt), d - 1).wait_send()

        @pl.when(xt < x)
        def _():
            g_copy(d).wait_send()

    @pl.when(y_hi == 0)
    def _():
        for part in range(2):
            kv_part(x, part, other_half, part).wait_send()
        kv_copy(sq, far_mate, 3).wait_send()

    @pl.when(y_hi == 1)
    def _():
        for n, d in enumerate((1, 3)):
            for part in range(2):
                kv_part(x, part, x_mate(lax.rem(x + d, NX)), 2 + 2 * part + n).wait_send()
                c_copy(n, part).wait_send()
        far_copy.wait_send()
        for part in range(2):
            cross(part).wait_send()

    for direction in range(2):
        for n in range(7):
            li_copy(direction, n).wait_send()
        for k in range(4):
            for half in range(2):
                if k > 0 or half == direction:
                    z_copy(direction, k, half).wait_send()
    for p in range(PARTS):
        core_copy(p).wait_send()
        for d in range(1, NX):
            st1_copy(p, d).wait_send()
            st2_copy(p, d).wait_send()
            ag_copy(p, d).wait_send()
        for d in range(NX):
            pair_copy(p, d).wait_send()
    qg_copy.wait()
    ig_copy.wait()
    for p in range(PARTS):
        for c in range(2):
            gp_copy(c, p).wait()


def finish(
    qg_in, ig_in, gp_in, qg_ref, ig_ref, gk_ref, gv_ref,
    low, key, value, qg_v, ig_v, sem_in, sem_key, sem_value, sem,
):
    step = D // PIECES
    loads = [
        pltpu.make_async_copy(gp_in.at[pl.ds(n * step, step), :], low.at[n], sem_in.at[n])
        for n in range(PIECES)
    ]
    loads.append(pltpu.make_async_copy(qg_in, qg_v, sem.at[0]))
    loads.append(pltpu.make_async_copy(ig_in, ig_v, sem.at[1]))
    for c in loads:
        c.start()
    copies = []
    for n in range(PIECES):
        rows = pl.ds(n * step, step)
        loads[n].wait()
        key[n] = low[n, :, 0:HD].astype(F32)
        copies.append(pltpu.make_async_copy(key.at[n], gk_ref.at[rows, :], sem_key.at[n]))
        copies[-1].start()
        value[n] = low[n, :, HD:].astype(F32)
        copies.append(pltpu.make_async_copy(value.at[n], gv_ref.at[rows, :], sem_value.at[n]))
        copies[-1].start()
    loads[PIECES].wait()
    copies.append(pltpu.make_async_copy(qg_v, qg_ref, sem.at[2]))
    copies[-1].start()
    loads[PIECES + 1].wait()
    copies.append(pltpu.make_async_copy(ig_v, ig_ref, sem.at[3]))
    copies[-1].start()
    for c in copies:
        c.wait()


def shards(queries, key_cache, value_cache, out_grad, doc_ids, layer_input, key_proj, value_proj):
    hbm = pl.BlockSpec(memory_space=pl.ANY)
    dma = pltpu.SemaphoreType.DMA
    scratch = [
        pltpu.VMEM((GROUP, ROWS, HD), BF),
        pltpu.VMEM((GROUP, ROWS, HD), BF),
        pltpu.VMEM((1, ROWS), jnp.int32),
        pltpu.VMEM((NS, 2 * ROWS + 16, HD), BF),
        pltpu.VMEM((NZ, 32, D), BF),
        pltpu.VMEM((D, ROWS), BF),
        pltpu.VMEM((D, 2 * HD), BF),
        pltpu.VMEM((NS, GROUP, ROWS, ROWS), F32),
        pltpu.VMEM((NS, GROUP, ROWS, ROWS), F32),
        pltpu.VMEM((NS, 8, ROWS), F32),
        pltpu.VMEM((NS, 8, ROWS), F32),
        pltpu.VMEM((NS, 8, ROWS), F32),
        pltpu.VMEM((NS, 8, ROWS), F32),
        pltpu.VMEM((GROUP, HD, ROWS), F32),
        pltpu.VMEM((NS, ROWS, 2 * HD), BF),
        pltpu.VMEM((NX - 1, ROWS, 2 * HD), BF),
        pltpu.VMEM((2, 2, ROWS, HD), BF),
        pltpu.VMEM((2, ROWS, HD), BF),
        pltpu.VMEM((2, ROWS, HD), BF),
        pltpu.VMEM((ROWS, 2 * HD), BF),
        pltpu.VMEM((ROWS, 2 * HD), F32),
        pltpu.VMEM((ROWS, 2 * HD), BF),
        pltpu.VMEM((NZ, 32, D), F32),
        pltpu.VMEM((2, 4, 2, 32, HALF), BF),
        pltpu.VMEM((2, 4, 2, 32, HALF), BF),
        pltpu.VMEM((32, D), BF),
        pltpu.VMEM((PARTS, PART, 2 * HD), BF),
        pltpu.VMEM((PARTS, PART, 2 * HD), BF),
        pltpu.VMEM((PARTS, NX, SUB, 2 * HD), F32),
        pltpu.VMEM((PARTS, NX, SUB, 2 * HD), BF),
        pltpu.VMEM((PARTS, NX - 1, SUB, 2 * HD), BF),
        pltpu.VMEM((PARTS, NX, SUB, 2 * HD), BF),
        pltpu.VMEM((2, PARTS, NX, SUB, 2 * HD), BF),
        pltpu.VMEM((ROWS, GROUP * HD), BF),
        dma((12,)),
        dma((NX,)),
        dma((NS,)),
        dma((6,)),
        dma((NX, 2)),
        dma((2, 7)),
        dma((2, 7)),
        dma((NX - 1,)),
        dma((NX - 1,)),
        dma((2, 2)),
        dma((2, 2)),
        dma((3,)),
        dma((3,)),
        dma((2, 4, 2)),
        dma((2, 4, 2)),
        dma((PARTS,)),
        dma((PARTS,)),
        dma((PARTS, 3)),
        dma((PARTS, 3)),
        dma((PARTS, 3)),
        dma((PARTS, 3)),
        dma((PARTS, 3)),
        dma((PARTS, 3)),
        dma((PARTS, 4)),
        dma((PARTS, 4)),
        dma((2,)),
        dma((2, PARTS)),
    ]
    qg, ig, gp = pl.pallas_call(
        kernel,
        out_shape=(
            jax.ShapeDtypeStruct((ROWS, GROUP * HD), BF),
            jax.ShapeDtypeStruct((32, D), BF),
            jax.ShapeDtypeStruct((2, PARTS, NX, SUB, 2 * HD), BF),
        ),
        in_specs=[hbm] * 8,
        out_specs=(hbm, hbm, hbm),
        scratch_shapes=scratch,
        compiler_params=pltpu.CompilerParams(
            collective_id=0, has_side_effects=True, vmem_limit_bytes=56 * 1024 * 1024
        ),
        cost_estimate=pl.CostEstimate(
            flops=3 * 10**9, bytes_accessed=8 * 10**6, transcendentals=2 * 10**6
        ),
    )(
        queries[0], key_cache[0], value_cache[0], out_grad[0], doc_ids, layer_input[0],
        key_proj, value_proj,
    )
    step = D // PIECES
    qg, ig, gk, gv = pl.pallas_call(
        finish,
        out_shape=(
            jax.ShapeDtypeStruct((ROWS, GROUP * HD), BF),
            jax.ShapeDtypeStruct((32, D), BF),
            jax.ShapeDtypeStruct((D, HD), F32),
            jax.ShapeDtypeStruct((D, HD), F32),
        ),
        in_specs=[hbm] * 3,
        out_specs=(hbm,) * 4,
        scratch_shapes=[
            pltpu.VMEM((PIECES, step, 2 * HD), BF),
            pltpu.VMEM((PIECES, step, HD), F32),
            pltpu.VMEM((PIECES, step, HD), F32),
            pltpu.VMEM((ROWS, GROUP * HD), BF),
            pltpu.VMEM((32, D), BF),
            dma((PIECES,)),
            dma((PIECES,)),
            dma((PIECES,)),
            dma((4,)),
        ],
        compiler_params=pltpu.CompilerParams(vmem_limit_bytes=60 * 1024 * 1024),
        cost_estimate=pl.CostEstimate(flops=0, bytes_accessed=6 * 10**6, transcendentals=0),
    )(qg, ig, gp.reshape(D, 2 * HD))
    return qg[None], ig[None], gk, gv


def solution(mesh):
    return jax.shard_map(
        shards,
        mesh=mesh,
        in_specs=(
            P("dp", "seq", "head"),
            P("dp", "seq", "head"),
            P("dp", "seq", "head"),
            P("dp", "seq", "head"),
            P("dp", "seq"),
            P("dp", ("seq", "head"), None),
            P(None, "head"),
            P(None, "head"),
        ),
        out_specs=(
            P("dp", "seq", "head"),
            P("dp", ("seq", "head"), None),
            P(None, "head"),
            P(None, "head"),
        ),
        check_vma=False,
    )
```

```python
import functools
import math

import jax
import jax.numpy as jnp
from jax import lax
from jax.experimental import pallas as pl
from jax.experimental.pallas import tpu as pltpu
from jax.sharding import PartitionSpec as P

D = 3072
HD = 128
GROUP = 3
ROWS = 256
NX = 4
NZ = 8
NEG_FILL = -1e30
SCALE = HD ** (-0.5)
EXP_SCALE = SCALE * math.log2(math.e)
HALF = D // 2
NS = 8
PARTS = 4
PART = HALF // PARTS
SUB = PART // NX
PIECES = 4
BF = jnp.bfloat16
F32 = jnp.float32
NT = (((1,), (1,)), ((), ()))
NN = (((1,), (0,)), ((), ()))


def dot(a, b, dims):
    return lax.dot_general(a, b, dims, preferred_element_type=F32)


def kernel(
    q_hbm, k_hbm, v_hbm, do_hbm, docs_hbm, li_hbm, wk_hbm, wv_hbm,
    qg_hbm, ig_hbm, gp_hbm,
    q_v, do_v, docs_ref, kvbuf, li_buf, li_t, wcat,
    p_buf, dp_buf, m_buf, l_buf, a_buf, f_buf, dq_t,
    gsend, grecv, crecv, xsend, xrecv, frecv, acc, kv_low,
    ipart, zs, zr, ig_out,
    csend, ccr, h32, s1, r1, r2, gfull, qg_out,
    loc, kv_ss, kv_rs, kv_ps, kv_pr, li_ss, li_rs, g_ss, g_rs, c_ss, c_rs, x_ss, x_rs,
    z_ss, z_rs, core_ss, core_rs, st1_ss, st1_rs, st2_ss, st2_rs,
    ag_ss, ag_rs, p_ss, p_rs, out_sem, gp_sem,
):
    dp = lax.axis_index("dp")
    sq = lax.axis_index("seq")
    hd = lax.axis_index("head")
    core = lax.rem(dp, 2)
    y_lo = lax.div(dp, 2)
    y_hi = lax.div(sq, NX)
    x = lax.rem(sq, NX)
    yi = y_hi * 2 + y_lo

    def x_mate(idx):
        return (dp, y_hi * NX + idx, hd)

    def y_mate(idx):
        return (lax.rem(idx, 2) * 2 + core, lax.div(idx, 2) * NX + x, hd)

    other_half = (dp, (1 - y_hi) * NX + x, hd)
    far_x = lax.rem(x + 2, NX)
    far_mate = (dp, (1 - y_hi) * NX + far_x, hd)
    other_core = (y_lo * 2 + 1 - core, sq, hd)

    def z_mate(d):
        return (dp, sq, lax.rem(hd + d + NZ, NZ))

    def remote(src, dst, ssem, rsem, dev):
        return pltpu.make_async_remote_copy(
            src_ref=src, dst_ref=dst, send_sem=ssem, recv_sem=rsem,
            device_id=dev, device_id_type=pl.DeviceIdType.MESH,
        )

    barrier = pltpu.get_barrier_semaphore()
    partners = [x_mate(lax.rem(x + d, NX)) for d in range(1, NX)]
    partners += [y_mate(lax.rem(yi + d, NX)) for d in range(1, NX)]
    partners += [far_mate, other_core, z_mate(1), z_mate(-1)]
    for dev in partners:
        pl.semaphore_signal(barrier, inc=1, device_id=dev, device_id_type=pl.DeviceIdType.MESH)

    loads = [
        pltpu.make_async_copy(docs_hbm, docs_ref, loc.at[0]),
        pltpu.make_async_copy(k_hbm, kvbuf.at[sq, pl.ds(0, ROWS), :], loc.at[1]),
        pltpu.make_async_copy(v_hbm, kvbuf.at[sq, pl.ds(ROWS, ROWS), :], loc.at[2]),
        pltpu.make_async_copy(li_hbm, li_buf.at[hd], loc.at[3]),
    ]
    for g in range(GROUP):
        loads.append(pltpu.make_async_copy(q_hbm.at[:, pl.ds(g * HD, HD)], q_v.at[g], loc.at[4 + g]))
        loads.append(pltpu.make_async_copy(do_hbm.at[:, pl.ds(g * HD, HD)], do_v.at[g], loc.at[7 + g]))
    loads.append(pltpu.make_async_copy(wk_hbm, wcat.at[:, pl.ds(0, HD)], loc.at[10]))
    loads.append(pltpu.make_async_copy(wv_hbm, wcat.at[:, pl.ds(HD, HD)], loc.at[11]))
    for c in loads:
        c.start()

    m_buf[...] = jnp.full(m_buf.shape, NEG_FILL, F32)
    l_buf[...] = jnp.zeros(l_buf.shape, F32)
    a_buf[...] = jnp.zeros(a_buf.shape, F32)
    dq_t[...] = jnp.zeros(dq_t.shape, F32)

    loads[0].wait()
    doc_row = docs_ref[...].astype(F32)
    upper = lax.broadcasted_iota(jnp.int32, (16, HD), 0) < 8
    doc_tile = jnp.where(
        upper,
        jnp.broadcast_to(doc_row[:, 0:HD], (16, HD)),
        jnp.broadcast_to(doc_row[:, HD:], (16, HD)),
    )
    kvbuf[sq, pl.ds(2 * ROWS, 16), :] = doc_tile.astype(BF)
    for c in loads[1:4]:
        c.wait()
    for c in loads[4:10]:
        c.wait()

    key_iota = lax.broadcasted_iota(jnp.int32, (ROWS, ROWS), 0).astype(F32)

    def score_block(b, diagonal):
        kb = kvbuf[b, pl.ds(0, ROWS), :]
        vb = kvbuf[b, pl.ds(ROWS, ROWS), :]
        docs = kvbuf[b, pl.ds(2 * ROWS, 16), :].astype(F32)
        ones = jnp.sum(jnp.sum(docs, axis=0, keepdims=True), axis=1, keepdims=True) * 0.125
        zeros = ROWS - ones
        low = doc_row * zeros
        high = zeros + doc_row * ones
        if diagonal:
            own = lax.broadcasted_iota(jnp.int32, (1, ROWS), 1).astype(F32)
            high = jnp.minimum(high, own + 1.0)
        allowed = (key_iota >= low) & (key_iota < high)
        for g in range(GROUP):
            s = jnp.where(allowed, dot(kb, q_v[g], NT), NEG_FILL)
            top = jnp.max(s, axis=0, keepdims=True)
            p = jnp.exp2((s - top) * EXP_SCALE)
            wg = dot(vb, do_v[g], NT)
            p_buf[b, g] = p
            dp_buf[b, g] = wg
            m_buf[b, g : g + 1, :] = top
            l_buf[b, g : g + 1, :] = jnp.sum(p, axis=0, keepdims=True)
            a_buf[b, g : g + 1, :] = jnp.sum(p * wg, axis=0, keepdims=True)

    score_block(sq, True)
    pl.semaphore_wait(barrier, len(partners))

    def kv_copy(block, dev, s):
        return remote(kvbuf.at[block], kvbuf.at[block], kv_ss.at[s], kv_rs.at[block], dev)

    def kv_arrived(block):
        return kv_copy(block, other_half, 0)

    def kv_part(block, part, dev, s):
        ref = kvbuf.at[block, pl.ds(part * ROWS, ROWS + 16 * part), :]
        return remote(ref, ref, kv_ps.at[s], kv_pr.at[block, part], dev)

    @pl.when(y_hi == 0)
    def _():
        for part in range(2):
            kv_part(x, part, other_half, part).start()
        kv_copy(sq, far_mate, 3).start()

    for d in (2, 1, 3):
        xt = lax.rem(x + d, NX)

        @pl.when(xt > x)
        def _():
            kv_copy(sq, x_mate(xt), d - 1).start()

    def li_copy(direction, n, arrived=False):
        sign = 1 - 2 * direction
        away = n // 2 + 1 if arrived else n // 2
        half = direction if n == 6 else n % 2
        ref = li_buf.at[lax.rem(hd - sign * away + NZ, NZ), pl.ds(16 * half, 16), :]
        return remote(ref, ref, li_ss.at[direction, n], li_rs.at[direction, n], z_mate(sign))

    def li_start(n):
        for direction in range(2):
            li_copy(direction, n).start()

    def li_wait(n):
        for direction in range(2):
            li_copy(direction, n, True).wait_recv()

    def li_next(n):
        li_wait(n)
        if n == 4:
            li_copy(0, 6).start()
        elif n == 5:
            li_copy(1, 6).start()
        else:
            li_start(n + 2)

    li_start(0)
    li_start(1)
    li_next(0)

    @pl.when(y_hi == 1)
    def _():
        for part in range(2):
            kv_part(x, part, other_half, 0).wait_recv()
            for n, d in enumerate((1, 3)):
                kv_part(x, part, x_mate(lax.rem(x + d, NX)), 2 + 2 * part + n).start()

    @pl.loop(1, NX)
    def _(d):
        @pl.when(d <= x)
        def _():
            kv_arrived(sq - d).wait_recv()
            score_block(sq - d, False)

    li_next(1)

    @pl.when(y_hi == 1)
    def _():
        score_block(x, False)

    li_next(2)

    @pl.when(y_hi == 1)
    def _():
        kv_arrived(far_x).wait_recv()
        score_block(far_x, False)

        @pl.loop(0, 2)
        def _(n):
            b = lax.rem(x + 1 + 2 * n, NX)
            for part in range(2):
                kv_part(b, part, other_half, 0).wait_recv()
            score_block(b, False)

    li_next(3)

    top = jnp.max(m_buf[...], axis=0)
    factor = jnp.exp2((m_buf[...] - top[None]) * EXP_SCALE)
    total = jnp.sum(factor * l_buf[...], axis=0)
    gathered = jnp.sum(factor * a_buf[...], axis=0)
    safe = jnp.where(total > 0.0, total, 1.0)
    inv = 1.0 / safe
    delta = gathered * inv
    f_buf[...] = factor * inv[None]

    def grad_block(b):
        kbt = kvbuf[b, pl.ds(0, ROWS), :].T
        dk = jnp.zeros((ROWS, HD), F32)
        dv = jnp.zeros((ROWS, HD), F32)
        for g in range(GROUP):
            w = p_buf[b, g] * f_buf[b, g : g + 1, :]
            sg = (w * (dp_buf[b, g] - delta[g : g + 1, :]) * SCALE).astype(BF)
            dv = dv + dot(w.astype(BF), do_v[g], NN)
            dk = dk + dot(sg, q_v[g], NN)
            dq_t[g] += dot(kbt, sg, NN)
        gsend[b, :, 0:HD] = dk.astype(BF)
        gsend[b, :, HD:] = dv.astype(BF)

    def g_copy(d):
        xt = lax.rem(x + d, NX)
        return remote(
            gsend.at[y_hi * NX + xt], grecv.at[d - 1], g_ss.at[d - 1], g_rs.at[d - 1], x_mate(xt)
        )

    def columns(part):
        return pl.ds(part * HD, HD)

    def c_copy(n, part):
        xt = lax.rem(x + 1 + 2 * n, NX)
        return remote(
            gsend.at[xt, :, columns(part)], crecv.at[n, part],
            c_ss.at[n, part], c_rs.at[n, part], x_mate(xt),
        )

    far_copy = remote(gsend.at[far_x], frecv, x_ss.at[2], x_rs.at[2], far_mate)

    def cross(part):
        return remote(xsend.at[part], xrecv.at[part], x_ss.at[part], x_rs.at[part], other_half)

    @pl.when(y_hi == 1)
    def _():
        @pl.loop(0, 2)
        def _(n):
            grad_block(lax.rem(x + 1 + 2 * n, NX))
            for part in range(2):
                c_copy(n, part).start()

        grad_block(far_x)
        far_copy.start()

    li_next(4)

    @pl.when(y_hi == 1)
    def _():
        grad_block(x)

    @pl.loop(1, NX)
    def _(d):
        xt = lax.rem(x + d, NX)

        @pl.when(xt < x)
        def _():
            grad_block(y_hi * NX + xt)
            g_copy(d).start()

    li_next(5)

    @pl.when(y_hi == 1)
    def _():
        for part in range(2):
            term = gsend[x, :, columns(part)].astype(F32)
            for n in range(2):
                c_copy(n, part).wait_recv()
                term = term + crecv[n, part].astype(F32)
            xsend[part] = term.astype(BF)
            cross(part).start()

    grad_block(sq)

    for g in range(GROUP):
        qg_out[:, g * HD : (g + 1) * HD] = dq_t[g].T.astype(BF)
    qg_copy = pltpu.make_async_copy(qg_out, qg_hbm, out_sem.at[0])
    qg_copy.start()

    for c in loads[10:]:
        c.wait()

    li_wait(6)
    for n in range(D // 512):
        cols = li_buf[:, :, n * 512 : (n + 1) * 512].reshape(ROWS, 512)
        li_t[n * 512 : (n + 1) * 512, :] = cols.T

    acc[...] = gsend[sq].astype(F32)

    for d in range(1, NX):

        @pl.when(lax.rem(x - d + NX, NX) > x)
        def _():
            g_copy(d).wait_recv()
            acc[...] += grecv[d - 1].astype(F32)

    @pl.when(y_hi == 0)
    def _():
        far_copy.wait_recv()
        acc[...] += frecv[...].astype(F32)
        for part in range(2):
            cross(part).wait_recv()
            acc[:, columns(part)] += xrecv[part].astype(F32)

    kv_low[...] = acc[...].astype(BF)

    def core_copy(p):
        return remote(csend.at[p], ccr.at[p], core_ss.at[p], core_rs.at[p], other_core)

    def proj_part(which, p):
        rows = pl.ds(pl.multiple_of(which * HALF + p * PART, PART), PART)
        return dot(li_t[rows, :], kv_low[...], NN)

    for p in range(PARTS):
        csend[p] = proj_part(1 - core, p).astype(BF)
        core_copy(p).start()

    for n in range(D // 512):
        part = dot(kv_low[...], wcat[n * 512 : (n + 1) * 512, :], NT)
        ipart[:, :, n * 512 : (n + 1) * 512] = part.reshape(NZ, 32, 512)

    def z_copy(direction, k, half):
        return remote(
            zs.at[direction, k, half], zr.at[direction, k, half],
            z_ss.at[direction, k, half], z_rs.at[direction, k, half],
            z_mate(1 - 2 * direction),
        )

    def z_send(direction, k, half, add):
        t = lax.rem(hd + 4 - k, NZ) if direction == 0 else lax.rem(hd + 4 + k, NZ)
        term = ipart[t, :, half * HALF : (half + 1) * HALF]
        if add:
            z_copy(direction, k - 1, half).wait_recv()
            term = term + zr[direction, k - 1, half].astype(F32)
        zs[direction, k, half] = term.astype(BF)
        z_copy(direction, k, half).start()

    def z_step(k, half, add=True):
        z_send(0, k, half, add)
        z_send(1, k, 1 - half, add)

    z_step(0, 0, False)
    z_step(1, 1, False)

    def index(axis):
        return yi if axis else x

    def mate(axis, d):
        if axis:
            return y_mate(lax.rem(yi + d, NX))
        return x_mate(lax.rem(x + d, NX))

    def st1_copy(p, d):
        a = p % 2
        return remote(
            s1.at[p, lax.rem(index(a) + d, NX)], r1.at[p, d - 1],
            st1_ss.at[p, d - 1], st1_rs.at[p, d - 1], mate(a, d),
        )

    def st2_copy(p, d, arrived=False):
        a = 1 - p % 2
        own = index(a)
        slot = lax.rem(own - d + NX, NX) if arrived else own
        return remote(
            r2.at[p, own], r2.at[p, slot], st2_ss.at[p, d - 1], st2_rs.at[p, d - 1], mate(a, d)
        )

    def ag_copy(p, d, arrived=False):
        own = index(p % 2)
        ref = gfull.at[core, p, lax.rem(own - d + NX, NX) if arrived else own]
        return remote(ref, ref, ag_ss.at[p, d - 1], ag_rs.at[p, d - 1], mate(p % 2, d))

    def pair_copy(p, d, arrived=False):
        ref = gfull.at[1 - core if arrived else core, p, lax.rem(index(p % 2) - d + NX, NX)]
        return remote(ref, ref, p_ss.at[p, d], p_rs.at[p, d], other_core)

    for p in range(PARTS):
        h32[p] = proj_part(core, p).reshape(NX, SUB, 2 * HD)

    for p in range(PARTS):
        core_copy(p).wait_recv()
        term = h32[p] + ccr[p].astype(F32).reshape(NX, SUB, 2 * HD)
        h32[p] = term
        s1[p] = term.astype(BF)
        for d in (2, 1, 3):
            st1_copy(p, d).start()

    def stage2(p):
        term = h32[p, index(p % 2)]
        for d in (1, 3, 2):
            st1_copy(p, d).wait_recv()
            term = term + r1[p, d - 1].astype(F32)
        r2[p, index(1 - p % 2)] = term.astype(BF)
        for d in (2, 1, 3):
            st2_copy(p, d).start()

    def gather(p):
        for d in (1, 3, 2):
            st2_copy(p, d, True).wait_recv()
        term = r2[p, 0].astype(F32)
        for i in range(1, NX):
            term = term + r2[p, i].astype(F32)
        gfull[core, p, index(p % 2)] = term.astype(BF)
        for d in (2, 1, 3):
            ag_copy(p, d).start()
        pair_copy(p, 0).start()

    def hand_over(p):
        for d in (1, 3, 2):
            ag_copy(p, d, True).wait_recv()
            pair_copy(p, d).start()

    z_step(1, 0)
    stage2(0)
    stage2(1)
    z_step(2, 1)
    stage2(2)
    stage2(3)
    z_step(2, 0)
    gather(0)
    gather(1)
    z_step(3, 1)
    gather(2)
    gather(3)
    z_step(3, 0)
    hand_over(0)
    hand_over(1)

    for half in range(2):
        term = ipart[hd, :, half * HALF : (half + 1) * HALF]
        for direction in range(2):
            z_copy(direction, 3, half).wait_recv()
            term = term + zr[direction, 3, half].astype(F32)
        ig_out[:, half * HALF : (half + 1) * HALF] = term.astype(BF)
    ig_copy = pltpu.make_async_copy(ig_out, ig_hbm, out_sem.at[1])
    ig_copy.start()

    def gp_copy(c, p):
        return pltpu.make_async_copy(gfull.at[c, p], gp_hbm.at[c, p], gp_sem.at[c, p])

    def part_done(p):
        for d in range(NX):
            pair_copy(p, d, True).wait_recv()
        for c in range(2):
            gp_copy(c, p).start()

    hand_over(2)
    part_done(0)
    part_done(1)
    hand_over(3)
    part_done(2)
    part_done(3)

    for d in range(1, NX):
        xt = lax.rem(x + d, NX)

        @pl.when(xt > x)
        def _():
            kv_copy(sq, x_mate(xt), d - 1).wait_send()

        @pl.when(xt < x)
        def _():
            g_copy(d).wait_send()

    @pl.when(y_hi == 0)
    def _():
        for part in range(2):
            kv_part(x, part, other_half, part).wait_send()
        kv_copy(sq, far_mate, 3).wait_send()

    @pl.when(y_hi == 1)
    def _():
        for n, d in enumerate((1, 3)):
            for part in range(2):
                kv_part(x, part, x_mate(lax.rem(x + d, NX)), 2 + 2 * part + n).wait_send()
                c_copy(n, part).wait_send()
        far_copy.wait_send()
        for part in range(2):
            cross(part).wait_send()

    for direction in range(2):
        for n in range(7):
            li_copy(direction, n).wait_send()
        for k in range(4):
            for half in range(2):
                if k > 0 or half == direction:
                    z_copy(direction, k, half).wait_send()
    for p in range(PARTS):
        core_copy(p).wait_send()
        for d in range(1, NX):
            st1_copy(p, d).wait_send()
            st2_copy(p, d).wait_send()
            ag_copy(p, d).wait_send()
        for d in range(NX):
            pair_copy(p, d).wait_send()
    qg_copy.wait()
    ig_copy.wait()
    for p in range(PARTS):
        for c in range(2):
            gp_copy(c, p).wait()


def finish(
    qg_in, ig_in, gp_in, qg_ref, ig_ref, gk_ref, gv_ref,
    key, value, sem_key, sem_value, sem,
):
    step = D // PIECES
    copies = [
        pltpu.make_async_copy(qg_in, qg_ref, sem.at[0]),
        pltpu.make_async_copy(ig_in, ig_ref, sem.at[1]),
    ]
    for c in copies:
        c.start()
    for n in range(PIECES):
        rows = pl.ds(n * step, step)
        key[n] = gp_in[rows, 0:HD].astype(F32)
        copies.append(pltpu.make_async_copy(key.at[n], gk_ref.at[rows, :], sem_key.at[n]))
        copies[-1].start()
        value[n] = gp_in[rows, HD:].astype(F32)
        copies.append(pltpu.make_async_copy(value.at[n], gv_ref.at[rows, :], sem_value.at[n]))
        copies[-1].start()
    for c in copies:
        c.wait()


def shards(queries, key_cache, value_cache, out_grad, doc_ids, layer_input, key_proj, value_proj):
    hbm = pl.BlockSpec(memory_space=pl.ANY)
    vmem = pl.BlockSpec(memory_space=pltpu.VMEM)
    dma = pltpu.SemaphoreType.DMA
    scratch = [
        pltpu.VMEM((GROUP, ROWS, HD), BF),
        pltpu.VMEM((GROUP, ROWS, HD), BF),
        pltpu.VMEM((1, ROWS), jnp.int32),
        pltpu.VMEM((NS, 2 * ROWS + 16, HD), BF),
        pltpu.VMEM((NZ, 32, D), BF),
        pltpu.VMEM((D, ROWS), BF),
        pltpu.VMEM((D, 2 * HD), BF),
        pltpu.VMEM((NS, GROUP, ROWS, ROWS), F32),
        pltpu.VMEM((NS, GROUP, ROWS, ROWS), F32),
        pltpu.VMEM((NS, 8, ROWS), F32),
        pltpu.VMEM((NS, 8, ROWS), F32),
        pltpu.VMEM((NS, 8, ROWS), F32),
        pltpu.VMEM((NS, 8, ROWS), F32),
        pltpu.VMEM((GROUP, HD, ROWS), F32),
        pltpu.VMEM((NS, ROWS, 2 * HD), BF),
        pltpu.VMEM((NX - 1, ROWS, 2 * HD), BF),
        pltpu.VMEM((2, 2, ROWS, HD), BF),
        pltpu.VMEM((2, ROWS, HD), BF),
        pltpu.VMEM((2, ROWS, HD), BF),
        pltpu.VMEM((ROWS, 2 * HD), BF),
        pltpu.VMEM((ROWS, 2 * HD), F32),
        pltpu.VMEM((ROWS, 2 * HD), BF),
        pltpu.VMEM((NZ, 32, D), F32),
        pltpu.VMEM((2, 4, 2, 32, HALF), BF),
        pltpu.VMEM((2, 4, 2, 32, HALF), BF),
        pltpu.VMEM((32, D), BF),
        pltpu.VMEM((PARTS, PART, 2 * HD), BF),
        pltpu.VMEM((PARTS, PART, 2 * HD), BF),
        pltpu.VMEM((PARTS, NX, SUB, 2 * HD), F32),
        pltpu.VMEM((PARTS, NX, SUB, 2 * HD), BF),
        pltpu.VMEM((PARTS, NX - 1, SUB, 2 * HD), BF),
        pltpu.VMEM((PARTS, NX, SUB, 2 * HD), BF),
        pltpu.VMEM((2, PARTS, NX, SUB, 2 * HD), BF),
        pltpu.VMEM((ROWS, GROUP * HD), BF),
        dma((12,)),
        dma((NX,)),
        dma((NS,)),
        dma((6,)),
        dma((NX, 2)),
        dma((2, 7)),
        dma((2, 7)),
        dma((NX - 1,)),
        dma((NX - 1,)),
        dma((2, 2)),
        dma((2, 2)),
        dma((3,)),
        dma((3,)),
        dma((2, 4, 2)),
        dma((2, 4, 2)),
        dma((PARTS,)),
        dma((PARTS,)),
        dma((PARTS, 3)),
        dma((PARTS, 3)),
        dma((PARTS, 3)),
        dma((PARTS, 3)),
        dma((PARTS, 3)),
        dma((PARTS, 3)),
        dma((PARTS, 4)),
        dma((PARTS, 4)),
        dma((2,)),
        dma((2, PARTS)),
    ]
    qg, ig, gp = pl.pallas_call(
        kernel,
        out_shape=(
            pltpu.VMEM((ROWS, GROUP * HD), BF),
            pltpu.VMEM((32, D), BF),
            pltpu.VMEM((2, PARTS, NX, SUB, 2 * HD), BF),
        ),
        in_specs=[hbm] * 8,
        out_specs=(vmem,) * 3,
        scratch_shapes=scratch,
        compiler_params=pltpu.CompilerParams(
            collective_id=0, has_side_effects=True, vmem_limit_bytes=56 * 1024 * 1024
        ),
        cost_estimate=pl.CostEstimate(
            flops=3 * 10**9, bytes_accessed=8 * 10**6, transcendentals=2 * 10**6
        ),
    )(
        queries[0], key_cache[0], value_cache[0], out_grad[0], doc_ids, layer_input[0],
        key_proj, value_proj,
    )
    step = D // PIECES
    qg, ig, gk, gv = pl.pallas_call(
        finish,
        out_shape=(
            jax.ShapeDtypeStruct((ROWS, GROUP * HD), BF),
            jax.ShapeDtypeStruct((32, D), BF),
            jax.ShapeDtypeStruct((D, HD), F32),
            jax.ShapeDtypeStruct((D, HD), F32),
        ),
        in_specs=[vmem] * 3,
        out_specs=(hbm,) * 4,
        scratch_shapes=[
            pltpu.VMEM((PIECES, step, HD), F32),
            pltpu.VMEM((PIECES, step, HD), F32),
            dma((PIECES,)),
            dma((PIECES,)),
            dma((2,)),
        ],
        compiler_params=pltpu.CompilerParams(vmem_limit_bytes=24 * 1024 * 1024),
        cost_estimate=pl.CostEstimate(flops=0, bytes_accessed=6 * 10**6, transcendentals=0),
    )(qg, ig, gp.reshape(D, 2 * HD))
    return qg[None], ig[None], gk, gv


def solution(mesh):
    return jax.shard_map(
        shards,
        mesh=mesh,
        in_specs=(
            P("dp", "seq", "head"),
            P("dp", "seq", "head"),
            P("dp", "seq", "head"),
            P("dp", "seq", "head"),
            P("dp", "seq"),
            P("dp", ("seq", "head"), None),
            P(None, "head"),
            P(None, "head"),
        ),
        out_specs=(
            P("dp", "seq", "head"),
            P("dp", ("seq", "head"), None),
            P(None, "head"),
            P(None, "head"),
        ),
        check_vma=False,
    )
```

```python
import functools
import math

import jax
import jax.numpy as jnp
from jax import lax
from jax.experimental import pallas as pl
from jax.experimental.pallas import tpu as pltpu
from jax.sharding import PartitionSpec as P

D = 3072
HD = 128
GROUP = 3
ROWS = 256
NX = 4
NZ = 8
NEG_FILL = -1e30
SCALE = HD ** (-0.5)
EXP_SCALE = SCALE * math.log2(math.e)
HALF = D // 2
NS = 8
PARTS = 4
PART = HALF // PARTS
SUB = PART // NX
PIECES = 4
BF = jnp.bfloat16
F32 = jnp.float32
NT = (((1,), (1,)), ((), ()))
NN = (((1,), (0,)), ((), ()))


def dot(a, b, dims):
    return lax.dot_general(a, b, dims, preferred_element_type=F32)


def kernel(
    q_hbm, k_hbm, v_hbm, do_hbm, docs_hbm, li_hbm, wk_hbm, wv_hbm,
    qg_out, ig_out, gfull,
    q_v, do_v, docs_ref, kvbuf, li_buf, li_t, wcat,
    p_buf, dp_buf, m_buf, l_buf, a_buf, f_buf, dq_t,
    gsend, grecv, crecv, xsend, xrecv, frecv, acc, kv_low,
    ipart, zs, zr,
    csend, ccr, h32, s1, r1, r2,
    loc, kv_ss, kv_rs, kv_ps, kv_pr, li_ss, li_rs, g_ss, g_rs, c_ss, c_rs, x_ss, x_rs,
    z_ss, z_rs, core_ss, core_rs, st1_ss, st1_rs, st2_ss, st2_rs,
    ag_ss, ag_rs, p_ss, p_rs,
):
    dp = lax.axis_index("dp")
    sq = lax.axis_index("seq")
    hd = lax.axis_index("head")
    core = lax.rem(dp, 2)
    y_lo = lax.div(dp, 2)
    y_hi = lax.div(sq, NX)
    x = lax.rem(sq, NX)
    yi = y_hi * 2 + y_lo

    def x_mate(idx):
        return (dp, y_hi * NX + idx, hd)

    def y_mate(idx):
        return (lax.rem(idx, 2) * 2 + core, lax.div(idx, 2) * NX + x, hd)

    other_half = (dp, (1 - y_hi) * NX + x, hd)
    far_x = lax.rem(x + 2, NX)
    far_mate = (dp, (1 - y_hi) * NX + far_x, hd)
    other_core = (y_lo * 2 + 1 - core, sq, hd)

    def z_mate(d):
        return (dp, sq, lax.rem(hd + d + NZ, NZ))

    def remote(src, dst, ssem, rsem, dev):
        return pltpu.make_async_remote_copy(
            src_ref=src, dst_ref=dst, send_sem=ssem, recv_sem=rsem,
            device_id=dev, device_id_type=pl.DeviceIdType.MESH,
        )

    barrier = pltpu.get_barrier_semaphore()
    partners = [x_mate(lax.rem(x + d, NX)) for d in range(1, NX)]
    partners += [y_mate(lax.rem(yi + d, NX)) for d in range(1, NX)]
    partners += [far_mate, other_core, z_mate(1), z_mate(-1)]
    for dev in partners:
        pl.semaphore_signal(barrier, inc=1, device_id=dev, device_id_type=pl.DeviceIdType.MESH)

    loads = [
        pltpu.make_async_copy(docs_hbm, docs_ref, loc.at[0]),
        pltpu.make_async_copy(k_hbm, kvbuf.at[sq, pl.ds(0, ROWS), :], loc.at[1]),
        pltpu.make_async_copy(v_hbm, kvbuf.at[sq, pl.ds(ROWS, ROWS), :], loc.at[2]),
        pltpu.make_async_copy(li_hbm, li_buf.at[hd], loc.at[3]),
    ]
    for g in range(GROUP):
        loads.append(pltpu.make_async_copy(q_hbm.at[:, pl.ds(g * HD, HD)], q_v.at[g], loc.at[4 + g]))
        loads.append(pltpu.make_async_copy(do_hbm.at[:, pl.ds(g * HD, HD)], do_v.at[g], loc.at[7 + g]))
    loads.append(pltpu.make_async_copy(wk_hbm, wcat.at[:, pl.ds(0, HD)], loc.at[10]))
    loads.append(pltpu.make_async_copy(wv_hbm, wcat.at[:, pl.ds(HD, HD)], loc.at[11]))
    for c in loads:
        c.start()

    m_buf[...] = jnp.full(m_buf.shape, NEG_FILL, F32)
    l_buf[...] = jnp.zeros(l_buf.shape, F32)
    a_buf[...] = jnp.zeros(a_buf.shape, F32)
    dq_t[...] = jnp.zeros(dq_t.shape, F32)

    loads[0].wait()
    doc_row = docs_ref[...].astype(F32)
    upper = lax.broadcasted_iota(jnp.int32, (16, HD), 0) < 8
    doc_tile = jnp.where(
        upper,
        jnp.broadcast_to(doc_row[:, 0:HD], (16, HD)),
        jnp.broadcast_to(doc_row[:, HD:], (16, HD)),
    )
    kvbuf[sq, pl.ds(2 * ROWS, 16), :] = doc_tile.astype(BF)
    for c in loads[1:3]:
        c.wait()
    pl.semaphore_wait(barrier, len(partners))

    def kv_copy(block, dev, s):
        return remote(kvbuf.at[block], kvbuf.at[block], kv_ss.at[s], kv_rs.at[block], dev)

    def kv_arrived(block):
        return kv_copy(block, other_half, 0)

    def kv_part(block, part, dev, s):
        ref = kvbuf.at[block, pl.ds(part * ROWS, ROWS + 16 * part), :]
        return remote(ref, ref, kv_ps.at[s], kv_pr.at[block, part], dev)

    @pl.when(y_hi == 0)
    def _():
        for part in range(2):
            kv_part(x, part, other_half, part).start()
        kv_copy(sq, far_mate, 3).start()

    for d in (2, 1, 3):
        xt = lax.rem(x + d, NX)

        @pl.when(xt > x)
        def _():
            kv_copy(sq, x_mate(xt), d - 1).start()

    def li_copy(direction, n, arrived=False):
        sign = 1 - 2 * direction
        away = n // 2 + 1 if arrived else n // 2
        half = direction if n == 6 else n % 2
        ref = li_buf.at[lax.rem(hd - sign * away + NZ, NZ), pl.ds(16 * half, 16), :]
        return remote(ref, ref, li_ss.at[direction, n], li_rs.at[direction, n], z_mate(sign))

    def li_start(n):
        for direction in range(2):
            li_copy(direction, n).start()

    def li_wait(n):
        for direction in range(2):
            li_copy(direction, n, True).wait_recv()

    def li_next(n):
        li_wait(n)
        if n == 4:
            li_copy(0, 6).start()
        elif n == 5:
            li_copy(1, 6).start()
        else:
            li_start(n + 2)

    loads[3].wait()
    li_start(0)
    li_start(1)

    for c in loads[4:10]:
        c.wait()

    key_iota = lax.broadcasted_iota(jnp.int32, (ROWS, ROWS), 0).astype(F32)

    def score_block(b, diagonal):
        kb = kvbuf[b, pl.ds(0, ROWS), :]
        vb = kvbuf[b, pl.ds(ROWS, ROWS), :]
        docs = kvbuf[b, pl.ds(2 * ROWS, 16), :].astype(F32)
        ones = jnp.sum(jnp.sum(docs, axis=0, keepdims=True), axis=1, keepdims=True) * 0.125
        zeros = ROWS - ones
        low = doc_row * zeros
        high = zeros + doc_row * ones
        if diagonal:
            own = lax.broadcasted_iota(jnp.int32, (1, ROWS), 1).astype(F32)
            high = jnp.minimum(high, own + 1.0)
        allowed = (key_iota >= low) & (key_iota < high)
        for g in range(GROUP):
            s = jnp.where(allowed, dot(kb, q_v[g], NT), NEG_FILL)
            top = jnp.max(s, axis=0, keepdims=True)
            p = jnp.exp2((s - top) * EXP_SCALE)
            wg = dot(vb, do_v[g], NT)
            p_buf[b, g] = p
            dp_buf[b, g] = wg
            m_buf[b, g : g + 1, :] = top
            l_buf[b, g : g + 1, :] = jnp.sum(p, axis=0, keepdims=True)
            a_buf[b, g : g + 1, :] = jnp.sum(p * wg, axis=0, keepdims=True)

    score_block(sq, True)

    li_next(0)

    @pl.when(y_hi == 1)
    def _():
        for part in range(2):
            kv_part(x, part, other_half, 0).wait_recv()
            for n, d in enumerate((1, 3)):
                kv_part(x, part, x_mate(lax.rem(x + d, NX)), 2 + 2 * part + n).start()

    @pl.loop(1, NX)
    def _(d):
        @pl.when(d <= x)
        def _():
            kv_arrived(sq - d).wait_recv()
            score_block(sq - d, False)

    li_next(1)

    @pl.when(y_hi == 1)
    def _():
        score_block(x, False)

    li_next(2)

    @pl.when(y_hi == 1)
    def _():
        kv_arrived(far_x).wait_recv()
        score_block(far_x, False)

        @pl.loop(0, 2)
        def _(n):
            b = lax.rem(x + 1 + 2 * n, NX)
            for part in range(2):
                kv_part(b, part, other_half, 0).wait_recv()
            score_block(b, False)

    li_next(3)

    top = jnp.max(m_buf[...], axis=0)
    factor = jnp.exp2((m_buf[...] - top[None]) * EXP_SCALE)
    total = jnp.sum(factor * l_buf[...], axis=0)
    gathered = jnp.sum(factor * a_buf[...], axis=0)
    safe = jnp.where(total > 0.0, total, 1.0)
    inv = 1.0 / safe
    delta = gathered * inv
    f_buf[...] = factor * inv[None]

    def grad_block(b):
        kbt = kvbuf[b, pl.ds(0, ROWS), :].T
        dk = jnp.zeros((ROWS, HD), F32)
        dv = jnp.zeros((ROWS, HD), F32)
        for g in range(GROUP):
            w = p_buf[b, g] * f_buf[b, g : g + 1, :]
            sg = (w * (dp_buf[b, g] - delta[g : g + 1, :]) * SCALE).astype(BF)
            dv = dv + dot(w.astype(BF), do_v[g], NN)
            dk = dk + dot(sg, q_v[g], NN)
            dq_t[g] += dot(kbt, sg, NN)
        gsend[b, :, 0:HD] = dk.astype(BF)
        gsend[b, :, HD:] = dv.astype(BF)

    def g_copy(d):
        xt = lax.rem(x + d, NX)
        return remote(
            gsend.at[y_hi * NX + xt], grecv.at[d - 1], g_ss.at[d - 1], g_rs.at[d - 1], x_mate(xt)
        )

    def columns(part):
        return pl.ds(part * HD, HD)

    def c_copy(n, part):
        xt = lax.rem(x + 1 + 2 * n, NX)
        return remote(
            gsend.at[xt, :, columns(part)], crecv.at[n, part],
            c_ss.at[n, part], c_rs.at[n, part], x_mate(xt),
        )

    far_copy = remote(gsend.at[far_x], frecv, x_ss.at[2], x_rs.at[2], far_mate)

    def cross(part):
        return remote(xsend.at[part], xrecv.at[part], x_ss.at[part], x_rs.at[part], other_half)

    @pl.when(y_hi == 1)
    def _():
        grad_block(far_x)
        far_copy.start()

        @pl.loop(0, 2)
        def _(n):
            grad_block(lax.rem(x + 1 + 2 * n, NX))
            for part in range(2):
                c_copy(n, part).start()

    li_next(4)

    @pl.when(y_hi == 1)
    def _():
        grad_block(x)

    @pl.loop(1, NX)
    def _(d):
        xt = lax.rem(x + d, NX)

        @pl.when(xt < x)
        def _():
            grad_block(y_hi * NX + xt)
            g_copy(d).start()

    li_next(5)

    @pl.when(y_hi == 1)
    def _():
        for part in range(2):
            term = gsend[x, :, columns(part)].astype(F32)
            for n in range(2):
                c_copy(n, part).wait_recv()
                term = term + crecv[n, part].astype(F32)
            xsend[part] = term.astype(BF)
            cross(part).start()

    grad_block(sq)

    for g in range(GROUP):
        qg_out[:, g * HD : (g + 1) * HD] = dq_t[g].T.astype(BF)

    for c in loads[10:]:
        c.wait()

    li_wait(6)
    for n in range(D // 512):
        cols = li_buf[:, :, n * 512 : (n + 1) * 512].reshape(ROWS, 512)
        li_t[n * 512 : (n + 1) * 512, :] = cols.T

    acc[...] = gsend[sq].astype(F32)

    for d in range(1, NX):

        @pl.when(lax.rem(x - d + NX, NX) > x)
        def _():
            g_copy(d).wait_recv()
            acc[...] += grecv[d - 1].astype(F32)

    @pl.when(y_hi == 0)
    def _():
        far_copy.wait_recv()
        acc[...] += frecv[...].astype(F32)
        for part in range(2):
            cross(part).wait_recv()
            acc[:, columns(part)] += xrecv[part].astype(F32)

    kv_low[...] = acc[...].astype(BF)

    def core_copy(p):
        return remote(csend.at[p], ccr.at[p], core_ss.at[p], core_rs.at[p], other_core)

    def proj_part(which, p):
        rows = pl.ds(pl.multiple_of(which * HALF + p * PART, PART), PART)
        return dot(li_t[rows, :], kv_low[...], NN)

    for p in range(PARTS):
        csend[p] = proj_part(1 - core, p).astype(BF)
        core_copy(p).start()

    for n in range(D // 512):
        part = dot(kv_low[...], wcat[n * 512 : (n + 1) * 512, :], NT)
        ipart[:, :, n * 512 : (n + 1) * 512] = part.reshape(NZ, 32, 512)

    def z_copy(direction, k, half):
        return remote(
            zs.at[direction, k, half], zr.at[direction, k, half],
            z_ss.at[direction, k, half], z_rs.at[direction, k, half],
            z_mate(1 - 2 * direction),
        )

    def z_send(direction, k, half, add):
        t = lax.rem(hd + 4 - k, NZ) if direction == 0 else lax.rem(hd + 4 + k, NZ)
        term = ipart[t, :, half * HALF : (half + 1) * HALF]
        if add:
            z_copy(direction, k - 1, half).wait_recv()
            term = term + zr[direction, k - 1, half].astype(F32)
        zs[direction, k, half] = term.astype(BF)
        z_copy(direction, k, half).start()

    def z_step(k, half, add=True):
        z_send(0, k, half, add)
        z_send(1, k, 1 - half, add)

    z_step(0, 0, False)
    z_step(1, 1, False)

    def index(axis):
        return yi if axis else x

    def mate(axis, d):
        if axis:
            return y_mate(lax.rem(yi + d, NX))
        return x_mate(lax.rem(x + d, NX))

    def st1_copy(p, d):
        a = p % 2
        return remote(
            s1.at[p, lax.rem(index(a) + d, NX)], r1.at[p, d - 1],
            st1_ss.at[p, d - 1], st1_rs.at[p, d - 1], mate(a, d),
        )

    def st2_copy(p, d, arrived=False):
        a = 1 - p % 2
        own = index(a)
        slot = lax.rem(own - d + NX, NX) if arrived else own
        return remote(
            r2.at[p, own], r2.at[p, slot], st2_ss.at[p, d - 1], st2_rs.at[p, d - 1], mate(a, d)
        )

    def ag_copy(p, d, arrived=False):
        own = index(p % 2)
        ref = gfull.at[core, p, lax.rem(own - d + NX, NX) if arrived else own]
        return remote(ref, ref, ag_ss.at[p, d - 1], ag_rs.at[p, d - 1], mate(p % 2, d))

    def pair_copy(p, d, arrived=False):
        ref = gfull.at[1 - core if arrived else core, p, lax.rem(index(p % 2) - d + NX, NX)]
        return remote(ref, ref, p_ss.at[p, d], p_rs.at[p, d], other_core)

    for p in range(PARTS):
        h32[p] = proj_part(core, p).reshape(NX, SUB, 2 * HD)

    for p in range(PARTS):
        core_copy(p).wait_recv()
        term = h32[p] + ccr[p].astype(F32).reshape(NX, SUB, 2 * HD)
        h32[p] = term
        s1[p] = term.astype(BF)
        for d in (2, 1, 3):
            st1_copy(p, d).start()

    def stage2(p):
        term = h32[p, index(p % 2)]
        for d in (1, 3, 2):
            st1_copy(p, d).wait_recv()
            term = term + r1[p, d - 1].astype(F32)
        r2[p, index(1 - p % 2)] = term.astype(BF)
        for d in (2, 1, 3):
            st2_copy(p, d).start()

    def gather(p):
        for d in (1, 3, 2):
            st2_copy(p, d, True).wait_recv()
        term = r2[p, 0].astype(F32)
        for i in range(1, NX):
            term = term + r2[p, i].astype(F32)
        gfull[core, p, index(p % 2)] = term.astype(BF)
        for d in (2, 1, 3):
            ag_copy(p, d).start()
        pair_copy(p, 0).start()

    def hand_over(p):
        for d in (1, 3, 2):
            ag_copy(p, d, True).wait_recv()
            pair_copy(p, d).start()

    z_step(1, 0)
    stage2(0)
    stage2(1)
    z_step(2, 1)
    stage2(2)
    stage2(3)
    z_step(2, 0)
    gather(0)
    gather(1)
    z_step(3, 1)
    gather(2)
    gather(3)
    z_step(3, 0)
    hand_over(0)
    hand_over(1)

    for half in range(2):
        term = ipart[hd, :, half * HALF : (half + 1) * HALF]
        for direction in range(2):
            z_copy(direction, 3, half).wait_recv()
            term = term + zr[direction, 3, half].astype(F32)
        ig_out[:, half * HALF : (half + 1) * HALF] = term.astype(BF)

    hand_over(2)
    hand_over(3)
    for p in range(PARTS):
        for d in range(NX):
            pair_copy(p, d, True).wait_recv()

    for d in range(1, NX):
        xt = lax.rem(x + d, NX)

        @pl.when(xt > x)
        def _():
            kv_copy(sq, x_mate(xt), d - 1).wait_send()

        @pl.when(xt < x)
        def _():
            g_copy(d).wait_send()

    @pl.when(y_hi == 0)
    def _():
        for part in range(2):
            kv_part(x, part, other_half, part).wait_send()
        kv_copy(sq, far_mate, 3).wait_send()

    @pl.when(y_hi == 1)
    def _():
        for n, d in enumerate((1, 3)):
            for part in range(2):
                kv_part(x, part, x_mate(lax.rem(x + d, NX)), 2 + 2 * part + n).wait_send()
                c_copy(n, part).wait_send()
        far_copy.wait_send()
        for part in range(2):
            cross(part).wait_send()

    for direction in range(2):
        for n in range(7):
            li_copy(direction, n).wait_send()
        for k in range(4):
            for half in range(2):
                if k > 0 or half == direction:
                    z_copy(direction, k, half).wait_send()
    for p in range(PARTS):
        core_copy(p).wait_send()
        for d in range(1, NX):
            st1_copy(p, d).wait_send()
            st2_copy(p, d).wait_send()
            ag_copy(p, d).wait_send()
        for d in range(NX):
            pair_copy(p, d).wait_send()


def finish(
    qg_in, ig_in, gp_in, qg_ref, ig_ref, gk_ref, gv_ref,
    key, value, sem_key, sem_value, sem,
):
    step = D // PIECES
    copies = [
        pltpu.make_async_copy(qg_in, qg_ref, sem.at[0]),
        pltpu.make_async_copy(ig_in, ig_ref, sem.at[1]),
    ]
    for c in copies:
        c.start()
    for n in range(PIECES):
        rows = pl.ds(n * step, step)
        key[n] = gp_in[rows, 0:HD].astype(F32)
        copies.append(pltpu.make_async_copy(key.at[n], gk_ref.at[rows, :], sem_key.at[n]))
        copies[-1].start()
        value[n] = gp_in[rows, HD:].astype(F32)
        copies.append(pltpu.make_async_copy(value.at[n], gv_ref.at[rows, :], sem_value.at[n]))
        copies[-1].start()
    for c in copies:
        c.wait()


def shards(queries, key_cache, value_cache, out_grad, doc_ids, layer_input, key_proj, value_proj):
    hbm = pl.BlockSpec(memory_space=pl.ANY)
    vmem = pl.BlockSpec(memory_space=pltpu.VMEM)
    dma = pltpu.SemaphoreType.DMA
    scratch = [
        pltpu.VMEM((GROUP, ROWS, HD), BF),
        pltpu.VMEM((GROUP, ROWS, HD), BF),
        pltpu.VMEM((1, ROWS), jnp.int32),
        pltpu.VMEM((NS, 2 * ROWS + 16, HD), BF),
        pltpu.VMEM((NZ, 32, D), BF),
        pltpu.VMEM((D, ROWS), BF),
        pltpu.VMEM((D, 2 * HD), BF),
        pltpu.VMEM((NS, GROUP, ROWS, ROWS), F32),
        pltpu.VMEM((NS, GROUP, ROWS, ROWS), F32),
        pltpu.VMEM((NS, 8, ROWS), F32),
        pltpu.VMEM((NS, 8, ROWS), F32),
        pltpu.VMEM((NS, 8, ROWS), F32),
        pltpu.VMEM((NS, 8, ROWS), F32),
        pltpu.VMEM((GROUP, HD, ROWS), F32),
        pltpu.VMEM((NS, ROWS, 2 * HD), BF),
        pltpu.VMEM((NX - 1, ROWS, 2 * HD), BF),
        pltpu.VMEM((2, 2, ROWS, HD), BF),
        pltpu.VMEM((2, ROWS, HD), BF),
        pltpu.VMEM((2, ROWS, HD), BF),
        pltpu.VMEM((ROWS, 2 * HD), BF),
        pltpu.VMEM((ROWS, 2 * HD), F32),
        pltpu.VMEM((ROWS, 2 * HD), BF),
        pltpu.VMEM((NZ, 32, D), F32),
        pltpu.VMEM((2, 4, 2, 32, HALF), BF),
        pltpu.VMEM((2, 4, 2, 32, HALF), BF),
        pltpu.VMEM((PARTS, PART, 2 * HD), BF),
        pltpu.VMEM((PARTS, PART, 2 * HD), BF),
        pltpu.VMEM((PARTS, NX, SUB, 2 * HD), F32),
        pltpu.VMEM((PARTS, NX, SUB, 2 * HD), BF),
        pltpu.VMEM((PARTS, NX - 1, SUB, 2 * HD), BF),
        pltpu.VMEM((PARTS, NX, SUB, 2 * HD), BF),
        dma((12,)),
        dma((NX,)),
        dma((NS,)),
        dma((6,)),
        dma((NX, 2)),
        dma((2, 7)),
        dma((2, 7)),
        dma((NX - 1,)),
        dma((NX - 1,)),
        dma((2, 2)),
        dma((2, 2)),
        dma((3,)),
        dma((3,)),
        dma((2, 4, 2)),
        dma((2, 4, 2)),
        dma((PARTS,)),
        dma((PARTS,)),
        dma((PARTS, 3)),
        dma((PARTS, 3)),
        dma((PARTS, 3)),
        dma((PARTS, 3)),
        dma((PARTS, 3)),
        dma((PARTS, 3)),
        dma((PARTS, 4)),
        dma((PARTS, 4)),
    ]
    qg, ig, gp = pl.pallas_call(
        kernel,
        out_shape=(
            pltpu.VMEM((ROWS, GROUP * HD), BF),
            pltpu.VMEM((32, D), BF),
            pltpu.VMEM((2, PARTS, NX, SUB, 2 * HD), BF),
        ),
        in_specs=[hbm] * 8,
        out_specs=(vmem,) * 3,
        scratch_shapes=scratch,
        compiler_params=pltpu.CompilerParams(
            collective_id=0, has_side_effects=True, vmem_limit_bytes=56 * 1024 * 1024
        ),
        cost_estimate=pl.CostEstimate(
            flops=3 * 10**9, bytes_accessed=8 * 10**6, transcendentals=2 * 10**6
        ),
    )(
        queries[0], key_cache[0], value_cache[0], out_grad[0], doc_ids, layer_input[0],
        key_proj, value_proj,
    )
    step = D // PIECES
    qg, ig, gk, gv = pl.pallas_call(
        finish,
        out_shape=(
            jax.ShapeDtypeStruct((ROWS, GROUP * HD), BF),
            jax.ShapeDtypeStruct((32, D), BF),
            jax.ShapeDtypeStruct((D, HD), F32),
            jax.ShapeDtypeStruct((D, HD), F32),
        ),
        in_specs=[vmem] * 3,
        out_specs=(hbm,) * 4,
        scratch_shapes=[
            pltpu.VMEM((PIECES, step, HD), F32),
            pltpu.VMEM((PIECES, step, HD), F32),
            dma((PIECES,)),
            dma((PIECES,)),
            dma((2,)),
        ],
        compiler_params=pltpu.CompilerParams(vmem_limit_bytes=24 * 1024 * 1024),
        cost_estimate=pl.CostEstimate(flops=0, bytes_accessed=6 * 10**6, transcendentals=0),
    )(qg, ig, gp.reshape(D, 2 * HD))
    return qg[None], ig[None], gk, gv


def solution(mesh):
    return jax.shard_map(
        shards,
        mesh=mesh,
        in_specs=(
            P("dp", "seq", "head"),
            P("dp", "seq", "head"),
            P("dp", "seq", "head"),
            P("dp", "seq", "head"),
            P("dp", "seq"),
            P("dp", ("seq", "head"), None),
            P(None, "head"),
            P(None, "head"),
        ),
        out_specs=(
            P("dp", "seq", "head"),
            P("dp", ("seq", "head"), None),
            P(None, "head"),
            P(None, "head"),
        ),
        check_vma=False,
    )
```

```python
import functools
import math

import jax
import jax.numpy as jnp
from jax import lax
from jax.experimental import pallas as pl
from jax.experimental.pallas import tpu as pltpu
from jax.sharding import PartitionSpec as P

D = 3072
HD = 128
GROUP = 3
ROWS = 256
NX = 4
NZ = 8
NEG_FILL = -1e30
SCALE = HD ** (-0.5)
EXP_SCALE = SCALE * math.log2(math.e)
HALF = D // 2
NS = 8
PARTS = 4
PART = HALF // PARTS
SUB = PART // NX
PIECES = 4
BF = jnp.bfloat16
F32 = jnp.float32
NT = (((1,), (1,)), ((), ()))
NN = (((1,), (0,)), ((), ()))


def dot(a, b, dims):
    return lax.dot_general(a, b, dims, preferred_element_type=F32)


def kernel(
    q_hbm, k_hbm, v_hbm, do_hbm, docs_hbm, li_hbm, wk_hbm, wv_hbm,
    qg_out, ig_out, gfull,
    q_v, do_v, docs_ref, kvbuf, li_buf, li_t, wcat,
    p_buf, dp_buf, m_buf, l_buf, a_buf, f_buf, dq_t,
    gsend, grecv, crecv, xsend, xrecv, frecv, acc, kv_low,
    ipart, zs, zr,
    csend, ccr, h32, s1, r1, r2,
    loc, kv_ss, kv_rs, kv_ps, kv_pr, li_ss, li_rs, g_ss, g_rs, c_ss, c_rs, x_ss, x_rs,
    z_ss, z_rs, core_ss, core_rs, st1_ss, st1_rs, st2_ss, st2_rs,
    ag_ss, ag_rs, p_ss, p_rs,
):
    dp = lax.axis_index("dp")
    sq = lax.axis_index("seq")
    hd = lax.axis_index("head")
    core = lax.rem(dp, 2)
    y_lo = lax.div(dp, 2)
    y_hi = lax.div(sq, NX)
    x = lax.rem(sq, NX)
    yi = y_hi * 2 + y_lo

    def x_mate(idx):
        return (dp, y_hi * NX + idx, hd)

    def y_mate(idx):
        return (lax.rem(idx, 2) * 2 + core, lax.div(idx, 2) * NX + x, hd)

    other_half = (dp, (1 - y_hi) * NX + x, hd)
    far_x = lax.rem(x + 2, NX)
    far_mate = (dp, (1 - y_hi) * NX + far_x, hd)
    other_core = (y_lo * 2 + 1 - core, sq, hd)

    def z_mate(d):
        return (dp, sq, lax.rem(hd + d + NZ, NZ))

    def remote(src, dst, ssem, rsem, dev):
        return pltpu.make_async_remote_copy(
            src_ref=src, dst_ref=dst, send_sem=ssem, recv_sem=rsem,
            device_id=dev, device_id_type=pl.DeviceIdType.MESH,
        )

    barrier = pltpu.get_barrier_semaphore()
    partners = [x_mate(lax.rem(x + d, NX)) for d in range(1, NX)]
    partners += [y_mate(lax.rem(yi + d, NX)) for d in range(1, NX)]
    partners += [far_mate, other_core, z_mate(1), z_mate(-1)]
    for dev in partners:
        pl.semaphore_signal(barrier, inc=1, device_id=dev, device_id_type=pl.DeviceIdType.MESH)

    loads = [
        pltpu.make_async_copy(docs_hbm, docs_ref, loc.at[0]),
        pltpu.make_async_copy(k_hbm, kvbuf.at[sq, pl.ds(0, ROWS), :], loc.at[1]),
        pltpu.make_async_copy(v_hbm, kvbuf.at[sq, pl.ds(ROWS, ROWS), :], loc.at[2]),
        pltpu.make_async_copy(li_hbm, li_buf.at[hd], loc.at[3]),
    ]
    for g in range(GROUP):
        loads.append(pltpu.make_async_copy(q_hbm.at[:, pl.ds(g * HD, HD)], q_v.at[g], loc.at[4 + g]))
        loads.append(pltpu.make_async_copy(do_hbm.at[:, pl.ds(g * HD, HD)], do_v.at[g], loc.at[7 + g]))
    loads.append(pltpu.make_async_copy(wk_hbm, wcat.at[:, pl.ds(0, HD)], loc.at[10]))
    loads.append(pltpu.make_async_copy(wv_hbm, wcat.at[:, pl.ds(HD, HD)], loc.at[11]))
    for c in loads:
        c.start()

    m_buf[...] = jnp.full(m_buf.shape, NEG_FILL, F32)
    l_buf[...] = jnp.zeros(l_buf.shape, F32)
    a_buf[...] = jnp.zeros(a_buf.shape, F32)
    dq_t[...] = jnp.zeros(dq_t.shape, F32)

    loads[0].wait()
    doc_row = docs_ref[...].astype(F32)
    upper = lax.broadcasted_iota(jnp.int32, (16, HD), 0) < 8
    doc_tile = jnp.where(
        upper,
        jnp.broadcast_to(doc_row[:, 0:HD], (16, HD)),
        jnp.broadcast_to(doc_row[:, HD:], (16, HD)),
    )
    kvbuf[sq, pl.ds(2 * ROWS, 16), :] = doc_tile.astype(BF)
    for c in loads[1:3]:
        c.wait()
    pl.semaphore_wait(barrier, len(partners))

    def kv_copy(block, dev, s):
        return remote(kvbuf.at[block], kvbuf.at[block], kv_ss.at[s], kv_rs.at[block], dev)

    def kv_arrived(block):
        return kv_copy(block, other_half, 0)

    def kv_part(block, part, dev, s):
        ref = kvbuf.at[block, pl.ds(part * ROWS, ROWS + 16 * part), :]
        return remote(ref, ref, kv_ps.at[s], kv_pr.at[block, part], dev)

    @pl.when(y_hi == 0)
    def _():
        for part in range(2):
            kv_part(x, part, other_half, part).start()
        kv_copy(sq, far_mate, 3).start()

    for d in (2, 1, 3):
        xt = lax.rem(x + d, NX)

        @pl.when(xt > x)
        def _():
            kv_copy(sq, x_mate(xt), d - 1).start()

    def li_copy(direction, n, arrived=False):
        sign = 1 - 2 * direction
        away = n // 2 + 1 if arrived else n // 2
        half = direction if n == 6 else n % 2
        ref = li_buf.at[lax.rem(hd - sign * away + NZ, NZ), pl.ds(16 * half, 16), :]
        return remote(ref, ref, li_ss.at[direction, n], li_rs.at[direction, n], z_mate(sign))

    def li_start(n):
        for direction in range(2):
            li_copy(direction, n).start()

    def li_wait(n):
        for direction in range(2):
            li_copy(direction, n, True).wait_recv()

    def li_next(n):
        li_wait(n)
        if n == 4:
            li_copy(0, 6).start()
        elif n == 5:
            li_copy(1, 6).start()
        else:
            li_start(n + 2)

    loads[3].wait()
    li_start(0)
    li_start(1)

    for c in loads[4:10]:
        c.wait()

    key_iota = lax.broadcasted_iota(jnp.int32, (ROWS, ROWS), 0).astype(F32)

    def score_block(b, diagonal):
        kb = kvbuf[b, pl.ds(0, ROWS), :]
        vb = kvbuf[b, pl.ds(ROWS, ROWS), :]
        docs = kvbuf[b, pl.ds(2 * ROWS, 16), :].astype(F32)
        ones = jnp.sum(jnp.sum(docs, axis=0, keepdims=True), axis=1, keepdims=True) * 0.125
        zeros = ROWS - ones
        low = doc_row * zeros
        high = zeros + doc_row * ones
        if diagonal:
            own = lax.broadcasted_iota(jnp.int32, (1, ROWS), 1).astype(F32)
            high = jnp.minimum(high, own + 1.0)
        allowed = (key_iota >= low) & (key_iota < high)
        for g in range(GROUP):
            s = jnp.where(allowed, dot(kb, q_v[g], NT), NEG_FILL)
            top = jnp.max(s, axis=0, keepdims=True)
            p = jnp.exp2((s - top) * EXP_SCALE)
            wg = dot(vb, do_v[g], NT)
            p_buf[b, g] = p
            dp_buf[b, g] = wg
            m_buf[b, g : g + 1, :] = top
            l_buf[b, g : g + 1, :] = jnp.sum(p, axis=0, keepdims=True)
            a_buf[b, g : g + 1, :] = jnp.sum(p * wg, axis=0, keepdims=True)

    score_block(sq, True)

    @pl.when(y_hi == 1)
    def _():
        for part in range(2):
            kv_part(x, part, other_half, 0).wait_recv()
            for n, d in enumerate((1, 3)):
                kv_part(x, part, x_mate(lax.rem(x + d, NX)), 2 + 2 * part + n).start()

    li_next(0)

    @pl.loop(1, NX)
    def _(d):
        @pl.when(d <= x)
        def _():
            kv_arrived(sq - d).wait_recv()
            score_block(sq - d, False)

    li_next(1)

    @pl.when(y_hi == 1)
    def _():
        score_block(x, False)

    li_next(2)

    @pl.when(y_hi == 1)
    def _():
        kv_arrived(far_x).wait_recv()
        score_block(far_x, False)

        @pl.loop(0, 2)
        def _(n):
            b = lax.rem(x + 1 + 2 * n, NX)
            for part in range(2):
                kv_part(b, part, other_half, 0).wait_recv()
            score_block(b, False)

    li_next(3)

    top = jnp.max(m_buf[...], axis=0)
    factor = jnp.exp2((m_buf[...] - top[None]) * EXP_SCALE)
    total = jnp.sum(factor * l_buf[...], axis=0)
    gathered = jnp.sum(factor * a_buf[...], axis=0)
    safe = jnp.where(total > 0.0, total, 1.0)
    inv = 1.0 / safe
    delta = gathered * inv
    f_buf[...] = factor * inv[None]

    def grad_block(b):
        kbt = kvbuf[b, pl.ds(0, ROWS), :].T
        dk = jnp.zeros((ROWS, HD), F32)
        dv = jnp.zeros((ROWS, HD), F32)
        for g in range(GROUP):
            w = p_buf[b, g] * f_buf[b, g : g + 1, :]
            sg = (w * (dp_buf[b, g] - delta[g : g + 1, :]) * SCALE).astype(BF)
            dv = dv + dot(w.astype(BF), do_v[g], NN)
            dk = dk + dot(sg, q_v[g], NN)
            dq_t[g] += dot(kbt, sg, NN)
        gsend[b, :, 0:HD] = dk.astype(BF)
        gsend[b, :, HD:] = dv.astype(BF)

    def g_copy(d):
        xt = lax.rem(x + d, NX)
        return remote(
            gsend.at[y_hi * NX + xt], grecv.at[d - 1], g_ss.at[d - 1], g_rs.at[d - 1], x_mate(xt)
        )

    def columns(part):
        return pl.ds(part * HD, HD)

    def c_copy(n, part):
        xt = lax.rem(x + 1 + 2 * n, NX)
        return remote(
            gsend.at[xt, :, columns(part)], crecv.at[n, part],
            c_ss.at[n, part], c_rs.at[n, part], x_mate(xt),
        )

    far_copy = remote(gsend.at[far_x], frecv, x_ss.at[2], x_rs.at[2], far_mate)

    def cross(part):
        return remote(xsend.at[part], xrecv.at[part], x_ss.at[part], x_rs.at[part], other_half)

    @pl.when(y_hi == 1)
    def _():
        grad_block(far_x)
        far_copy.start()

        @pl.loop(0, 2)
        def _(n):
            grad_block(lax.rem(x + 1 + 2 * n, NX))
            for part in range(2):
                c_copy(n, part).start()

    li_next(4)

    @pl.when(y_hi == 1)
    def _():
        grad_block(x)

    @pl.loop(1, NX)
    def _(d):
        xt = lax.rem(x + d, NX)

        @pl.when(xt < x)
        def _():
            grad_block(y_hi * NX + xt)
            g_copy(d).start()

    li_next(5)

    @pl.when(y_hi == 1)
    def _():
        for part in range(2):
            term = gsend[x, :, columns(part)].astype(F32)
            for n in range(2):
                c_copy(n, part).wait_recv()
                term = term + crecv[n, part].astype(F32)
            xsend[part] = term.astype(BF)
            cross(part).start()

    grad_block(sq)

    for g in range(GROUP):
        qg_out[:, g * HD : (g + 1) * HD] = dq_t[g].T.astype(BF)

    for c in loads[10:]:
        c.wait()

    li_wait(6)
    for n in range(D // 512):
        cols = li_buf[:, :, n * 512 : (n + 1) * 512].reshape(ROWS, 512)
        li_t[n * 512 : (n + 1) * 512, :] = cols.T

    acc[...] = gsend[sq].astype(F32)

    for d in range(1, NX):

        @pl.when(lax.rem(x - d + NX, NX) > x)
        def _():
            g_copy(d).wait_recv()
            acc[...] += grecv[d - 1].astype(F32)

    @pl.when(y_hi == 0)
    def _():
        far_copy.wait_recv()
        acc[...] += frecv[...].astype(F32)
        for part in range(2):
            cross(part).wait_recv()
            acc[:, columns(part)] += xrecv[part].astype(F32)

    kv_low[...] = acc[...].astype(BF)

    def core_copy(p):
        return remote(csend.at[p], ccr.at[p], core_ss.at[p], core_rs.at[p], other_core)

    def proj_part(which, p):
        rows = pl.ds(pl.multiple_of(which * HALF + p * PART, PART), PART)
        return dot(li_t[rows, :], kv_low[...], NN)

    for p in range(PARTS):
        csend[p] = proj_part(1 - core, p).astype(BF)
        core_copy(p).start()

    for n in range(D // 512):
        part = dot(kv_low[...], wcat[n * 512 : (n + 1) * 512, :], NT)
        ipart[:, :, n * 512 : (n + 1) * 512] = part.reshape(NZ, 32, 512)

    def z_copy(direction, k, half):
        return remote(
            zs.at[direction, k, half], zr.at[direction, k, half],
            z_ss.at[direction, k, half], z_rs.at[direction, k, half],
            z_mate(1 - 2 * direction),
        )

    def z_send(direction, k, half, add):
        t = lax.rem(hd + 4 - k, NZ) if direction == 0 else lax.rem(hd + 4 + k, NZ)
        term = ipart[t, :, half * HALF : (half + 1) * HALF]
        if add:
            z_copy(direction, k - 1, half).wait_recv()
            term = term + zr[direction, k - 1, half].astype(F32)
        zs[direction, k, half] = term.astype(BF)
        z_copy(direction, k, half).start()

    def z_step(k, half, add=True):
        z_send(0, k, half, add)
        z_send(1, k, 1 - half, add)

    z_step(0, 0, False)
    z_step(1, 1, False)

    def index(axis):
        return yi if axis else x

    def mate(axis, d):
        if axis:
            return y_mate(lax.rem(yi + d, NX))
        return x_mate(lax.rem(x + d, NX))

    def st1_copy(p, d):
        a = p % 2
        return remote(
            s1.at[p, lax.rem(index(a) + d, NX)], r1.at[p, d - 1],
            st1_ss.at[p, d - 1], st1_rs.at[p, d - 1], mate(a, d),
        )

    def st2_copy(p, d, arrived=False):
        a = 1 - p % 2
        own = index(a)
        slot = lax.rem(own - d + NX, NX) if arrived else own
        return remote(
            r2.at[p, own], r2.at[p, slot], st2_ss.at[p, d - 1], st2_rs.at[p, d - 1], mate(a, d)
        )

    def ag_copy(p, d, arrived=False):
        own = index(p % 2)
        ref = gfull.at[core, p, lax.rem(own - d + NX, NX) if arrived else own]
        return remote(ref, ref, ag_ss.at[p, d - 1], ag_rs.at[p, d - 1], mate(p % 2, d))

    def pair_copy(p, d, arrived=False):
        ref = gfull.at[1 - core if arrived else core, p, lax.rem(index(p % 2) - d + NX, NX)]
        return remote(ref, ref, p_ss.at[p, d], p_rs.at[p, d], other_core)

    for p in range(PARTS):
        h32[p] = proj_part(core, p).reshape(NX, SUB, 2 * HD)

    for p in range(PARTS):
        core_copy(p).wait_recv()
        term = h32[p] + ccr[p].astype(F32).reshape(NX, SUB, 2 * HD)
        h32[p] = term
        s1[p] = term.astype(BF)
        for d in (2, 1, 3):
            st1_copy(p, d).start()

    def stage2(p):
        term = h32[p, index(p % 2)]
        for d in (1, 3, 2):
            st1_copy(p, d).wait_recv()
            term = term + r1[p, d - 1].astype(F32)
        r2[p, index(1 - p % 2)] = term.astype(BF)
        for d in (2, 1, 3):
            st2_copy(p, d).start()

    def gather(p):
        for d in (1, 3, 2):
            st2_copy(p, d, True).wait_recv()
        term = r2[p, 0].astype(F32)
        for i in range(1, NX):
            term = term + r2[p, i].astype(F32)
        gfull[core, p, index(p % 2)] = term.astype(BF)
        for d in (2, 1, 3):
            ag_copy(p, d).start()
        pair_copy(p, 0).start()

    def hand_over(p):
        for d in (1, 3, 2):
            ag_copy(p, d, True).wait_recv()
            pair_copy(p, d).start()

    z_step(1, 0)
    stage2(0)
    stage2(1)
    z_step(2, 1)
    stage2(2)
    stage2(3)
    z_step(2, 0)
    gather(0)
    gather(1)
    z_step(3, 1)
    gather(2)
    gather(3)
    z_step(3, 0)
    hand_over(0)
    hand_over(1)

    for half in range(2):
        term = ipart[hd, :, half * HALF : (half + 1) * HALF]
        for direction in range(2):
            z_copy(direction, 3, half).wait_recv()
            term = term + zr[direction, 3, half].astype(F32)
        ig_out[:, half * HALF : (half + 1) * HALF] = term.astype(BF)

    hand_over(2)
    hand_over(3)
    for p in range(PARTS):
        for d in range(NX):
            pair_copy(p, d, True).wait_recv()

    for d in range(1, NX):
        xt = lax.rem(x + d, NX)

        @pl.when(xt > x)
        def _():
            kv_copy(sq, x_mate(xt), d - 1).wait_send()

        @pl.when(xt < x)
        def _():
            g_copy(d).wait_send()

    @pl.when(y_hi == 0)
    def _():
        for part in range(2):
            kv_part(x, part, other_half, part).wait_send()
        kv_copy(sq, far_mate, 3).wait_send()

    @pl.when(y_hi == 1)
    def _():
        for n, d in enumerate((1, 3)):
            for part in range(2):
                kv_part(x, part, x_mate(lax.rem(x + d, NX)), 2 + 2 * part + n).wait_send()
                c_copy(n, part).wait_send()
        far_copy.wait_send()
        for part in range(2):
            cross(part).wait_send()

    for direction in range(2):
        for n in range(7):
            li_copy(direction, n).wait_send()
        for k in range(4):
            for half in range(2):
                if k > 0 or half == direction:
                    z_copy(direction, k, half).wait_send()
    for p in range(PARTS):
        core_copy(p).wait_send()
        for d in range(1, NX):
            st1_copy(p, d).wait_send()
            st2_copy(p, d).wait_send()
            ag_copy(p, d).wait_send()
        for d in range(NX):
            pair_copy(p, d).wait_send()


def finish(
    qg_in, ig_in, gp_in, qg_ref, ig_ref, gk_ref, gv_ref,
    key, value, sem_key, sem_value, sem,
):
    step = D // PIECES
    copies = [
        pltpu.make_async_copy(qg_in, qg_ref, sem.at[0]),
        pltpu.make_async_copy(ig_in, ig_ref, sem.at[1]),
    ]
    for c in copies:
        c.start()
    for n in range(PIECES):
        rows = pl.ds(n * step, step)
        key[n] = gp_in[rows, 0:HD].astype(F32)
        copies.append(pltpu.make_async_copy(key.at[n], gk_ref.at[rows, :], sem_key.at[n]))
        copies[-1].start()
        value[n] = gp_in[rows, HD:].astype(F32)
        copies.append(pltpu.make_async_copy(value.at[n], gv_ref.at[rows, :], sem_value.at[n]))
        copies[-1].start()
    for c in copies:
        c.wait()


def shards(queries, key_cache, value_cache, out_grad, doc_ids, layer_input, key_proj, value_proj):
    hbm = pl.BlockSpec(memory_space=pl.ANY)
    vmem = pl.BlockSpec(memory_space=pltpu.VMEM)
    dma = pltpu.SemaphoreType.DMA
    scratch = [
        pltpu.VMEM((GROUP, ROWS, HD), BF),
        pltpu.VMEM((GROUP, ROWS, HD), BF),
        pltpu.VMEM((1, ROWS), jnp.int32),
        pltpu.VMEM((NS, 2 * ROWS + 16, HD), BF),
        pltpu.VMEM((NZ, 32, D), BF),
        pltpu.VMEM((D, ROWS), BF),
        pltpu.VMEM((D, 2 * HD), BF),
        pltpu.VMEM((NS, GROUP, ROWS, ROWS), F32),
        pltpu.VMEM((NS, GROUP, ROWS, ROWS), F32),
        pltpu.VMEM((NS, 8, ROWS), F32),
        pltpu.VMEM((NS, 8, ROWS), F32),
        pltpu.VMEM((NS, 8, ROWS), F32),
        pltpu.VMEM((NS, 8, ROWS), F32),
        pltpu.VMEM((GROUP, HD, ROWS), F32),
        pltpu.VMEM((NS, ROWS, 2 * HD), BF),
        pltpu.VMEM((NX - 1, ROWS, 2 * HD), BF),
        pltpu.VMEM((2, 2, ROWS, HD), BF),
        pltpu.VMEM((2, ROWS, HD), BF),
        pltpu.VMEM((2, ROWS, HD), BF),
        pltpu.VMEM((ROWS, 2 * HD), BF),
        pltpu.VMEM((ROWS, 2 * HD), F32),
        pltpu.VMEM((ROWS, 2 * HD), BF),
        pltpu.VMEM((NZ, 32, D), F32),
        pltpu.VMEM((2, 4, 2, 32, HALF), BF),
        pltpu.VMEM((2, 4, 2, 32, HALF), BF),
        pltpu.VMEM((PARTS, PART, 2 * HD), BF),
        pltpu.VMEM((PARTS, PART, 2 * HD), BF),
        pltpu.VMEM((PARTS, NX, SUB, 2 * HD), F32),
        pltpu.VMEM((PARTS, NX, SUB, 2 * HD), BF),
        pltpu.VMEM((PARTS, NX - 1, SUB, 2 * HD), BF),
        pltpu.VMEM((PARTS, NX, SUB, 2 * HD), BF),
        dma((12,)),
        dma((NX,)),
        dma((NS,)),
        dma((6,)),
        dma((NX, 2)),
        dma((2, 7)),
        dma((2, 7)),
        dma((NX - 1,)),
        dma((NX - 1,)),
        dma((2, 2)),
        dma((2, 2)),
        dma((3,)),
        dma((3,)),
        dma((2, 4, 2)),
        dma((2, 4, 2)),
        dma((PARTS,)),
        dma((PARTS,)),
        dma((PARTS, 3)),
        dma((PARTS, 3)),
        dma((PARTS, 3)),
        dma((PARTS, 3)),
        dma((PARTS, 3)),
        dma((PARTS, 3)),
        dma((PARTS, 4)),
        dma((PARTS, 4)),
    ]
    qg, ig, gp = pl.pallas_call(
        kernel,
        out_shape=(
            pltpu.VMEM((ROWS, GROUP * HD), BF),
            pltpu.VMEM((32, D), BF),
            pltpu.VMEM((2, PARTS, NX, SUB, 2 * HD), BF),
        ),
        in_specs=[hbm] * 8,
        out_specs=(vmem,) * 3,
        scratch_shapes=scratch,
        compiler_params=pltpu.CompilerParams(
            collective_id=0, has_side_effects=True, vmem_limit_bytes=56 * 1024 * 1024
        ),
        cost_estimate=pl.CostEstimate(
            flops=3 * 10**9, bytes_accessed=8 * 10**6, transcendentals=2 * 10**6
        ),
    )(
        queries[0], key_cache[0], value_cache[0], out_grad[0], doc_ids, layer_input[0],
        key_proj, value_proj,
    )
    step = D // PIECES
    qg, ig, gk, gv = pl.pallas_call(
        finish,
        out_shape=(
            jax.ShapeDtypeStruct((ROWS, GROUP * HD), BF),
            jax.ShapeDtypeStruct((32, D), BF),
            jax.ShapeDtypeStruct((D, HD), F32),
            jax.ShapeDtypeStruct((D, HD), F32),
        ),
        in_specs=[vmem] * 3,
        out_specs=(hbm,) * 4,
        scratch_shapes=[
            pltpu.VMEM((PIECES, step, HD), F32),
            pltpu.VMEM((PIECES, step, HD), F32),
            dma((PIECES,)),
            dma((PIECES,)),
            dma((2,)),
        ],
        compiler_params=pltpu.CompilerParams(vmem_limit_bytes=24 * 1024 * 1024),
        cost_estimate=pl.CostEstimate(flops=0, bytes_accessed=6 * 10**6, transcendentals=0),
    )(qg, ig, gp.reshape(D, 2 * HD))
    return qg[None], ig[None], gk, gv


def solution(mesh):
    return jax.shard_map(
        shards,
        mesh=mesh,
        in_specs=(
            P("dp", "seq", "head"),
            P("dp", "seq", "head"),
            P("dp", "seq", "head"),
            P("dp", "seq", "head"),
            P("dp", "seq"),
            P("dp", ("seq", "head"), None),
            P(None, "head"),
            P(None, "head"),
        ),
        out_specs=(
            P("dp", "seq", "head"),
            P("dp", ("seq", "head"), None),
            P(None, "head"),
            P(None, "head"),
        ),
        check_vma=False,
    )
```

```python
import functools
import math

import jax
import jax.numpy as jnp
from jax import lax
from jax.experimental import pallas as pl
from jax.experimental.pallas import tpu as pltpu
from jax.sharding import PartitionSpec as P

D = 3072
HD = 128
GROUP = 3
ROWS = 256
NX = 4
NZ = 8
NEG_FILL = -1e30
SCALE = HD ** (-0.5)
EXP_SCALE = SCALE * math.log2(math.e)
HALF = D // 2
NS = 8
PARTS = 4
PART = HALF // PARTS
SUB = PART // NX
PIECES = 4
BF = jnp.bfloat16
F32 = jnp.float32
NT = (((1,), (1,)), ((), ()))
NN = (((1,), (0,)), ((), ()))


def dot(a, b, dims):
    return lax.dot_general(a, b, dims, preferred_element_type=F32)


def kernel(
    q_hbm, k_hbm, v_hbm, do_hbm, docs_hbm, li_hbm, wk_hbm, wv_hbm,
    qg_out, ig_out, gfull,
    q_v, do_v, docs_ref, kvbuf, li_buf, li_t, wcat,
    p_buf, dp_buf, m_buf, l_buf, a_buf, f_buf, dq_t,
    gsend, grecv, crecv, xsend, xrecv, frecv, acc, kv_low,
    ipart, zs, zr,
    csend, ccr, h32, s1, r1, r2,
    loc, kv_ss, kv_rs, kv_ps, kv_pr, li_ss, li_rs, g_ss, g_rs, c_ss, c_rs, x_ss, x_rs,
    z_ss, z_rs, core_ss, core_rs, st1_ss, st1_rs, st2_ss, st2_rs,
    ag_ss, ag_rs, p_ss, p_rs,
):
    dp = lax.axis_index("dp")
    sq = lax.axis_index("seq")
    hd = lax.axis_index("head")
    core = lax.rem(dp, 2)
    y_lo = lax.div(dp, 2)
    y_hi = lax.div(sq, NX)
    x = lax.rem(sq, NX)
    yi = y_hi * 2 + y_lo

    def x_mate(idx):
        return (dp, y_hi * NX + idx, hd)

    def y_mate(idx):
        return (lax.rem(idx, 2) * 2 + core, lax.div(idx, 2) * NX + x, hd)

    other_half = (dp, (1 - y_hi) * NX + x, hd)
    far_x = lax.rem(x + 2, NX)
    far_mate = (dp, (1 - y_hi) * NX + far_x, hd)
    other_core = (y_lo * 2 + 1 - core, sq, hd)

    def z_mate(d):
        return (dp, sq, lax.rem(hd + d + NZ, NZ))

    def remote(src, dst, ssem, rsem, dev):
        return pltpu.make_async_remote_copy(
            src_ref=src, dst_ref=dst, send_sem=ssem, recv_sem=rsem,
            device_id=dev, device_id_type=pl.DeviceIdType.MESH,
        )

    barrier = pltpu.get_barrier_semaphore()
    partners = [x_mate(lax.rem(x + d, NX)) for d in range(1, NX)]
    partners += [y_mate(lax.rem(yi + d, NX)) for d in range(1, NX)]
    partners += [other_core, z_mate(1), z_mate(-1)]
    for dev in partners:
        pl.semaphore_signal(barrier, inc=1, device_id=dev, device_id_type=pl.DeviceIdType.MESH)

    loads = [
        pltpu.make_async_copy(docs_hbm, docs_ref, loc.at[0]),
        pltpu.make_async_copy(k_hbm, kvbuf.at[sq, pl.ds(0, ROWS), :], loc.at[1]),
        pltpu.make_async_copy(v_hbm, kvbuf.at[sq, pl.ds(ROWS, ROWS), :], loc.at[2]),
        pltpu.make_async_copy(li_hbm, li_buf.at[hd], loc.at[3]),
    ]
    for g in range(GROUP):
        loads.append(pltpu.make_async_copy(q_hbm.at[:, pl.ds(g * HD, HD)], q_v.at[g], loc.at[4 + g]))
        loads.append(pltpu.make_async_copy(do_hbm.at[:, pl.ds(g * HD, HD)], do_v.at[g], loc.at[7 + g]))
    loads.append(pltpu.make_async_copy(wk_hbm, wcat.at[:, pl.ds(0, HD)], loc.at[10]))
    loads.append(pltpu.make_async_copy(wv_hbm, wcat.at[:, pl.ds(HD, HD)], loc.at[11]))
    for c in loads:
        c.start()

    m_buf[...] = jnp.full(m_buf.shape, NEG_FILL, F32)
    l_buf[...] = jnp.zeros(l_buf.shape, F32)
    a_buf[...] = jnp.zeros(a_buf.shape, F32)
    dq_t[...] = jnp.zeros(dq_t.shape, F32)

    loads[0].wait()
    doc_row = docs_ref[...].astype(F32)
    upper = lax.broadcasted_iota(jnp.int32, (16, HD), 0) < 8
    doc_tile = jnp.where(
        upper,
        jnp.broadcast_to(doc_row[:, 0:HD], (16, HD)),
        jnp.broadcast_to(doc_row[:, HD:], (16, HD)),
    )
    kvbuf[sq, pl.ds(2 * ROWS, 16), :] = doc_tile.astype(BF)
    for c in loads[1:3]:
        c.wait()
    pl.semaphore_wait(barrier, len(partners))

    def kv_copy(block, dev, s):
        return remote(kvbuf.at[block], kvbuf.at[block], kv_ss.at[s], kv_rs.at[block], dev)

    def kv_arrived(block):
        return kv_copy(block, other_half, 0)

    def kv_part(block, part, dev, s):
        ref = kvbuf.at[block, pl.ds(part * ROWS, ROWS + 16 * part), :]
        return remote(ref, ref, kv_ps.at[s], kv_pr.at[block, part], dev)

    @pl.when(y_hi == 0)
    def _():
        for part in range(2):
            kv_part(x, part, other_half, part).start()
        kv_copy(sq, x_mate(far_x), 1).start()

    for d in (2, 1, 3):
        xt = lax.rem(x + d, NX)

        @pl.when((xt > x) & ((y_hi == 1) if d == 2 else True))
        def _():
            kv_copy(sq, x_mate(xt), d - 1).start()

    def li_copy(direction, n, arrived=False):
        sign = 1 - 2 * direction
        away = n // 2 + 1 if arrived else n // 2
        half = direction if n == 6 else n % 2
        ref = li_buf.at[lax.rem(hd - sign * away + NZ, NZ), pl.ds(16 * half, 16), :]
        return remote(ref, ref, li_ss.at[direction, n], li_rs.at[direction, n], z_mate(sign))

    def li_start(n):
        for direction in range(2):
            li_copy(direction, n).start()

    def li_wait(n):
        for direction in range(2):
            li_copy(direction, n, True).wait_recv()

    def li_next(n):
        li_wait(n)
        if n == 4:
            li_copy(0, 6).start()
        elif n == 5:
            li_copy(1, 6).start()
        else:
            li_start(n + 2)

    loads[3].wait()
    li_start(0)
    li_start(1)

    for c in loads[4:10]:
        c.wait()

    key_iota = lax.broadcasted_iota(jnp.int32, (ROWS, ROWS), 0).astype(F32)

    def score_block(b, diagonal):
        kb = kvbuf[b, pl.ds(0, ROWS), :]
        vb = kvbuf[b, pl.ds(ROWS, ROWS), :]
        docs = kvbuf[b, pl.ds(2 * ROWS, 16), :].astype(F32)
        ones = jnp.sum(jnp.sum(docs, axis=0, keepdims=True), axis=1, keepdims=True) * 0.125
        zeros = ROWS - ones
        low = doc_row * zeros
        high = zeros + doc_row * ones
        if diagonal:
            own = lax.broadcasted_iota(jnp.int32, (1, ROWS), 1).astype(F32)
            high = jnp.minimum(high, own + 1.0)
        allowed = (key_iota >= low) & (key_iota < high)
        for g in range(GROUP):
            s = jnp.where(allowed, dot(kb, q_v[g], NT), NEG_FILL)
            top = jnp.max(s, axis=0, keepdims=True)
            p = jnp.exp2((s - top) * EXP_SCALE)
            wg = dot(vb, do_v[g], NT)
            p_buf[b, g] = p
            dp_buf[b, g] = wg
            m_buf[b, g : g + 1, :] = top
            l_buf[b, g : g + 1, :] = jnp.sum(p, axis=0, keepdims=True)
            a_buf[b, g : g + 1, :] = jnp.sum(p * wg, axis=0, keepdims=True)

    score_block(sq, True)

    li_next(0)

    @pl.when(y_hi == 0)
    def _():
        kv_arrived(far_x).wait_recv()
        kv_copy(far_x, other_half, 3).start()

    @pl.when(y_hi == 1)
    def _():
        for part in range(2):
            kv_part(x, part, other_half, 0).wait_recv()
            for n, d in enumerate((1, 3)):
                kv_part(x, part, x_mate(lax.rem(x + d, NX)), 2 + 2 * part + n).start()

    @pl.loop(1, NX)
    def _(d):
        @pl.when(d <= x)
        def _():
            @pl.when((y_hi == 1) | (d != 2))
            def _():
                kv_arrived(sq - d).wait_recv()

            score_block(sq - d, False)

    li_next(1)

    @pl.when(y_hi == 1)
    def _():
        score_block(x, False)

    li_next(2)

    @pl.when(y_hi == 1)
    def _():
        kv_arrived(far_x).wait_recv()
        score_block(far_x, False)

        @pl.loop(0, 2)
        def _(n):
            b = lax.rem(x + 1 + 2 * n, NX)
            for part in range(2):
                kv_part(b, part, other_half, 0).wait_recv()
            score_block(b, False)

    li_next(3)

    top = jnp.max(m_buf[...], axis=0)
    factor = jnp.exp2((m_buf[...] - top[None]) * EXP_SCALE)
    total = jnp.sum(factor * l_buf[...], axis=0)
    gathered = jnp.sum(factor * a_buf[...], axis=0)
    safe = jnp.where(total > 0.0, total, 1.0)
    inv = 1.0 / safe
    delta = gathered * inv
    f_buf[...] = factor * inv[None]

    def grad_block(b):
        kbt = kvbuf[b, pl.ds(0, ROWS), :].T
        dk = jnp.zeros((ROWS, HD), F32)
        dv = jnp.zeros((ROWS, HD), F32)
        for g in range(GROUP):
            w = p_buf[b, g] * f_buf[b, g : g + 1, :]
            sg = (w * (dp_buf[b, g] - delta[g : g + 1, :]) * SCALE).astype(BF)
            dv = dv + dot(w.astype(BF), do_v[g], NN)
            dk = dk + dot(sg, q_v[g], NN)
            dq_t[g] += dot(kbt, sg, NN)
        gsend[b, :, 0:HD] = dk.astype(BF)
        gsend[b, :, HD:] = dv.astype(BF)

    def g_copy(d):
        xt = lax.rem(x + d, NX)
        return remote(
            gsend.at[y_hi * NX + xt], grecv.at[d - 1], g_ss.at[d - 1], g_rs.at[d - 1], x_mate(xt)
        )

    def columns(part):
        return pl.ds(part * HD, HD)

    def c_copy(n, part):
        xt = lax.rem(x + 1 + 2 * n, NX)
        return remote(
            gsend.at[xt, :, columns(part)], crecv.at[n, part],
            c_ss.at[n, part], c_rs.at[n, part], x_mate(xt),
        )

    far_copy = remote(gsend.at[far_x], frecv, x_ss.at[2], x_rs.at[2], far_mate)

    def cross(part):
        return remote(xsend.at[part], xrecv.at[part], x_ss.at[part], x_rs.at[part], other_half)

    @pl.when(y_hi == 1)
    def _():
        grad_block(far_x)
        far_copy.start()

        @pl.loop(0, 2)
        def _(n):
            grad_block(lax.rem(x + 1 + 2 * n, NX))
            for part in range(2):
                c_copy(n, part).start()

    li_next(4)

    @pl.when(y_hi == 1)
    def _():
        grad_block(x)

    @pl.loop(1, NX)
    def _(d):
        xt = lax.rem(x + d, NX)

        @pl.when(xt < x)
        def _():
            grad_block(y_hi * NX + xt)
            g_copy(d).start()

    li_next(5)

    @pl.when(y_hi == 1)
    def _():
        for part in range(2):
            term = gsend[x, :, columns(part)].astype(F32)
            for n in range(2):
                c_copy(n, part).wait_recv()
                term = term + crecv[n, part].astype(F32)
            xsend[part] = term.astype(BF)
            cross(part).start()

    grad_block(sq)

    for g in range(GROUP):
        qg_out[:, g * HD : (g + 1) * HD] = dq_t[g].T.astype(BF)

    for c in loads[10:]:
        c.wait()

    li_wait(6)
    for n in range(D // 512):
        cols = li_buf[:, :, n * 512 : (n + 1) * 512].reshape(ROWS, 512)
        li_t[n * 512 : (n + 1) * 512, :] = cols.T

    acc[...] = gsend[sq].astype(F32)

    for d in range(1, NX):

        @pl.when(lax.rem(x - d + NX, NX) > x)
        def _():
            g_copy(d).wait_recv()
            acc[...] += grecv[d - 1].astype(F32)

    @pl.when(y_hi == 0)
    def _():
        far_copy.wait_recv()
        acc[...] += frecv[...].astype(F32)
        for part in range(2):
            cross(part).wait_recv()
            acc[:, columns(part)] += xrecv[part].astype(F32)

    kv_low[...] = acc[...].astype(BF)

    def core_copy(p):
        return remote(csend.at[p], ccr.at[p], core_ss.at[p], core_rs.at[p], other_core)

    def proj_part(which, p):
        rows = pl.ds(pl.multiple_of(which * HALF + p * PART, PART), PART)
        return dot(li_t[rows, :], kv_low[...], NN)

    for p in range(PARTS):
        csend[p] = proj_part(1 - core, p).astype(BF)
        core_copy(p).start()

    for n in range(D // 512):
        part = dot(kv_low[...], wcat[n * 512 : (n + 1) * 512, :], NT)
        ipart[:, :, n * 512 : (n + 1) * 512] = part.reshape(NZ, 32, 512)

    def z_copy(direction, k, half):
        return remote(
            zs.at[direction, k, half], zr.at[direction, k, half],
            z_ss.at[direction, k, half], z_rs.at[direction, k, half],
            z_mate(1 - 2 * direction),
        )

    def z_send(direction, k, half, add):
        t = lax.rem(hd + 4 - k, NZ) if direction == 0 else lax.rem(hd + 4 + k, NZ)
        term = ipart[t, :, half * HALF : (half + 1) * HALF]
        if add:
            z_copy(direction, k - 1, half).wait_recv()
            term = term + zr[direction, k - 1, half].astype(F32)
        zs[direction, k, half] = term.astype(BF)
        z_copy(direction, k, half).start()

    def z_step(k, half, add=True):
        z_send(0, k, half, add)
        z_send(1, k, 1 - half, add)

    z_step(0, 0, False)
    z_step(1, 1, False)

    def index(axis):
        return yi if axis else x

    def mate(axis, d):
        if axis:
            return y_mate(lax.rem(yi + d, NX))
        return x_mate(lax.rem(x + d, NX))

    def st1_copy(p, d):
        a = p % 2
        return remote(
            s1.at[p, lax.rem(index(a) + d, NX)], r1.at[p, d - 1],
            st1_ss.at[p, d - 1], st1_rs.at[p, d - 1], mate(a, d),
        )

    def st2_copy(p, d, arrived=False):
        a = 1 - p % 2
        own = index(a)
        slot = lax.rem(own - d + NX, NX) if arrived else own
        return remote(
            r2.at[p, own], r2.at[p, slot], st2_ss.at[p, d - 1], st2_rs.at[p, d - 1], mate(a, d)
        )

    def ag_copy(p, d, arrived=False):
        own = index(p % 2)
        ref = gfull.at[core, p, lax.rem(own - d + NX, NX) if arrived else own]
        return remote(ref, ref, ag_ss.at[p, d - 1], ag_rs.at[p, d - 1], mate(p % 2, d))

    def pair_copy(p, arrived=False):
        ref = gfull.at[1 - core if arrived else core, p]
        return remote(ref, ref, p_ss.at[p], p_rs.at[p], other_core)

    for p in range(PARTS):
        h32[p] = proj_part(core, p).reshape(NX, SUB, 2 * HD)

    for p in range(PARTS):
        core_copy(p).wait_recv()
        term = h32[p] + ccr[p].astype(F32).reshape(NX, SUB, 2 * HD)
        h32[p] = term
        s1[p] = term.astype(BF)
        for d in (2, 1, 3):
            st1_copy(p, d).start()

    def stage2(p):
        term = h32[p, index(p % 2)]
        for d in (1, 3, 2):
            st1_copy(p, d).wait_recv()
            term = term + r1[p, d - 1].astype(F32)
        r2[p, index(1 - p % 2)] = term.astype(BF)
        for d in (2, 1, 3):
            st2_copy(p, d).start()

    def gather(p):
        for d in (1, 3, 2):
            st2_copy(p, d, True).wait_recv()
        term = r2[p, 0].astype(F32)
        for i in range(1, NX):
            term = term + r2[p, i].astype(F32)
        gfull[core, p, index(p % 2)] = term.astype(BF)
        for d in (2, 1, 3):
            ag_copy(p, d).start()

    def hand_over(p):
        for d in (1, 3, 2):
            ag_copy(p, d, True).wait_recv()
        pair_copy(p).start()

    z_step(1, 0)
    stage2(0)
    stage2(1)
    z_step(2, 1)
    stage2(2)
    stage2(3)
    z_step(2, 0)
    gather(0)
    gather(1)
    z_step(3, 1)
    gather(2)
    gather(3)
    z_step(3, 0)
    hand_over(0)
    hand_over(1)

    for half in range(2):
        term = ipart[hd, :, half * HALF : (half + 1) * HALF]
        for direction in range(2):
            z_copy(direction, 3, half).wait_recv()
            term = term + zr[direction, 3, half].astype(F32)
        ig_out[:, half * HALF : (half + 1) * HALF] = term.astype(BF)

    hand_over(2)
    hand_over(3)
    for p in range(PARTS):
        pair_copy(p, True).wait_recv()

    for d in range(1, NX):
        xt = lax.rem(x + d, NX)

        @pl.when((xt > x) & ((y_hi == 1) if d == 2 else True))
        def _():
            kv_copy(sq, x_mate(xt), d - 1).wait_send()

        @pl.when(xt < x)
        def _():
            g_copy(d).wait_send()

    @pl.when(y_hi == 0)
    def _():
        for part in range(2):
            kv_part(x, part, other_half, part).wait_send()
        kv_copy(sq, x_mate(far_x), 1).wait_send()
        kv_copy(far_x, other_half, 3).wait_send()

    @pl.when(y_hi == 1)
    def _():
        for n, d in enumerate((1, 3)):
            for part in range(2):
                kv_part(x, part, x_mate(lax.rem(x + d, NX)), 2 + 2 * part + n).wait_send()
                c_copy(n, part).wait_send()
        far_copy.wait_send()
        for part in range(2):
            cross(part).wait_send()

    for direction in range(2):
        for n in range(7):
            li_copy(direction, n).wait_send()
        for k in range(4):
            for half in range(2):
                if k > 0 or half == direction:
                    z_copy(direction, k, half).wait_send()
    for p in range(PARTS):
        core_copy(p).wait_send()
        for d in range(1, NX):
            st1_copy(p, d).wait_send()
            st2_copy(p, d).wait_send()
            ag_copy(p, d).wait_send()
        pair_copy(p).wait_send()


def finish(
    qg_in, ig_in, gp_in, qg_ref, ig_ref, gk_ref, gv_ref,
    key, value, sem_key, sem_value, sem,
):
    step = D // PIECES
    copies = [
        pltpu.make_async_copy(qg_in, qg_ref, sem.at[0]),
        pltpu.make_async_copy(ig_in, ig_ref, sem.at[1]),
    ]
    for c in copies:
        c.start()
    for n in range(PIECES):
        rows = pl.ds(n * step, step)
        key[n] = gp_in[rows, 0:HD].astype(F32)
        copies.append(pltpu.make_async_copy(key.at[n], gk_ref.at[rows, :], sem_key.at[n]))
        copies[-1].start()
        value[n] = gp_in[rows, HD:].astype(F32)
        copies.append(pltpu.make_async_copy(value.at[n], gv_ref.at[rows, :], sem_value.at[n]))
        copies[-1].start()
    for c in copies:
        c.wait()


def shards(queries, key_cache, value_cache, out_grad, doc_ids, layer_input, key_proj, value_proj):
    hbm = pl.BlockSpec(memory_space=pl.ANY)
    vmem = pl.BlockSpec(memory_space=pltpu.VMEM)
    dma = pltpu.SemaphoreType.DMA
    scratch = [
        pltpu.VMEM((GROUP, ROWS, HD), BF),
        pltpu.VMEM((GROUP, ROWS, HD), BF),
        pltpu.VMEM((1, ROWS), jnp.int32),
        pltpu.VMEM((NS, 2 * ROWS + 16, HD), BF),
        pltpu.VMEM((NZ, 32, D), BF),
        pltpu.VMEM((D, ROWS), BF),
        pltpu.VMEM((D, 2 * HD), BF),
        pltpu.VMEM((NS, GROUP, ROWS, ROWS), F32),
        pltpu.VMEM((NS, GROUP, ROWS, ROWS), F32),
        pltpu.VMEM((NS, 8, ROWS), F32),
        pltpu.VMEM((NS, 8, ROWS), F32),
        pltpu.VMEM((NS, 8, ROWS), F32),
        pltpu.VMEM((NS, 8, ROWS), F32),
        pltpu.VMEM((GROUP, HD, ROWS), F32),
        pltpu.VMEM((NS, ROWS, 2 * HD), BF),
        pltpu.VMEM((NX - 1, ROWS, 2 * HD), BF),
        pltpu.VMEM((2, 2, ROWS, HD), BF),
        pltpu.VMEM((2, ROWS, HD), BF),
        pltpu.VMEM((2, ROWS, HD), BF),
        pltpu.VMEM((ROWS, 2 * HD), BF),
        pltpu.VMEM((ROWS, 2 * HD), F32),
        pltpu.VMEM((ROWS, 2 * HD), BF),
        pltpu.VMEM((NZ, 32, D), F32),
        pltpu.VMEM((2, 4, 2, 32, HALF), BF),
        pltpu.VMEM((2, 4, 2, 32, HALF), BF),
        pltpu.VMEM((PARTS, PART, 2 * HD), BF),
        pltpu.VMEM((PARTS, PART, 2 * HD), BF),
        pltpu.VMEM((PARTS, NX, SUB, 2 * HD), F32),
        pltpu.VMEM((PARTS, NX, SUB, 2 * HD), BF),
        pltpu.VMEM((PARTS, NX - 1, SUB, 2 * HD), BF),
        pltpu.VMEM((PARTS, NX, SUB, 2 * HD), BF),
        dma((12,)),
        dma((NX,)),
        dma((NS,)),
        dma((6,)),
        dma((NX, 2)),
        dma((2, 7)),
        dma((2, 7)),
        dma((NX - 1,)),
        dma((NX - 1,)),
        dma((2, 2)),
        dma((2, 2)),
        dma((3,)),
        dma((3,)),
        dma((2, 4, 2)),
        dma((2, 4, 2)),
        dma((PARTS,)),
        dma((PARTS,)),
        dma((PARTS, 3)),
        dma((PARTS, 3)),
        dma((PARTS, 3)),
        dma((PARTS, 3)),
        dma((PARTS, 3)),
        dma((PARTS, 3)),
        dma((PARTS,)),
        dma((PARTS,)),
    ]
    qg, ig, gp = pl.pallas_call(
        kernel,
        out_shape=(
            pltpu.VMEM((ROWS, GROUP * HD), BF),
            pltpu.VMEM((32, D), BF),
            pltpu.VMEM((2, PARTS, NX, SUB, 2 * HD), BF),
        ),
        in_specs=[hbm] * 8,
        out_specs=(vmem,) * 3,
        scratch_shapes=scratch,
        compiler_params=pltpu.CompilerParams(
            collective_id=0, has_side_effects=True, vmem_limit_bytes=56 * 1024 * 1024
        ),
        cost_estimate=pl.CostEstimate(
            flops=3 * 10**9, bytes_accessed=8 * 10**6, transcendentals=2 * 10**6
        ),
    )(
        queries[0], key_cache[0], value_cache[0], out_grad[0], doc_ids, layer_input[0],
        key_proj, value_proj,
    )
    step = D // PIECES
    qg, ig, gk, gv = pl.pallas_call(
        finish,
        out_shape=(
            jax.ShapeDtypeStruct((ROWS, GROUP * HD), BF),
            jax.ShapeDtypeStruct((32, D), BF),
            jax.ShapeDtypeStruct((D, HD), F32),
            jax.ShapeDtypeStruct((D, HD), F32),
        ),
        in_specs=[vmem] * 3,
        out_specs=(hbm,) * 4,
        scratch_shapes=[
            pltpu.VMEM((PIECES, step, HD), F32),
            pltpu.VMEM((PIECES, step, HD), F32),
            dma((PIECES,)),
            dma((PIECES,)),
            dma((2,)),
        ],
        compiler_params=pltpu.CompilerParams(vmem_limit_bytes=24 * 1024 * 1024),
        cost_estimate=pl.CostEstimate(flops=0, bytes_accessed=6 * 10**6, transcendentals=0),
    )(qg, ig, gp.reshape(D, 2 * HD))
    return qg[None], ig[None], gk, gv


def solution(mesh):
    return jax.shard_map(
        shards,
        mesh=mesh,
        in_specs=(
            P("dp", "seq", "head"),
            P("dp", "seq", "head"),
            P("dp", "seq", "head"),
            P("dp", "seq", "head"),
            P("dp", "seq"),
            P("dp", ("seq", "head"), None),
            P(None, "head"),
            P(None, "head"),
        ),
        out_specs=(
            P("dp", "seq", "head"),
            P("dp", ("seq", "head"), None),
            P(None, "head"),
            P(None, "head"),
        ),
        check_vma=False,
    )
```
